32 devices in a mesh: gx: 4 (over y, x), pa: 8 (over z, core).
Axes of the slice: x: 2, y: 2, z: 4, core: 2. Of those that a mesh axis runs over, the one named last changes fastest.
Arguments:
- plastic: float32 [6, 128, 128, 128], P(None, 'gx', 'pa'), may hold values from -6 to 6
- offsets: float32 [3, 8, 16, 128], P(None, 'pa', 'gx'), may hold values from 0 to 1
- lines: float32 [3, 8, 16, 128], P(None, 'pa', 'gx'), may hold values from -3 to 3
- burgers: float32 [3, 8, 16, 128], P(None, 'pa', 'gx'), may hold values from -3.6 to 3.6
- counts: int32 [8, 16], P('pa', 'gx'), may hold values from 1 to 128, as said below
- voxels: int32 [8, 16, 128], P('pa', 'gx'), may hold values from 0 to 65535, as said below
Outputs:
- stress: float32 [6, 128, 128, 128], P(None, 'gx', 'pa')
- moved: float32 [3, 8, 16, 128], P(None, 'pa', 'gx')
The draws below stay inside these ranges and needn't reach their ends.
Inputs may be any that keep to these rules, and one draw needn't show every extreme that they name: `counts`: each count is at least 1 and some cell holds 128 live segments. `voxels`: A segment of cell c lies in its device's block of 32 x 16 x 128 grid points: v = (x * 16 + y) * 128 + z with local plane x among the 8 planes of cell c % 4.
All inputs are finite; a program needn't handle non-finite values.
Results may differ from the reference program's by a relative error of at most 0.0003.
Values sent between devices are 32-bit elements; how exact they have to be, the bound alone decides.
No kernel may reach another device: no remote copies, remote signals or barrier semaphores. Data moves between devices by JAX's collectives and lax.ppermute only.
A program may use at most 128 MiB of HBM per device.

```python
import math
import jax
import jax.numpy as jnp
from jax import lax

GRID = 128
CELLS_DEV = 4
CAP = 128
SUB = 3
CELLS = 16
SLABS = 8
XL = 32
YL = 16


def draw_counts(key, part):
    first_key, second_key = jax.random.split(key)
    raw_count = jax.random.randint(first_key, (SLABS, CELLS // CELLS_DEV, CELLS_DEV), 1, CAP + 1)
    load_level = jax.random.randint(second_key, (SLABS, CELLS // CELLS_DEV, 1), 1, 5)
    scaled = jnp.maximum(1, raw_count * load_level // 4).reshape(SLABS, CELLS)
    return scaled.at[0, 0].set(CAP).astype(jnp.int32)


def draw_voxels(key, part):
    subkeys = jax.random.split(key, 3)
    per_cell = XL // CELLS_DEV
    cell_local = (jnp.arange(CELLS, dtype=jnp.int32) % CELLS_DEV)[None, :, None]
    pick_x = jax.random.randint(subkeys[0], (SLABS, CELLS, CAP), 0, per_cell)
    pick_y = jax.random.randint(subkeys[1], (SLABS, CELLS, CAP), 0, YL)
    pick_z = jax.random.randint(subkeys[2], (SLABS, CELLS, CAP), 0, GRID)
    return (((cell_local * per_cell + pick_x) * YL + pick_y) * GRID + pick_z).astype(jnp.int32)


def levels(stream_key, shape, pieces, least, largest):
    def one(dim, parts):
        heights = jax.random.uniform(jax.random.fold_in(jax.random.fold_in(stream_key, 6), dim), (parts,), jnp.float32, least / len(pieces), largest / len(pieces))
        return jnp.repeat(jnp.exp(heights), shape[dim] // parts).reshape((-1,) + (1,) * (len(shape) - dim - 1))

    factor_of = one(*pieces[0])
    for cut in pieces[1:]:
        factor_of = factor_of * one(*cut)
    return factor_of


def gaussian(stream_key, extent, deviation, limit, shards=(), kind=jnp.bfloat16):
    values = jax.random.normal(stream_key, extent, jnp.float32) * deviation
    if len(shards) > 0:
        values = levels(stream_key, extent, shards, -0.22, 0.18) * values
    return jnp.clip(values, min=-limit, max=limit).astype(kind)


def setup_inputs(seed: int = 0) -> dict:
    key_of = jax.random.split(jax.random.key(seed), 7)
    return {
        "plastic": gaussian(key_of[0], (6, GRID, GRID, GRID), 1.0, 6.0, ((1, 4), (2, 8)), jnp.float32),
        "offsets": jnp.clip(1.0 * jax.random.uniform(key_of[1], (3, SLABS, CELLS, CAP), jnp.float32) ** levels(key_of[1], (3, SLABS, CELLS, CAP), ((1, 8), (2, 4)), -0.2, 0.2), 0.0, 1.0),
        "lines": gaussian(key_of[2], (3, SLABS, CELLS, CAP), 0.5, 3.0, ((1, 8), (2, 4)), jnp.float32),
        "burgers": gaussian(key_of[3], (3, SLABS, CELLS, CAP), 0.6, 3.6, ((1, 8), (2, 4)), jnp.float32),
        "counts": draw_counts(jax.random.fold_in(key_of[6], 71), 0),
        "voxels": draw_voxels(jax.random.fold_in(key_of[6], 71), 0),
    }


lame_lambda = 1.5
shear_modulus = 1.0
green_coef = 2.5 / 3.5
core_square = 0.09
pair_factor = 1.0 / (4.0 * math.pi)
step_size = 0.05
full_index = ((0, 5, 4), (5, 1, 3), (4, 3, 2))

def stress_of(strain, freq_x, freq_y, freq_z):
    strain_xx, strain_yy, strain_zz = (strain[0], strain[1], strain[2])
    strain_yz, strain_xz, strain_xy = (strain[3], strain[4], strain[5])
    trace = strain_xx + strain_yy + strain_zz
    tau_xx = lame_lambda * trace + 2.0 * shear_modulus * strain_xx
    tau_yy = lame_lambda * trace + 2.0 * shear_modulus * strain_yy
    tau_zz = lame_lambda * trace + 2.0 * shear_modulus * strain_zz
    tau_yz = 2.0 * shear_modulus * strain_yz
    tau_xz = 2.0 * shear_modulus * strain_xz
    tau_xy = 2.0 * shear_modulus * strain_xy
    norm_x = tau_xx * freq_x + tau_xy * freq_y + tau_xz * freq_z
    norm_y = tau_xy * freq_x + tau_yy * freq_y + tau_yz * freq_z
    norm_z = tau_xz * freq_x + tau_yz * freq_y + tau_zz * freq_z
    square = freq_x * freq_x + freq_y * freq_y + freq_z * freq_z
    inverse = 1.0 / jnp.maximum(square, 1.0)
    along_k = (freq_x * norm_x + freq_y * norm_y + freq_z * norm_z) * inverse * inverse * green_coef

    def strain_term(first_q, second_q, first_n, second_n, plastic_part):
        total = (first_q * second_n + second_q * first_n) * inverse / (2.0 * shear_modulus) - first_q * second_q * along_k
        return total - plastic_part
    el_xx = strain_term(freq_x, freq_x, norm_x, norm_x, strain_xx)
    el_yy = strain_term(freq_y, freq_y, norm_y, norm_y, strain_yy)
    el_zz = strain_term(freq_z, freq_z, norm_z, norm_z, strain_zz)
    el_yz = strain_term(freq_y, freq_z, norm_y, norm_z, strain_yz)
    el_xz = strain_term(freq_x, freq_z, norm_x, norm_z, strain_xz)
    el_xy = strain_term(freq_x, freq_y, norm_x, norm_y, strain_xy)
    el_trace = el_xx + el_yy + el_zz
    return jnp.stack([lame_lambda * el_trace + 2.0 * shear_modulus * el_xx, lame_lambda * el_trace + 2.0 * shear_modulus * el_yy, lame_lambda * el_trace + 2.0 * shear_modulus * el_zz, 2.0 * shear_modulus * el_yz, 2.0 * shear_modulus * el_xz, 2.0 * shear_modulus * el_xy])

def advance(position, lines, burgers, sampled):
    cell_count = sampled.shape[1]
    unit_x = jnp.array([1.0, 0.0, 0.0], jnp.float32)[:, None, None]
    source = jnp.concatenate([position[:, shifted:shifted + cell_count] + (shifted - 1.0) * unit_x for shifted in range(3)], axis=2)
    source_line = jnp.concatenate([lines[:, shifted:shifted + cell_count] for shifted in range(3)], axis=2)
    source_burgers = jnp.concatenate([burgers[:, shifted:shifted + cell_count] for shifted in range(3)], axis=2)
    target = position[:, 1:cell_count + 1]
    own_line = lines[:, 1:cell_count + 1]
    own_burgers = burgers[:, 1:cell_count + 1]
    offset_vec = target[:, :, :, None] - source[:, :, None, :]
    radius = offset_vec[0] ** 2 + offset_vec[1] ** 2 + offset_vec[2] ** 2 + core_square
    weight = lax.rsqrt(radius) / radius
    line_b = source_line[:, :, None, :]
    cross = jnp.stack([offset_vec[1] * line_b[2] - offset_vec[2] * line_b[1], offset_vec[2] * line_b[0] - offset_vec[0] * line_b[2], offset_vec[0] * line_b[1] - offset_vec[1] * line_b[0]]) * weight[None]
    moment = jnp.einsum('acij,bcj->abci', cross, source_burgers, precision=lax.Precision.HIGHEST)
    pair_field = pair_factor * (moment + jnp.swapaxes(moment, 0, 1))
    traction = []
    for first in range(3):
        acc_row = jnp.zeros_like(target[0])
        for second in range(3):
            acc_row = acc_row + (sampled[full_index[first][second]] + pair_field[first, second]) * own_burgers[second]
        traction.append(acc_row)
    force_x = traction[1] * own_line[2] - traction[2] * own_line[1]
    force_y = traction[2] * own_line[0] - traction[0] * own_line[2]
    force_z = traction[0] * own_line[1] - traction[1] * own_line[0]
    return target + step_size * jnp.stack([force_x, force_y, force_z])

def extend(array):
    return jnp.concatenate([array[:, -1:], array, array[:, :1]], axis=1)

def reference(plastic, offsets, lines, burgers, counts, voxels):
    spectrum = jnp.fft.rfftn(plastic, axes=(1, 2, 3))
    grid_index = jnp.arange(GRID, dtype=jnp.int32)
    signed = jnp.where(grid_index < GRID // 2, grid_index, jnp.where(grid_index == GRID // 2, 0, grid_index - GRID)).astype(jnp.float32)
    half_index = jnp.arange(GRID // 2 + 1, dtype=jnp.int32)
    half_freq = jnp.where(half_index < GRID // 2, half_index, 0).astype(jnp.float32)
    freq_x = signed[:, None, None]
    freq_y = signed[None, :, None]
    freq_z = half_freq[None, None, :]
    real_part = stress_of(jnp.real(spectrum), freq_x, freq_y, freq_z)
    imag_part = stress_of(jnp.imag(spectrum), freq_x, freq_y, freq_z)
    stress_spectrum = lax.complex(real_part, imag_part)
    stress = jnp.fft.irfftn(stress_spectrum, s=(GRID, GRID, GRID), axes=(1, 2, 3)).astype(jnp.float32)
    live_mask = (jnp.arange(CAP, dtype=jnp.int32)[None, None, :] < counts[:, :, None]).astype(jnp.float32)
    masked = burgers * live_mask[None]
    local_x = voxels // (YL * GRID)
    remain = voxels % (YL * GRID)
    local_y = remain // GRID
    local_z = remain % GRID
    owner_gx = (jnp.arange(CELLS, dtype=jnp.int32) // CELLS_DEV)[None, :, None]
    slab_index = jnp.arange(SLABS, dtype=jnp.int32)[:, None, None]
    grid_x = (owner_gx * XL + local_x).astype(jnp.int32)
    grid_y = (slab_index * YL + local_y).astype(jnp.int32)
    sampled = stress[:, grid_x, grid_y, local_z.astype(jnp.int32)]

    def per_slab(items):
        initial, line_dirs, burg_dirs, sample_slab = items
        position = initial
        for repeat in range(SUB):
            position = advance(extend(position), extend(line_dirs), extend(burg_dirs), sample_slab)
        return position - initial
    moved = lax.map(per_slab, (jnp.moveaxis(offsets, 1, 0), jnp.moveaxis(lines, 1, 0), jnp.moveaxis(masked, 1, 0), jnp.moveaxis(sampled, 1, 0)))
    return (stress, jnp.moveaxis(moved, 0, 1))
```

```python
import functools
import math

import jax
import jax.numpy as jnp
import ml_dtypes
import numpy as np
from jax import lax
from jax.experimental import pallas as pl
from jax.experimental.pallas import tpu as pltpu
from jax.sharding import PartitionSpec as P

SUB = 3


lame_lambda = 1.5
shear_modulus = 1.0
green_coef = 2.5 / 3.5
core_square = 0.09
pair_factor = 1.0 / (4.0 * math.pi)
step_size = 0.05
full_index = ((0, 5, 4), (5, 1, 3), (4, 3, 2))


def with_halo(block, sides, width):
    for axis, dim in sides:
        count = lax.axis_size(axis)
        forward = [(i, i + 1) for i in range(count - 1)]
        forward.append((count - 1, 0))
        backward = [(target, source) for source, target in forward]
        low = lax.ppermute(
            lax.slice_in_dim(block, block.shape[dim] - width, None, axis=dim), axis, forward
        )
        high = lax.ppermute(lax.slice_in_dim(block, 0, width, axis=dim), axis, backward)
        block = jnp.concatenate([low, block, high], axis=dim)
    return block


def stress_of(strain, freq_x, freq_y, freq_z):
    strain_xx, strain_yy, strain_zz = (strain[0], strain[1], strain[2])
    strain_yz, strain_xz, strain_xy = (strain[3], strain[4], strain[5])
    trace = strain_xx + strain_yy + strain_zz
    tau_xx = lame_lambda * trace + 2.0 * shear_modulus * strain_xx
    tau_yy = lame_lambda * trace + 2.0 * shear_modulus * strain_yy
    tau_zz = lame_lambda * trace + 2.0 * shear_modulus * strain_zz
    tau_yz = 2.0 * shear_modulus * strain_yz
    tau_xz = 2.0 * shear_modulus * strain_xz
    tau_xy = 2.0 * shear_modulus * strain_xy
    norm_x = tau_xx * freq_x + tau_xy * freq_y + tau_xz * freq_z
    norm_y = tau_xy * freq_x + tau_yy * freq_y + tau_yz * freq_z
    norm_z = tau_xz * freq_x + tau_yz * freq_y + tau_zz * freq_z
    square = freq_x * freq_x + freq_y * freq_y + freq_z * freq_z
    inverse = 1.0 / jnp.maximum(square, 1.0)
    along_k = (freq_x * norm_x + freq_y * norm_y + freq_z * norm_z) * inverse * inverse * green_coef

    def strain_term(first_q, second_q, first_n, second_n, plastic_part):
        total = (first_q * second_n + second_q * first_n) * inverse / (
            2.0 * shear_modulus
        ) - first_q * second_q * along_k
        return total - plastic_part

    el_xx = strain_term(freq_x, freq_x, norm_x, norm_x, strain_xx)
    el_yy = strain_term(freq_y, freq_y, norm_y, norm_y, strain_yy)
    el_zz = strain_term(freq_z, freq_z, norm_z, norm_z, strain_zz)
    el_yz = strain_term(freq_y, freq_z, norm_y, norm_z, strain_yz)
    el_xz = strain_term(freq_x, freq_z, norm_x, norm_z, strain_xz)
    el_xy = strain_term(freq_x, freq_y, norm_x, norm_y, strain_xy)
    el_trace = el_xx + el_yy + el_zz
    return jnp.stack(
        [
            lame_lambda * el_trace + 2.0 * shear_modulus * el_xx,
            lame_lambda * el_trace + 2.0 * shear_modulus * el_yy,
            lame_lambda * el_trace + 2.0 * shear_modulus * el_zz,
            2.0 * shear_modulus * el_yz,
            2.0 * shear_modulus * el_xz,
            2.0 * shear_modulus * el_xy,
        ]
    )


def advance(position, lines, burgers, sampled):
    cell_count = sampled.shape[1]
    unit_x = jnp.array([1.0, 0.0, 0.0], jnp.float32)[:, None, None]
    source = jnp.concatenate(
        [
            position[:, shifted : shifted + cell_count] + (shifted - 1.0) * unit_x
            for shifted in range(3)
        ],
        axis=2,
    )
    source_line = jnp.concatenate(
        [lines[:, shifted : shifted + cell_count] for shifted in range(3)], axis=2
    )
    source_burgers = jnp.concatenate(
        [burgers[:, shifted : shifted + cell_count] for shifted in range(3)], axis=2
    )
    target = position[:, 1 : cell_count + 1]
    own_line = lines[:, 1 : cell_count + 1]
    own_burgers = burgers[:, 1 : cell_count + 1]
    offset_vec = target[:, :, :, None] - source[:, :, None, :]
    radius = offset_vec[0] ** 2 + offset_vec[1] ** 2 + offset_vec[2] ** 2 + core_square
    weight = lax.rsqrt(radius) / radius
    line_b = source_line[:, :, None, :]
    cross = (
        jnp.stack(
            [
                offset_vec[1] * line_b[2] - offset_vec[2] * line_b[1],
                offset_vec[2] * line_b[0] - offset_vec[0] * line_b[2],
                offset_vec[0] * line_b[1] - offset_vec[1] * line_b[0],
            ]
        )
        * weight[None]
    )
    moment = jnp.einsum("acij,bcj->abci", cross, source_burgers, precision=lax.Precision.HIGHEST)
    pair_field = pair_factor * (moment + jnp.swapaxes(moment, 0, 1))
    traction = []
    for first in range(3):
        acc_row = jnp.zeros_like(target[0])
        for second in range(3):
            acc_row = (
                acc_row
                + (sampled[full_index[first][second]] + pair_field[first, second])
                * own_burgers[second]
            )
        traction.append(acc_row)
    force_x = traction[1] * own_line[2] - traction[2] * own_line[1]
    force_y = traction[2] * own_line[0] - traction[0] * own_line[2]
    force_z = traction[0] * own_line[1] - traction[1] * own_line[0]
    return target + step_size * jnp.stack([force_x, force_y, force_z])


def phases(row_index, col_index, grid_len):
    product = row_index[:, None] * col_index[None, :] % grid_len
    angle = product.astype(jnp.float32) * (2.0 * math.pi / grid_len)
    return (jnp.cos(angle), jnp.sin(angle))


def transform_last(field, matrix):
    shape = field.shape
    flat = field.reshape(-1, shape[-2] * shape[-1])
    result = jnp.dot(flat, matrix, precision=lax.Precision.HIGHEST)
    return result.reshape(shape[:-2] + (2, matrix.shape[1] // 2))


def body(plastic, offsets, lines, burgers, counts, voxels):
    grid_len = plastic.shape[3]
    pa_count = lax.axis_size("pa")
    grid_index = jnp.arange(grid_len, dtype=jnp.int32)
    bin_count = grid_len // 2 + pa_count
    bin_index = jnp.arange(bin_count, dtype=jnp.int32)
    kept_bins = (bin_index <= grid_len // 2).astype(jnp.float32)
    weights = jnp.where((bin_index == 0) | (bin_index == grid_len // 2), 1.0, 2.0) * kept_bins
    front_cos, front_sin = phases(grid_index, bin_index, grid_len)
    front_table = jnp.concatenate(
        [front_cos * kept_bins[None, :], -front_sin * kept_bins[None, :]], axis=1
    )
    final_cos, final_sin = phases(bin_index, grid_index, grid_len)
    final_table = (
        jnp.concatenate([final_cos * weights[:, None], -final_sin * weights[:, None]], axis=0)
        / grid_len
    )
    turn_cos, turn_sin = phases(grid_index, grid_index, grid_len)
    ahead_table = jnp.block([[turn_cos, -turn_sin], [turn_sin, turn_cos]])
    return_table = jnp.block([[turn_cos, turn_sin], [-turn_sin, turn_cos]]) / grid_len
    comp_count, x_local, y_local = (plastic.shape[0], plastic.shape[1], plastic.shape[2])
    field = jnp.dot(plastic.reshape(-1, grid_len), front_table, precision=lax.Precision.HIGHEST)
    field = field.reshape(comp_count, x_local, y_local, 2, bin_count)
    field = lax.all_to_all(field, "pa", split_axis=4, concat_axis=2, tiled=True)
    field = jnp.transpose(field, (0, 1, 4, 3, 2))
    field = transform_last(field, ahead_table)
    field = lax.all_to_all(field, "gx", split_axis=4, concat_axis=1, tiled=True)
    field = jnp.transpose(field, (0, 4, 2, 3, 1))
    field = transform_last(field, ahead_table)
    y_count = field.shape[1]
    z_count = field.shape[2]
    signed = jnp.where(
        grid_index < grid_len // 2,
        grid_index,
        jnp.where(grid_index == grid_len // 2, 0, grid_index - grid_len),
    ).astype(jnp.float32)
    freq_x = signed[None, None, :]
    freq_y = lax.dynamic_slice_in_dim(signed, lax.axis_index("gx") * y_count, y_count)[
        :, None, None
    ]
    freq_z = lax.dynamic_slice_in_dim(signed, lax.axis_index("pa") * z_count, z_count)[
        None, :, None
    ]
    real_part = stress_of(field[:, :, :, 0], freq_x, freq_y, freq_z)
    imag_part = stress_of(field[:, :, :, 1], freq_x, freq_y, freq_z)
    field = jnp.stack([real_part, imag_part], axis=3)
    field = transform_last(field, return_table)
    field = lax.all_to_all(field, "gx", split_axis=4, concat_axis=1, tiled=True)
    field = jnp.transpose(field, (0, 4, 2, 3, 1))
    field = transform_last(field, return_table)
    field = lax.all_to_all(field, "pa", split_axis=4, concat_axis=2, tiled=True)
    field = jnp.transpose(field, (0, 1, 4, 3, 2))
    flat = field.reshape(-1, 2 * bin_count)
    stress = jnp.dot(flat, final_table, precision=lax.Precision.HIGHEST).reshape(
        comp_count, x_local, y_local, grid_len
    )
    cell_count = offsets.shape[2]
    width_cap = offsets.shape[3]
    flat_stress = stress.reshape(6, -1)
    sampled = jnp.take(flat_stress, voxels.reshape(-1), axis=1).reshape(6, cell_count, width_cap)
    live_mask = (jnp.arange(width_cap, dtype=jnp.int32)[None, :] < counts[0][:, None]).astype(
        jnp.float32
    )
    initial = offsets[:, 0]
    line_dirs = lines[:, 0]
    masked = burgers[:, 0] * live_mask[None]
    fixed_rim = with_halo(jnp.concatenate([line_dirs, masked], axis=0), (("gx", 1),), 1)
    position = initial
    for repeat in range(SUB):
        widened = with_halo(position, (("gx", 1),), 1)
        position = advance(widened, fixed_rim[0:3], fixed_rim[3:6], sampled)
    moved = position - initial
    return (stress, moved[:, None])


LANES = 128
COMPS = 6
FEATURES = 24
SLOTS = 16
VMEM_LIMIT = 48 * 1024 * 1024


def split(value):
    high = value.astype(jnp.bfloat16)
    low = (value - high.astype(jnp.float32)).astype(jnp.bfloat16)
    return high, low


def split_table(table):
    table = np.asarray(table, np.float32)
    high = table.astype(ml_dtypes.bfloat16)
    low = (table - high.astype(np.float32)).astype(ml_dtypes.bfloat16)
    return high, low


def product(left, right, dims=((1,), (0,))):
    def one(first, second):
        return lax.dot_general(
            first, second, (dims, ((), ())), preferred_element_type=jnp.float32
        )

    left_high, left_low = left
    right_high, right_low = right
    return one(left_high, right_high) + (one(left_high, right_low) + one(left_low, right_high))


def tables(grid_len, pa_count, y_local):
    index = np.arange(grid_len)
    bins = np.arange(grid_len // 2)
    angle = 2.0 * np.pi * (np.outer(bins, index) % grid_len) / grid_len
    nyquist = 1.0 - 2.0 * (index % 2)
    forward_z = np.stack([np.cos(angle), -np.sin(angle)], axis=1)
    forward_z[0, 1] = nyquist
    inverse_z = 2.0 * forward_z / grid_len
    inverse_z[0] = forward_z[0] / grid_len
    forward_z = forward_z.reshape(grid_len, grid_len)
    inverse_z = inverse_z.reshape(grid_len, grid_len)
    turn = 2.0 * np.pi * (np.outer(index, index) % grid_len) / grid_len
    cos, sin = np.cos(turn), np.sin(turn)
    ahead = np.array([[cos, sin], [-sin, cos]]).transpose(0, 2, 1, 3)
    back = np.array([[cos, -sin], [sin, cos]]).transpose(0, 2, 1, 3) / grid_len
    size = 2 * grid_len
    forward_y = ahead.reshape(2, grid_len, 2, pa_count, y_local).transpose(0, 1, 3, 2, 4)
    forward_y = forward_y.reshape(size, size)
    forward_x = ahead.reshape(size, size).T
    inverse_x = back.reshape(size, size).T
    inverse_y = back.reshape(2, pa_count, y_local, 2, grid_len).transpose(1, 0, 2, 3, 4)
    inverse_y = inverse_y.reshape(size, size)
    return [split_table(t) for t in (forward_z, forward_y, forward_x, inverse_x, inverse_y, inverse_z)]


def lane_iota(rows):
    return lax.broadcasted_iota(jnp.int32, (rows, LANES), 1)


def forward_z_kernel(x_local, y_local, plane_ref, high_ref, low_ref, out_ref):
    table = (high_ref[...], low_ref[...])
    half = LANES // 2
    per_comp = x_local * y_local
    stride = (COMPS // 2) * y_local
    first_half = lane_iota(half) < half
    for pair in range(y_local // 2):
        for tile in range(COMPS // 2):
            rows = [
                plane_ref[pl.ds((2 * tile + c) * per_comp + 2 * pair + y, x_local, stride=y_local), :]
                for y in range(2)
                for c in range(2)
            ]
            lines = split(jnp.concatenate(rows, axis=0))
            waves = product(table, lines, ((1,), (1,)))
            low_bins, high_bins = waves[:half], waves[half:]
            even = jnp.where(first_half, low_bins, pltpu.roll(high_bins, half, 1))
            odd = jnp.where(first_half, pltpu.roll(low_bins, half, 1), high_bins)
            base = tile * y_local + 2 * pair
            out_ref[pl.ds(base, half, stride=stride), :] = even
            out_ref[pl.ds(base + 1, half, stride=stride), :] = odd


def swap_blocks(tiles):
    lane = lane_iota(tiles[0].shape[0])
    lower = lane < LANES // 2
    even = (lane // (LANES // 4)) % 2 == 0
    tiles = list(tiles)
    for a, b in ((0, 2), (1, 3)):
        first, second = tiles[a], tiles[b]
        tiles[a] = jnp.where(lower, first, pltpu.roll(second, LANES // 2, 1))
        tiles[b] = jnp.where(lower, pltpu.roll(first, LANES // 2, 1), second)
    for a, b in ((0, 1), (2, 3)):
        first, second = tiles[a], tiles[b]
        tiles[a] = jnp.where(even, first, pltpu.roll(second, LANES // 4, 1))
        tiles[b] = jnp.where(even, pltpu.roll(first, 3 * LANES // 4, 1), second)
    return tiles


def spectral_kernel(
    gx_count,
    pa_count,
    y_local,
    freq_ref,
    data_ref,
    fyh_ref,
    fyl_ref,
    fxh_ref,
    fxl_ref,
    ixh_ref,
    ixl_ref,
    iyh_ref,
    iyl_ref,
    out_ref,
    waves,
):
    grid_len = LANES
    size = 2 * grid_len
    tile_count = COMPS // 2
    forward_y = (fyh_ref[...], fyl_ref[...])
    forward_x = (fxh_ref[...], fxl_ref[...])
    inverse_x = (ixh_ref[...], ixl_ref[...])
    inverse_y = (iyh_ref[...], iyl_ref[...])
    for tile in range(tile_count):
        blocks = []
        for g in range(gx_count):
            field = data_ref[pl.ds(g * pa_count, pa_count), :, tile, :, :].reshape(size, LANES)
            blocks.append(product(forward_y, split(field)))
        for slot, block in enumerate(swap_blocks(blocks)):
            rows = jnp.concatenate([block[:grid_len], block[grid_len:]], axis=1)
            waves[tile, slot] = product(split(rows), forward_x)

    def signed(index):
        plain = jnp.where(index < grid_len // 2, index, index - grid_len)
        return jnp.where(index == grid_len // 2, 0, plain).astype(jnp.float32)

    step = 16
    freq_x = signed(lax.broadcasted_iota(jnp.int32, (step, LANES), 1))
    row_index = lax.broadcasted_iota(jnp.int32, (step, LANES), 0)

    def operate(chunk, carry):
        start = pl.multiple_of(chunk * step, step)
        freq_y = signed(row_index + start)
        for j in range(2):
            freq_z = freq_ref[j]
            square = freq_x * freq_x + freq_y * freq_y + freq_z * freq_z
            inverse = 1.0 / jnp.maximum(square, 1.0)
            scaled = inverse * inverse * green_coef
            for part in range(2):
                lanes = pl.ds(part * LANES, LANES)

                def at(comp):
                    return (comp // 2, 2 * j + comp % 2, pl.ds(start, step), lanes)

                e_xx, e_yy, e_zz, e_yz, e_xz, e_xy = [waves[at(c)] for c in range(COMPS)]
                trace = (0.5 * lame_lambda) * (e_xx + e_yy + e_zz)
                n_x = (trace + e_xx) * freq_x + e_xy * freq_y + e_xz * freq_z
                n_y = e_xy * freq_x + (trace + e_yy) * freq_y + e_yz * freq_z
                n_z = e_xz * freq_x + e_yz * freq_y + (trace + e_zz) * freq_z
                along = (freq_x * n_x + freq_y * n_y + freq_z * n_z) * scaled
                u_x = n_x * inverse - freq_x * along
                u_y = n_y * inverse - freq_y * along
                u_z = n_z * inverse - freq_z * along
                waves[at(0)] = 2.0 * (freq_x * u_x)
                waves[at(1)] = 2.0 * (freq_y * u_y)
                waves[at(2)] = 2.0 * (freq_z * u_z)
                waves[at(3)] = freq_y * u_z + freq_z * u_y
                waves[at(4)] = freq_x * u_z + freq_z * u_x
                waves[at(5)] = freq_x * u_y + freq_y * u_x
        return carry

    lax.fori_loop(0, grid_len // step, operate, 0)

    for tile in range(tile_count):
        blocks = []
        for slot in range(4):
            rows = product(split(waves[tile, slot]), inverse_x)
            blocks.append(jnp.concatenate([rows[:, :LANES], rows[:, LANES:]], axis=0))
        for g, block in enumerate(swap_blocks(blocks)):
            field = product(inverse_y, split(block))
            out_ref[pl.ds(g * pa_count, pa_count), :, tile, :, :] = field.reshape(
                pa_count, 2, y_local, LANES
            )


def inverse_z_kernel(
    x_local,
    y_local,
    cell_count,
    voxel_ref,
    waves_ref,
    plastic_ref,
    high_ref,
    low_ref,
    stress_ref,
    own_ref,
    low_cells_ref,
    high_cells_ref,
):
    table = (high_ref[...], low_ref[...])
    half = LANES // 2
    per_comp = x_local * y_local
    stride = (COMPS // 2) * y_local
    first_half = lane_iota(half) < half
    for pair in range(y_local // 2):
        elastic = [[None] * COMPS for _ in range(2)]
        for tile in range(COMPS // 2):
            base = tile * y_local + 2 * pair
            even = waves_ref[pl.ds(base, half, stride=stride), :]
            odd = waves_ref[pl.ds(base + 1, half, stride=stride), :]
            low_bins = jnp.where(first_half, even, pltpu.roll(odd, half, 1))
            high_bins = jnp.where(first_half, pltpu.roll(even, half, 1), odd)
            turned = jnp.concatenate([low_bins, high_bins], axis=0).T
            lines = product(split(turned), table)
            for y in range(2):
                for c in range(2):
                    begin = (2 * y + c) * x_local
                    comp = 2 * tile + c
                    own = plastic_ref[
                        pl.ds(comp * per_comp + 2 * pair + y, x_local, stride=y_local), :
                    ]
                    elastic[y][comp] = lines[begin : begin + x_local] - own
        for y in range(2):
            trace = lame_lambda * (elastic[y][0] + elastic[y][1] + elastic[y][2])
            for comp in range(COMPS):
                value = 2.0 * shear_modulus * elastic[y][comp]
                if comp < 3:
                    value = value + trace
                stress_ref[
                    pl.ds(comp * per_comp + 2 * pair + y, x_local, stride=y_local), :
                ] = value

    cell_rows = per_comp // cell_count
    lane = lane_iota(LANES)
    row_lane = lax.broadcasted_iota(jnp.int32, (LANES, cell_rows), 1)
    for cell in range(cell_count):
        places = jnp.broadcast_to(voxel_ref[pl.ds(cell, 1), :], (LANES, LANES)).astype(jnp.float32)
        places = places.T.astype(jnp.int32)
        picked_row = lax.div(places, LANES)
        picked_lane = places - picked_row * LANES
        picked_row = picked_row[:, :1] - cell * cell_rows
        choose = (row_lane == picked_row).astype(jnp.bfloat16)
        keep = lane == picked_lane
        found = jnp.zeros((LANES, LANES), jnp.float32)
        for comp in range(COMPS):
            block = stress_ref[pl.ds(comp * per_comp + cell * cell_rows, cell_rows), :]
            high, low = split(block)
            rows = jnp.dot(choose, high, preferred_element_type=jnp.float32) + jnp.dot(
                choose, low, preferred_element_type=jnp.float32
            )
            value = jnp.sum(jnp.where(keep, rows, 0.0), axis=1, keepdims=True)
            found = jnp.where(lane == comp, value, found)
        found = found.T[:8]
        own_ref[cell] = found
        if cell < 2:
            low_cells_ref[cell] = found
        if cell >= cell_count - 2:
            high_cells_ref[cell - cell_count + 2] = found


def pair_moments(state, fixed, scratch, first, last):
    position = state
    columns, features, moments = scratch
    slots = position[0].shape[0]
    lines, burgers = fixed
    moved = [
        position[1] * lines[2] - position[2] * lines[1],
        position[2] * lines[0] - position[0] * lines[2],
        position[0] * lines[1] - position[1] * lines[0],
    ]
    for shift in range(3):
        offset = shift - 1.0
        shifted = [moved[0], moved[1] - offset * lines[2], moved[2] + offset * lines[1]]
        for b in range(3):
            for a in range(3):
                features[shift, pl.ds((3 * a + b) * slots, slots), :] = lines[a] * burgers[b]
                features[shift, pl.ds((9 + 3 * a + b) * slots, slots), :] = shifted[a] * burgers[b]
    for source in range(first - 1, last + 1):
        for a in range(3):
            row = position[a][source : source + 1]
            columns[source, a] = jnp.broadcast_to(row, (LANES, LANES)).T
    for target in range(first, last):
        weights = []
        sources = []
        own = [position[a][target : target + 1] for a in range(3)]
        for shift in range(3):
            source = target + shift - 1
            d_x = (own[0] - (shift - 1.0)) - columns[source, 0]
            d_y = own[1] - columns[source, 1]
            d_z = own[2] - columns[source, 2]
            inverse = lax.rsqrt(d_x * d_x + d_y * d_y + d_z * d_z + core_square)
            weights.append(inverse * inverse * inverse)
            sources.append(features[shift, pl.ds(source, FEATURES, stride=slots), :])
        total = product(
            split(jnp.concatenate(sources, axis=1)), split(jnp.concatenate(weights, axis=0))
        )
        moments[pl.ds(target * FEATURES, FEATURES), :] = total


def pair_field(position, moments):
    slots = position[0].shape[0]

    def feature(index):
        return moments[pl.ds(index, slots, stride=FEATURES), :]

    moment = [[None] * 3 for _ in range(3)]
    for b in range(3):
        g = [feature(3 * a + b) for a in range(3)]
        moment[0][b] = position[1] * g[2] - position[2] * g[1] - feature(9 + b)
        moment[1][b] = position[2] * g[0] - position[0] * g[2] - feature(12 + b)
        moment[2][b] = position[0] * g[1] - position[1] * g[0] - feature(15 + b)
    pairs = ((0, 0), (1, 1), (2, 2), (1, 2), (0, 2), (0, 1))
    return [pair_factor * (moment[a][b] + moment[b][a]) for a, b in pairs]


def load_fixed(start_ref):
    values = [start_ref[a] for a in range(9)]
    return values[0:3], values[3:6], values[6:9]


def clear(features, moments):
    features[...] = jnp.zeros_like(features)
    moments[...] = jnp.zeros_like(moments)


def first_field_kernel(last, start_ref, out_ref, columns, features, moments):
    clear(features, moments)
    position, lines, burgers = load_fixed(start_ref)
    pair_moments(position, (lines, burgers), (columns, features, moments), 1, last)
    for comp, value in enumerate(pair_field(position, moments)):
        out_ref[comp] = value


def moves_kernel(
    cell_count,
    start_ref,
    first_ref,
    left_ref,
    own_ref,
    right_ref,
    out_ref,
    columns,
    features,
    moments,
    sampled_ref,
):
    clear(features, moments)
    position, lines, burgers = load_fixed(start_ref)
    initial = position
    sampled_ref[...] = jnp.zeros_like(sampled_ref)
    sampled_ref[pl.ds(8, 16), :] = left_ref[...].reshape(16, LANES)
    sampled_ref[pl.ds(24, 8 * cell_count), :] = own_ref[...].reshape(8 * cell_count, LANES)
    sampled_ref[pl.ds(24 + 8 * cell_count, 16), :] = right_ref[...].reshape(16, LANES)
    slots = position[0].shape[0]
    sampled = [sampled_ref[pl.ds(comp, slots, stride=8), :] for comp in range(COMPS)]
    for repeat in range(SUB):
        if repeat == 0:
            field = [first_ref[comp] for comp in range(COMPS)]
        else:
            pair_moments(
                position,
                (lines, burgers),
                (columns, features, moments),
                1 + repeat,
                cell_count + 5 - repeat,
            )
            field = pair_field(position, moments)
        sigma = [sampled[comp] + field[comp] for comp in range(COMPS)]
        traction = [
            sigma[full_index[a][0]] * burgers[0]
            + sigma[full_index[a][1]] * burgers[1]
            + sigma[full_index[a][2]] * burgers[2]
            for a in range(3)
        ]
        position = [
            position[0] + step_size * (traction[1] * lines[2] - traction[2] * lines[1]),
            position[1] + step_size * (traction[2] * lines[0] - traction[0] * lines[2]),
            position[2] + step_size * (traction[0] * lines[1] - traction[1] * lines[0]),
        ]
    for a in range(3):
        out_ref[a] = (position[a] - initial[a])[3 : 3 + cell_count]


def kernel_call(kernel, outs, scratch=(), flops=0, scalars=0, count=0):
    specs = [pl.BlockSpec(memory_space=pltpu.SMEM)] * scalars
    specs += [pl.BlockSpec(memory_space=pltpu.VMEM)] * (count - scalars)
    return pl.pallas_call(
        kernel,
        out_shape=outs,
        in_specs=specs,
        out_specs=jax.tree.map(lambda _: pl.BlockSpec(memory_space=pltpu.VMEM), outs),
        scratch_shapes=list(scratch),
        compiler_params=pltpu.CompilerParams(vmem_limit_bytes=VMEM_LIMIT),
        cost_estimate=pl.CostEstimate(flops=flops, bytes_accessed=1 << 20, transcendentals=0),
    )


def neighbours(low, high):
    count = lax.axis_size("gx")
    forward = [(i, (i + 1) % count) for i in range(count)]
    backward = [(target, source) for source, target in forward]
    return lax.ppermute(high, "gx", forward), lax.ppermute(low, "gx", backward)


def slab_body(plastic, offsets, lines, burgers, counts, voxels):
    f32 = jnp.float32
    comp_count, x_local, y_local, grid_len = plastic.shape
    gx_count = lax.axis_size("gx")
    pa_count = lax.axis_size("pa")
    devices = gx_count * pa_count
    cell_count, cap = voxels.shape[1:]
    rows = devices * 2 * (comp_count // 2) * y_local
    blocks = (devices, rows // devices, LANES)
    parts = (devices, 2, comp_count // 2, y_local, LANES)
    forward_z, forward_y, forward_x, inverse_x, inverse_y, inverse_z = [
        [jnp.asarray(t) for t in pair] for pair in tables(grid_len, pa_count, y_local)
    ]
    axes = ("gx", "pa")
    own = lax.axis_index(axes)
    bins = (own + devices * jnp.arange(2, dtype=jnp.int32)).astype(f32)
    flat_plastic = plastic.reshape(-1, grid_len)

    waves = kernel_call(
        functools.partial(forward_z_kernel, x_local, y_local),
        jax.ShapeDtypeStruct((rows, LANES), f32),
        count=3,
    )(flat_plastic, *forward_z)
    waves = lax.all_to_all(waves.reshape(blocks), axes, 0, 0, tiled=True)
    waves = kernel_call(
        functools.partial(spectral_kernel, gx_count, pa_count, y_local),
        jax.ShapeDtypeStruct(parts, f32),
        [pltpu.VMEM((comp_count // 2, 4, grid_len, 2 * grid_len), f32)],
        count=10,
        scalars=1,
    )(bins, waves.reshape(parts), *forward_y, *forward_x, *inverse_x, *inverse_y)
    waves = lax.all_to_all(waves.reshape(blocks), axes, 0, 0, tiled=True)

    live = (jnp.arange(cap, dtype=jnp.int32)[None, :] < counts[0][:, None]).astype(f32)
    start = jnp.concatenate([offsets[:, 0], lines[:, 0], burgers[:, 0] * live[None]], axis=0)
    below, above = neighbours(start[:, :3], start[:, cell_count - 3 :])
    padding = jnp.zeros((9, SLOTS - cell_count - 6, cap), f32)
    start = jnp.concatenate([below, start, above, padding], axis=1)
    pair_scratch = [
        pltpu.VMEM((SLOTS, 3, LANES, LANES), f32),
        pltpu.VMEM((3, FEATURES * SLOTS, LANES), f32),
        pltpu.VMEM((SLOTS * FEATURES, LANES), f32),
    ]
    first = kernel_call(
        functools.partial(first_field_kernel, cell_count + 5),
        jax.ShapeDtypeStruct((comp_count, SLOTS, cap), f32),
        pair_scratch,
        count=1,
        flops=1 << 28,
    )(start)

    end = jax.ShapeDtypeStruct((2, 8, cap), f32)
    stress, own_cells, low_cells, high_cells = kernel_call(
        functools.partial(inverse_z_kernel, x_local, y_local, cell_count),
        [
            jax.ShapeDtypeStruct(flat_plastic.shape, f32),
            jax.ShapeDtypeStruct((cell_count, 8, cap), f32),
            end,
            end,
        ],
        count=5,
    )(voxels[0], waves.reshape(rows, LANES), flat_plastic, *inverse_z)
    left, right = neighbours(low_cells, high_cells)
    moved = kernel_call(
        functools.partial(moves_kernel, cell_count),
        jax.ShapeDtypeStruct((3, cell_count, cap), f32),
        pair_scratch + [pltpu.VMEM((8 * SLOTS, LANES), f32)],
        count=5,
    )(start, first, left, own_cells, right)
    return (stress.reshape(plastic.shape), moved[:, None])


def fits(mesh, plastic, voxels):
    gx_count, pa_count = mesh.shape["gx"], mesh.shape["pa"]
    grid_len = plastic.shape[3]
    x_local, y_local = plastic.shape[1] // gx_count, plastic.shape[2] // pa_count
    cell_count = voxels.shape[1] // gx_count
    return (
        plastic.shape == (COMPS, LANES, LANES, LANES)
        and 4 * gx_count * pa_count == grid_len
        and 4 * x_local == LANES
        and y_local % 8 == 0
        and voxels.shape[2] == LANES
        and 3 <= cell_count <= SLOTS - 6
        and x_local % cell_count == 0
    )


def solution(mesh):
    placed = (
        P(None, "gx", "pa", None),
        P(None, "pa", "gx", None),
        P(None, "pa", "gx", None),
        P(None, "pa", "gx", None),
        P("pa", "gx"),
        P("pa", "gx", None),
    )

    def step(plastic, offsets, lines, burgers, counts, voxels):
        chosen = slab_body if fits(mesh, plastic, voxels) else body
        return jax.shard_map(
            chosen,
            mesh=mesh,
            in_specs=placed,
            out_specs=(P(None, "gx", "pa", None), P(None, "pa", "gx", None)),
            check_vma=False,
        )(plastic, offsets, lines, burgers, counts, voxels)

    return step
```

```python
import functools
import math

import jax
import jax.numpy as jnp
import ml_dtypes
import numpy as np
from jax import lax
from jax.experimental import pallas as pl
from jax.experimental.pallas import tpu as pltpu
from jax.sharding import PartitionSpec as P

SUB = 3


lame_lambda = 1.5
shear_modulus = 1.0
green_coef = 2.5 / 3.5
core_square = 0.09
pair_factor = 1.0 / (4.0 * math.pi)
step_size = 0.05
full_index = ((0, 5, 4), (5, 1, 3), (4, 3, 2))


def with_halo(block, sides, width):
    for axis, dim in sides:
        count = lax.axis_size(axis)
        forward = [(i, i + 1) for i in range(count - 1)]
        forward.append((count - 1, 0))
        backward = [(target, source) for source, target in forward]
        low = lax.ppermute(
            lax.slice_in_dim(block, block.shape[dim] - width, None, axis=dim), axis, forward
        )
        high = lax.ppermute(lax.slice_in_dim(block, 0, width, axis=dim), axis, backward)
        block = jnp.concatenate([low, block, high], axis=dim)
    return block


def stress_of(strain, freq_x, freq_y, freq_z):
    strain_xx, strain_yy, strain_zz = (strain[0], strain[1], strain[2])
    strain_yz, strain_xz, strain_xy = (strain[3], strain[4], strain[5])
    trace = strain_xx + strain_yy + strain_zz
    tau_xx = lame_lambda * trace + 2.0 * shear_modulus * strain_xx
    tau_yy = lame_lambda * trace + 2.0 * shear_modulus * strain_yy
    tau_zz = lame_lambda * trace + 2.0 * shear_modulus * strain_zz
    tau_yz = 2.0 * shear_modulus * strain_yz
    tau_xz = 2.0 * shear_modulus * strain_xz
    tau_xy = 2.0 * shear_modulus * strain_xy
    norm_x = tau_xx * freq_x + tau_xy * freq_y + tau_xz * freq_z
    norm_y = tau_xy * freq_x + tau_yy * freq_y + tau_yz * freq_z
    norm_z = tau_xz * freq_x + tau_yz * freq_y + tau_zz * freq_z
    square = freq_x * freq_x + freq_y * freq_y + freq_z * freq_z
    inverse = 1.0 / jnp.maximum(square, 1.0)
    along_k = (freq_x * norm_x + freq_y * norm_y + freq_z * norm_z) * inverse * inverse * green_coef

    def strain_term(first_q, second_q, first_n, second_n, plastic_part):
        total = (first_q * second_n + second_q * first_n) * inverse / (
            2.0 * shear_modulus
        ) - first_q * second_q * along_k
        return total - plastic_part

    el_xx = strain_term(freq_x, freq_x, norm_x, norm_x, strain_xx)
    el_yy = strain_term(freq_y, freq_y, norm_y, norm_y, strain_yy)
    el_zz = strain_term(freq_z, freq_z, norm_z, norm_z, strain_zz)
    el_yz = strain_term(freq_y, freq_z, norm_y, norm_z, strain_yz)
    el_xz = strain_term(freq_x, freq_z, norm_x, norm_z, strain_xz)
    el_xy = strain_term(freq_x, freq_y, norm_x, norm_y, strain_xy)
    el_trace = el_xx + el_yy + el_zz
    return jnp.stack(
        [
            lame_lambda * el_trace + 2.0 * shear_modulus * el_xx,
            lame_lambda * el_trace + 2.0 * shear_modulus * el_yy,
            lame_lambda * el_trace + 2.0 * shear_modulus * el_zz,
            2.0 * shear_modulus * el_yz,
            2.0 * shear_modulus * el_xz,
            2.0 * shear_modulus * el_xy,
        ]
    )


def advance(position, lines, burgers, sampled):
    cell_count = sampled.shape[1]
    unit_x = jnp.array([1.0, 0.0, 0.0], jnp.float32)[:, None, None]
    source = jnp.concatenate(
        [
            position[:, shifted : shifted + cell_count] + (shifted - 1.0) * unit_x
            for shifted in range(3)
        ],
        axis=2,
    )
    source_line = jnp.concatenate(
        [lines[:, shifted : shifted + cell_count] for shifted in range(3)], axis=2
    )
    source_burgers = jnp.concatenate(
        [burgers[:, shifted : shifted + cell_count] for shifted in range(3)], axis=2
    )
    target = position[:, 1 : cell_count + 1]
    own_line = lines[:, 1 : cell_count + 1]
    own_burgers = burgers[:, 1 : cell_count + 1]
    offset_vec = target[:, :, :, None] - source[:, :, None, :]
    radius = offset_vec[0] ** 2 + offset_vec[1] ** 2 + offset_vec[2] ** 2 + core_square
    weight = lax.rsqrt(radius) / radius
    line_b = source_line[:, :, None, :]
    cross = (
        jnp.stack(
            [
                offset_vec[1] * line_b[2] - offset_vec[2] * line_b[1],
                offset_vec[2] * line_b[0] - offset_vec[0] * line_b[2],
                offset_vec[0] * line_b[1] - offset_vec[1] * line_b[0],
            ]
        )
        * weight[None]
    )
    moment = jnp.einsum("acij,bcj->abci", cross, source_burgers, precision=lax.Precision.HIGHEST)
    pair_field = pair_factor * (moment + jnp.swapaxes(moment, 0, 1))
    traction = []
    for first in range(3):
        acc_row = jnp.zeros_like(target[0])
        for second in range(3):
            acc_row = (
                acc_row
                + (sampled[full_index[first][second]] + pair_field[first, second])
                * own_burgers[second]
            )
        traction.append(acc_row)
    force_x = traction[1] * own_line[2] - traction[2] * own_line[1]
    force_y = traction[2] * own_line[0] - traction[0] * own_line[2]
    force_z = traction[0] * own_line[1] - traction[1] * own_line[0]
    return target + step_size * jnp.stack([force_x, force_y, force_z])


def phases(row_index, col_index, grid_len):
    product = row_index[:, None] * col_index[None, :] % grid_len
    angle = product.astype(jnp.float32) * (2.0 * math.pi / grid_len)
    return (jnp.cos(angle), jnp.sin(angle))


def transform_last(field, matrix):
    shape = field.shape
    flat = field.reshape(-1, shape[-2] * shape[-1])
    result = jnp.dot(flat, matrix, precision=lax.Precision.HIGHEST)
    return result.reshape(shape[:-2] + (2, matrix.shape[1] // 2))


def body(plastic, offsets, lines, burgers, counts, voxels):
    grid_len = plastic.shape[3]
    pa_count = lax.axis_size("pa")
    grid_index = jnp.arange(grid_len, dtype=jnp.int32)
    bin_count = grid_len // 2 + pa_count
    bin_index = jnp.arange(bin_count, dtype=jnp.int32)
    kept_bins = (bin_index <= grid_len // 2).astype(jnp.float32)
    weights = jnp.where((bin_index == 0) | (bin_index == grid_len // 2), 1.0, 2.0) * kept_bins
    front_cos, front_sin = phases(grid_index, bin_index, grid_len)
    front_table = jnp.concatenate(
        [front_cos * kept_bins[None, :], -front_sin * kept_bins[None, :]], axis=1
    )
    final_cos, final_sin = phases(bin_index, grid_index, grid_len)
    final_table = (
        jnp.concatenate([final_cos * weights[:, None], -final_sin * weights[:, None]], axis=0)
        / grid_len
    )
    turn_cos, turn_sin = phases(grid_index, grid_index, grid_len)
    ahead_table = jnp.block([[turn_cos, -turn_sin], [turn_sin, turn_cos]])
    return_table = jnp.block([[turn_cos, turn_sin], [-turn_sin, turn_cos]]) / grid_len
    comp_count, x_local, y_local = (plastic.shape[0], plastic.shape[1], plastic.shape[2])
    field = jnp.dot(plastic.reshape(-1, grid_len), front_table, precision=lax.Precision.HIGHEST)
    field = field.reshape(comp_count, x_local, y_local, 2, bin_count)
    field = lax.all_to_all(field, "pa", split_axis=4, concat_axis=2, tiled=True)
    field = jnp.transpose(field, (0, 1, 4, 3, 2))
    field = transform_last(field, ahead_table)
    field = lax.all_to_all(field, "gx", split_axis=4, concat_axis=1, tiled=True)
    field = jnp.transpose(field, (0, 4, 2, 3, 1))
    field = transform_last(field, ahead_table)
    y_count = field.shape[1]
    z_count = field.shape[2]
    signed = jnp.where(
        grid_index < grid_len // 2,
        grid_index,
        jnp.where(grid_index == grid_len // 2, 0, grid_index - grid_len),
    ).astype(jnp.float32)
    freq_x = signed[None, None, :]
    freq_y = lax.dynamic_slice_in_dim(signed, lax.axis_index("gx") * y_count, y_count)[
        :, None, None
    ]
    freq_z = lax.dynamic_slice_in_dim(signed, lax.axis_index("pa") * z_count, z_count)[
        None, :, None
    ]
    real_part = stress_of(field[:, :, :, 0], freq_x, freq_y, freq_z)
    imag_part = stress_of(field[:, :, :, 1], freq_x, freq_y, freq_z)
    field = jnp.stack([real_part, imag_part], axis=3)
    field = transform_last(field, return_table)
    field = lax.all_to_all(field, "gx", split_axis=4, concat_axis=1, tiled=True)
    field = jnp.transpose(field, (0, 4, 2, 3, 1))
    field = transform_last(field, return_table)
    field = lax.all_to_all(field, "pa", split_axis=4, concat_axis=2, tiled=True)
    field = jnp.transpose(field, (0, 1, 4, 3, 2))
    flat = field.reshape(-1, 2 * bin_count)
    stress = jnp.dot(flat, final_table, precision=lax.Precision.HIGHEST).reshape(
        comp_count, x_local, y_local, grid_len
    )
    cell_count = offsets.shape[2]
    width_cap = offsets.shape[3]
    flat_stress = stress.reshape(6, -1)
    sampled = jnp.take(flat_stress, voxels.reshape(-1), axis=1).reshape(6, cell_count, width_cap)
    live_mask = (jnp.arange(width_cap, dtype=jnp.int32)[None, :] < counts[0][:, None]).astype(
        jnp.float32
    )
    initial = offsets[:, 0]
    line_dirs = lines[:, 0]
    masked = burgers[:, 0] * live_mask[None]
    fixed_rim = with_halo(jnp.concatenate([line_dirs, masked], axis=0), (("gx", 1),), 1)
    position = initial
    for repeat in range(SUB):
        widened = with_halo(position, (("gx", 1),), 1)
        position = advance(widened, fixed_rim[0:3], fixed_rim[3:6], sampled)
    moved = position - initial
    return (stress, moved[:, None])


LANES = 128
COMPS = 6
FEATURES = 24
SLOTS = 16
VMEM_LIMIT = 48 * 1024 * 1024
VMEM_WHOLE = 63 * 1024 * 1024


def split(value):
    high = value.astype(jnp.bfloat16)
    low = (value - high.astype(jnp.float32)).astype(jnp.bfloat16)
    return high, low


def split_table(table):
    table = np.asarray(table, np.float32)
    high = table.astype(ml_dtypes.bfloat16)
    low = (table - high.astype(np.float32)).astype(ml_dtypes.bfloat16)
    return np.stack([high, low])


def product(left, right, dims=((1,), (0,))):
    left_high, left_low = left
    right_high, right_low = right
    left_all = jnp.concatenate([left_high, left_high, left_low], axis=dims[0][0])
    right_all = jnp.concatenate([right_high, right_low, right_high], axis=dims[1][0])
    return lax.dot_general(
        left_all, right_all, (dims, ((), ())), preferred_element_type=jnp.float32
    )


def tables(grid_len, pa_count, y_local):
    index = np.arange(grid_len)
    bins = np.arange(grid_len // 2)
    angle = 2.0 * np.pi * (np.outer(bins, index) % grid_len) / grid_len
    nyquist = 1.0 - 2.0 * (index % 2)
    forward_z = np.stack([np.cos(angle), -np.sin(angle)], axis=1)
    forward_z[0, 1] = nyquist
    inverse_z = 2.0 * forward_z / grid_len
    inverse_z[0] = forward_z[0] / grid_len
    forward_z = forward_z.reshape(grid_len, grid_len)
    inverse_z = inverse_z.reshape(grid_len, grid_len)
    turn = 2.0 * np.pi * (np.outer(index, index) % grid_len) / grid_len
    cos, sin = np.cos(turn), np.sin(turn)
    ahead = np.array([[cos, sin], [-sin, cos]]).transpose(0, 2, 1, 3)
    back = np.array([[cos, -sin], [sin, cos]]).transpose(0, 2, 1, 3) / grid_len
    size = 2 * grid_len
    forward_y = ahead.reshape(2, grid_len, 2, pa_count, y_local).transpose(0, 1, 3, 2, 4)
    forward_y = forward_y.reshape(size, size)
    forward_x = ahead.reshape(size, size).T
    inverse_x = back.reshape(size, size).T
    inverse_y = back.reshape(2, pa_count, y_local, 2, grid_len).transpose(1, 0, 2, 3, 4)
    inverse_y = inverse_y.reshape(size, size)
    return [split_table(t) for t in (forward_z, forward_y, forward_x, inverse_x, inverse_y, inverse_z)]


def lane_iota(rows):
    return lax.broadcasted_iota(jnp.int32, (rows, LANES), 1)


def forward_z_kernel(
    x_local,
    y_local,
    plane_ref,
    table_ref,
    out_ref,
    planes,
    table,
    table_sem,
    in_sems,
):
    half = LANES // 2
    tiles = COMPS // 2
    per_comp = x_local * y_local
    first_half = lane_iota(half) < half
    fetch_table = pltpu.make_async_copy(table_ref, table, table_sem)
    fetch_table.start()
    fetches = []
    for tile in range(tiles):
        span = pl.ds(2 * tile * per_comp, 2 * per_comp)
        fetches.append(
            pltpu.make_async_copy(plane_ref.at[span], planes.at[span], in_sems.at[tile])
        )
        fetches[-1].start()
    fetch_table.wait()
    stride = tiles * y_local
    for tile in range(tiles):
        fetches[tile].wait()
        for base in range(0, y_local, 4):
            rows = [
                planes[pl.ds((2 * tile + c) * per_comp + base + y, x_local, stride=y_local), :]
                for y in range(4)
                for c in range(2)
            ]
            lines = split(jnp.concatenate(rows, axis=0))
            waves = product((table[0], table[1]), lines, ((1,), (1,)))
            for y in range(0, 4, 2):
                begin = y * LANES // 2
                low_bins = waves[:half, begin : begin + LANES]
                high_bins = waves[half:, begin : begin + LANES]
                even = jnp.where(first_half, low_bins, pltpu.roll(high_bins, half, 1))
                odd = jnp.where(first_half, pltpu.roll(low_bins, half, 1), high_bins)
                begin = tile * y_local + base + y
                out_ref[pl.ds(begin, half, stride=stride), :] = even
                out_ref[pl.ds(begin + 1, half, stride=stride), :] = odd


def swap_blocks(tiles):
    lane = lane_iota(tiles[0].shape[0])
    lower = lane < LANES // 2
    even = (lane // (LANES // 4)) % 2 == 0
    tiles = list(tiles)
    for a, b in ((0, 2), (1, 3)):
        first, second = tiles[a], tiles[b]
        tiles[a] = jnp.where(lower, first, pltpu.roll(second, LANES // 2, 1))
        tiles[b] = jnp.where(lower, pltpu.roll(first, LANES // 2, 1), second)
    for a, b in ((0, 1), (2, 3)):
        first, second = tiles[a], tiles[b]
        tiles[a] = jnp.where(even, first, pltpu.roll(second, LANES // 4, 1))
        tiles[b] = jnp.where(even, pltpu.roll(first, 3 * LANES // 4, 1), second)
    return tiles


def spectral_kernel(
    gx_count,
    pa_count,
    y_local,
    freq_ref,
    data_ref,
    forward_y_ref,
    forward_x_ref,
    inverse_x_ref,
    inverse_y_ref,
    out_ref,
    waves,
    blocks_ref,
    sems,
):
    grid_len = LANES
    size = 2 * grid_len
    tile_count = COMPS // 2
    forward_y = (forward_y_ref[0], forward_y_ref[1])
    forward_x = (forward_x_ref[0], forward_x_ref[1])
    inverse_x = (inverse_x_ref[0], inverse_x_ref[1])
    inverse_y = (inverse_y_ref[0], inverse_y_ref[1])
    for tile in range(tile_count):
        fields = [
            data_ref[pl.ds(g * pa_count, pa_count), :, tile, :, :].reshape(size, LANES)
            for g in range(gx_count)
        ]
        wide = product(forward_y, split(jnp.concatenate(fields, axis=1)))
        blocks = [wide[:, g * LANES : (g + 1) * LANES] for g in range(gx_count)]
        for slot, block in enumerate(swap_blocks(blocks)):
            rows = jnp.concatenate([block[:grid_len], block[grid_len:]], axis=1)
            waves[tile, slot] = product(split(rows), forward_x)

    def signed(index):
        plain = jnp.where(index < grid_len // 2, index, index - grid_len)
        return jnp.where(index == grid_len // 2, 0, plain).astype(jnp.float32)

    step = 16
    freq_x = signed(lax.broadcasted_iota(jnp.int32, (step, LANES), 1))
    row_index = lax.broadcasted_iota(jnp.int32, (step, LANES), 0)

    def operate(chunk, carry):
        start = pl.multiple_of(chunk * step, step)
        freq_y = signed(row_index + start)
        for j in range(2):
            freq_z = freq_ref[j]
            square = freq_x * freq_x + freq_y * freq_y + freq_z * freq_z
            inverse = 1.0 / jnp.maximum(square, 1.0)
            scaled = inverse * inverse * green_coef
            for part in range(2):
                lanes = pl.ds(part * LANES, LANES)

                def at(comp):
                    return (comp // 2, 2 * j + comp % 2, pl.ds(start, step), lanes)

                e_xx, e_yy, e_zz, e_yz, e_xz, e_xy = [waves[at(c)] for c in range(COMPS)]
                trace = (0.5 * lame_lambda) * (e_xx + e_yy + e_zz)
                n_x = (trace + e_xx) * freq_x + e_xy * freq_y + e_xz * freq_z
                n_y = e_xy * freq_x + (trace + e_yy) * freq_y + e_yz * freq_z
                n_z = e_xz * freq_x + e_yz * freq_y + (trace + e_zz) * freq_z
                along = (freq_x * n_x + freq_y * n_y + freq_z * n_z) * scaled
                u_x = n_x * inverse - freq_x * along
                u_y = n_y * inverse - freq_y * along
                u_z = n_z * inverse - freq_z * along
                waves[at(0)] = 2.0 * (freq_x * u_x)
                waves[at(1)] = 2.0 * (freq_y * u_y)
                waves[at(2)] = 2.0 * (freq_z * u_z)
                waves[at(3)] = freq_y * u_z + freq_z * u_y
                waves[at(4)] = freq_x * u_z + freq_z * u_x
                waves[at(5)] = freq_x * u_y + freq_y * u_x
        return carry

    lax.fori_loop(0, grid_len // step, operate, 0)

    stores = []
    for tile in range(tile_count):
        blocks = []
        for slot in range(4):
            rows = product(split(waves[tile, slot]), inverse_x)
            blocks.append(jnp.concatenate([rows[:, :LANES], rows[:, LANES:]], axis=0))
        wide = jnp.concatenate(swap_blocks(blocks), axis=1)
        wide = product(inverse_y, split(wide))
        for g in range(gx_count):
            blocks_ref[tile, pl.ds(g * size, size), :] = wide[:, g * LANES : (g + 1) * LANES]
        done = blocks_ref.at[tile].reshape(gx_count * pa_count, 2, y_local, LANES)
        stores.append(pltpu.make_async_copy(done, out_ref.at[:, :, tile], sems.at[tile]))
        stores[-1].start()
    for store in stores:
        store.wait()


def inverse_z_kernel(
    x_local,
    y_local,
    cell_count,
    voxel_ref,
    waves_ref,
    plastic_ref,
    table_ref,
    stress_ref,
    own_ref,
    low_cells_ref,
    high_cells_ref,
):
    table = (table_ref[0], table_ref[1])
    half = LANES // 2
    per_comp = x_local * y_local
    stride = (COMPS // 2) * y_local
    first_half = lane_iota(half) < half
    for pair in range(y_local // 2):
        elastic = [[None] * COMPS for _ in range(2)]
        for tile in range(COMPS // 2):
            base = tile * y_local + 2 * pair
            even = waves_ref[pl.ds(base, half, stride=stride), :]
            odd = waves_ref[pl.ds(base + 1, half, stride=stride), :]
            low_bins = jnp.where(first_half, even, pltpu.roll(odd, half, 1))
            high_bins = jnp.where(first_half, pltpu.roll(even, half, 1), odd)
            turned = jnp.concatenate([low_bins, high_bins], axis=0).T
            lines = product(split(turned), table)
            for y in range(2):
                for c in range(2):
                    begin = (2 * y + c) * x_local
                    comp = 2 * tile + c
                    own = plastic_ref[
                        pl.ds(comp * per_comp + 2 * pair + y, x_local, stride=y_local), :
                    ]
                    elastic[y][comp] = lines[begin : begin + x_local] - own
        for y in range(2):
            trace = lame_lambda * (elastic[y][0] + elastic[y][1] + elastic[y][2])
            for comp in range(COMPS):
                value = 2.0 * shear_modulus * elastic[y][comp]
                if comp < 3:
                    value = value + trace
                stress_ref[
                    pl.ds(comp * per_comp + 2 * pair + y, x_local, stride=y_local), :
                ] = value

    cell_rows = per_comp // cell_count
    lane = lane_iota(LANES)
    row_lane = lax.broadcasted_iota(jnp.int32, (LANES, cell_rows), 1)
    for cell in range(cell_count):
        places = jnp.broadcast_to(voxel_ref[pl.ds(cell, 1), :], (LANES, LANES)).astype(jnp.float32)
        places = places.T.astype(jnp.int32)
        picked_row = lax.div(places, LANES)
        picked_lane = places - picked_row * LANES
        picked_row = picked_row[:, :1] - cell * cell_rows
        choose = (row_lane == picked_row).astype(jnp.bfloat16)
        keep = lane == picked_lane
        found = jnp.zeros((LANES, LANES), jnp.float32)
        for comp in range(COMPS):
            block = stress_ref[pl.ds(comp * per_comp + cell * cell_rows, cell_rows), :]
            high, low = split(block)
            rows = jnp.dot(choose, high, preferred_element_type=jnp.float32) + jnp.dot(
                choose, low, preferred_element_type=jnp.float32
            )
            value = jnp.sum(jnp.where(keep, rows, 0.0), axis=1, keepdims=True)
            found = jnp.where(lane == comp, value, found)
        found = found.T[:8]
        own_ref[cell] = found
        if cell < 2:
            low_cells_ref[cell] = found
        if cell >= cell_count - 2:
            high_cells_ref[cell - cell_count + 2] = found


def pair_moments(state, fixed, scratch, first, last):
    position = state
    columns, features, moments = scratch
    slots = position[0].shape[0]
    lines, burgers = fixed
    moved = [
        position[1] * lines[2] - position[2] * lines[1],
        position[2] * lines[0] - position[0] * lines[2],
        position[0] * lines[1] - position[1] * lines[0],
    ]
    for shift in range(3):
        offset = shift - 1.0
        shifted = [moved[0], moved[1] - offset * lines[2], moved[2] + offset * lines[1]]
        for b in range(3):
            for a in range(3):
                features[shift, pl.ds((3 * a + b) * slots, slots), :] = lines[a] * burgers[b]
                features[shift, pl.ds((9 + 3 * a + b) * slots, slots), :] = shifted[a] * burgers[b]
    for source in range(first - 1, last + 1):
        for a in range(3):
            row = position[a][source : source + 1]
            columns[source, a] = jnp.broadcast_to(row, (LANES, LANES)).T
    for target in range(first, last):
        weights = []
        sources = []
        own = [position[a][target : target + 1] for a in range(3)]
        for shift in range(3):
            source = target + shift - 1
            d_x = (own[0] - (shift - 1.0)) - columns[source, 0]
            d_y = own[1] - columns[source, 1]
            d_z = own[2] - columns[source, 2]
            inverse = lax.rsqrt(d_x * d_x + d_y * d_y + d_z * d_z + core_square)
            weights.append(inverse * inverse * inverse)
            sources.append(features[shift, pl.ds(source, FEATURES, stride=slots), :])
        total = product(
            split(jnp.concatenate(sources, axis=1)), split(jnp.concatenate(weights, axis=0))
        )
        moments[pl.ds(target * FEATURES, FEATURES), :] = total


def pair_field(position, moments):
    slots = position[0].shape[0]

    def feature(index):
        return moments[pl.ds(index, slots, stride=FEATURES), :]

    moment = [[None] * 3 for _ in range(3)]
    for b in range(3):
        g = [feature(3 * a + b) for a in range(3)]
        moment[0][b] = position[1] * g[2] - position[2] * g[1] - feature(9 + b)
        moment[1][b] = position[2] * g[0] - position[0] * g[2] - feature(12 + b)
        moment[2][b] = position[0] * g[1] - position[1] * g[0] - feature(15 + b)
    pairs = ((0, 0), (1, 1), (2, 2), (1, 2), (0, 2), (0, 1))
    return [pair_factor * (moment[a][b] + moment[b][a]) for a, b in pairs]


def load_fixed(start_ref):
    values = [start_ref[a] for a in range(9)]
    return values[0:3], values[3:6], values[6:9]


def clear(features, moments):
    features[...] = jnp.zeros_like(features)
    moments[...] = jnp.zeros_like(moments)


def first_field_kernel(last, start_ref, out_ref, columns, features, moments):
    clear(features, moments)
    position, lines, burgers = load_fixed(start_ref)
    pair_moments(position, (lines, burgers), (columns, features, moments), 1, last)
    for comp, value in enumerate(pair_field(position, moments)):
        out_ref[comp] = value


def moves_kernel(
    cell_count,
    start_ref,
    first_ref,
    left_ref,
    own_ref,
    right_ref,
    out_ref,
    columns,
    features,
    moments,
    sampled_ref,
):
    clear(features, moments)
    position, lines, burgers = load_fixed(start_ref)
    initial = position
    sampled_ref[...] = jnp.zeros_like(sampled_ref)
    sampled_ref[pl.ds(8, 16), :] = left_ref[...].reshape(16, LANES)
    sampled_ref[pl.ds(24, 8 * cell_count), :] = own_ref[...].reshape(8 * cell_count, LANES)
    sampled_ref[pl.ds(24 + 8 * cell_count, 16), :] = right_ref[...].reshape(16, LANES)
    slots = position[0].shape[0]
    sampled = [sampled_ref[pl.ds(comp, slots, stride=8), :] for comp in range(COMPS)]
    for repeat in range(SUB):
        if repeat == 0:
            field = [first_ref[comp] for comp in range(COMPS)]
        else:
            pair_moments(
                position,
                (lines, burgers),
                (columns, features, moments),
                1 + repeat,
                cell_count + 5 - repeat,
            )
            field = pair_field(position, moments)
        sigma = [sampled[comp] + field[comp] for comp in range(COMPS)]
        traction = [
            sigma[full_index[a][0]] * burgers[0]
            + sigma[full_index[a][1]] * burgers[1]
            + sigma[full_index[a][2]] * burgers[2]
            for a in range(3)
        ]
        position = [
            position[0] + step_size * (traction[1] * lines[2] - traction[2] * lines[1]),
            position[1] + step_size * (traction[2] * lines[0] - traction[0] * lines[2]),
            position[2] + step_size * (traction[0] * lines[1] - traction[1] * lines[0]),
        ]
    for a in range(3):
        out_ref[a] = (position[a] - initial[a])[3 : 3 + cell_count]


def kernel_call(kernel, outs, scratch=(), flops=0, places="", out_places="", limit=VMEM_LIMIT):
    spaces = {"s": pltpu.SMEM, "v": pltpu.VMEM, "h": pltpu.HBM}
    return pl.pallas_call(
        kernel,
        out_shape=outs,
        in_specs=[pl.BlockSpec(memory_space=spaces[p]) for p in places],
        out_specs=[pl.BlockSpec(memory_space=spaces[p]) for p in out_places],
        scratch_shapes=list(scratch),
        compiler_params=pltpu.CompilerParams(vmem_limit_bytes=limit),
        cost_estimate=pl.CostEstimate(flops=flops, bytes_accessed=1 << 20, transcendentals=0),
    )


def in_hbm(array):
    return pltpu.with_memory_space_constraint(array, pltpu.HBM)


def neighbours(low, high):
    count = lax.axis_size("gx")
    forward = [(i, (i + 1) % count) for i in range(count)]
    backward = [(target, source) for source, target in forward]
    return lax.ppermute(high, "gx", forward), lax.ppermute(low, "gx", backward)


def slab_body(plastic, offsets, lines, burgers, counts, voxels):
    f32 = jnp.float32
    comp_count, x_local, y_local, grid_len = plastic.shape
    gx_count = lax.axis_size("gx")
    pa_count = lax.axis_size("pa")
    devices = gx_count * pa_count
    cell_count, cap = voxels.shape[1:]
    tiles = comp_count // 2
    rows = devices * 2 * tiles * y_local
    blocks = (devices, rows // devices, LANES)
    parts = (devices, 2, tiles, y_local, LANES)
    forward_z, forward_y, forward_x, inverse_x, inverse_y, inverse_z = [
        jnp.asarray(t) for t in tables(grid_len, pa_count, y_local)
    ]
    axes = ("gx", "pa")
    own = lax.axis_index(axes)
    bins = (own + devices * jnp.arange(2, dtype=jnp.int32)).astype(f32)
    flat_plastic = plastic.reshape(-1, grid_len)
    tile_sems = pltpu.SemaphoreType.DMA((tiles,))

    bins, flat_plastic = lax.optimization_barrier((bins, flat_plastic))

    (waves,) = kernel_call(
        functools.partial(forward_z_kernel, x_local, y_local),
        [pltpu.VMEM((rows, LANES), f32)],
        [
            pltpu.VMEM(flat_plastic.shape, f32),
            pltpu.VMEM(forward_z.shape, jnp.bfloat16),
            pltpu.SemaphoreType.DMA,
            tile_sems,
        ],
        places="hh",
        out_places="v",
    )(in_hbm(flat_plastic), in_hbm(forward_z))
    waves = lax.all_to_all(waves.reshape(blocks), axes, 0, 0, tiled=True)
    (waves,) = kernel_call(
        functools.partial(spectral_kernel, gx_count, pa_count, y_local),
        [jax.ShapeDtypeStruct(parts, f32)],
        [
            pltpu.VMEM((tiles, 4, grid_len, 2 * grid_len), f32),
            pltpu.VMEM((tiles, rows // tiles, LANES), f32),
            tile_sems,
        ],
        places="svvvvv",
        out_places="h",
    )(bins, waves.reshape(parts), forward_y, forward_x, inverse_x, inverse_y)
    waves, offsets, lines, burgers, counts = lax.optimization_barrier(
        (waves, offsets, lines, burgers, counts)
    )
    waves = lax.all_to_all(waves.reshape(blocks), axes, 0, 0, tiled=True)

    live = (jnp.arange(cap, dtype=jnp.int32)[None, :] < counts[0][:, None]).astype(f32)
    start = jnp.concatenate([offsets[:, 0], lines[:, 0], burgers[:, 0] * live[None]], axis=0)
    below, above = neighbours(start[:, :3], start[:, cell_count - 3 :])
    padding = jnp.zeros((9, SLOTS - cell_count - 6, cap), f32)
    start = jnp.concatenate([below, start, above, padding], axis=1)
    pair_scratch = [
        pltpu.VMEM((SLOTS, 3, LANES, LANES), f32),
        pltpu.VMEM((3, FEATURES * SLOTS, LANES), f32),
        pltpu.VMEM((SLOTS * FEATURES, LANES), f32),
    ]
    (first,) = kernel_call(
        functools.partial(first_field_kernel, cell_count + 5),
        [jax.ShapeDtypeStruct((comp_count, SLOTS, cap), f32)],
        pair_scratch,
        places="v",
        out_places="v",
    )(start)

    end = jax.ShapeDtypeStruct((2, 8, cap), f32)
    stress, own_cells, low_cells, high_cells = kernel_call(
        functools.partial(inverse_z_kernel, x_local, y_local, cell_count),
        [
            jax.ShapeDtypeStruct(flat_plastic.shape, f32),
            jax.ShapeDtypeStruct((cell_count, 8, cap), f32),
            end,
            end,
        ],
        places="vvvv",
        out_places="vvvv",
    )(voxels[0], waves.reshape(rows, LANES), flat_plastic, inverse_z)
    left, right = neighbours(low_cells, high_cells)
    (moved,) = kernel_call(
        functools.partial(moves_kernel, cell_count),
        [jax.ShapeDtypeStruct((3, cell_count, cap), f32)],
        pair_scratch + [pltpu.VMEM((8 * SLOTS, LANES), f32)],
        places="vvvvv",
        out_places="v",
    )(start, first, left, own_cells, right)
    return (stress.reshape(plastic.shape), moved[:, None])


def fits(mesh, plastic, voxels):
    gx_count, pa_count = mesh.shape["gx"], mesh.shape["pa"]
    grid_len = plastic.shape[3]
    x_local, y_local = plastic.shape[1] // gx_count, plastic.shape[2] // pa_count
    cell_count = voxels.shape[1] // gx_count
    return (
        plastic.shape == (COMPS, LANES, LANES, LANES)
        and 4 * gx_count * pa_count == grid_len
        and 4 * x_local == LANES
        and y_local % 8 == 0
        and voxels.shape[2] == LANES
        and 3 <= cell_count <= SLOTS - 6
        and x_local % cell_count == 0
    )


def solution(mesh):
    placed = (
        P(None, "gx", "pa", None),
        P(None, "pa", "gx", None),
        P(None, "pa", "gx", None),
        P(None, "pa", "gx", None),
        P("pa", "gx"),
        P("pa", "gx", None),
    )

    def step(plastic, offsets, lines, burgers, counts, voxels):
        chosen = slab_body if fits(mesh, plastic, voxels) else body
        return jax.shard_map(
            chosen,
            mesh=mesh,
            in_specs=placed,
            out_specs=(P(None, "gx", "pa", None), P(None, "pa", "gx", None)),
            check_vma=False,
        )(plastic, offsets, lines, burgers, counts, voxels)

    return step
```

```python
import functools
import math

import jax
import jax.numpy as jnp
import ml_dtypes
import numpy as np
from jax import lax
from jax.experimental import pallas as pl
from jax.experimental.pallas import tpu as pltpu
from jax.sharding import PartitionSpec as P

SUB = 3


lame_lambda = 1.5
shear_modulus = 1.0
green_coef = 2.5 / 3.5
core_square = 0.09
pair_factor = 1.0 / (4.0 * math.pi)
step_size = 0.05
full_index = ((0, 5, 4), (5, 1, 3), (4, 3, 2))


def with_halo(block, sides, width):
    for axis, dim in sides:
        count = lax.axis_size(axis)
        forward = [(i, i + 1) for i in range(count - 1)]
        forward.append((count - 1, 0))
        backward = [(target, source) for source, target in forward]
        low = lax.ppermute(
            lax.slice_in_dim(block, block.shape[dim] - width, None, axis=dim), axis, forward
        )
        high = lax.ppermute(lax.slice_in_dim(block, 0, width, axis=dim), axis, backward)
        block = jnp.concatenate([low, block, high], axis=dim)
    return block


def stress_of(strain, freq_x, freq_y, freq_z):
    strain_xx, strain_yy, strain_zz = (strain[0], strain[1], strain[2])
    strain_yz, strain_xz, strain_xy = (strain[3], strain[4], strain[5])
    trace = strain_xx + strain_yy + strain_zz
    tau_xx = lame_lambda * trace + 2.0 * shear_modulus * strain_xx
    tau_yy = lame_lambda * trace + 2.0 * shear_modulus * strain_yy
    tau_zz = lame_lambda * trace + 2.0 * shear_modulus * strain_zz
    tau_yz = 2.0 * shear_modulus * strain_yz
    tau_xz = 2.0 * shear_modulus * strain_xz
    tau_xy = 2.0 * shear_modulus * strain_xy
    norm_x = tau_xx * freq_x + tau_xy * freq_y + tau_xz * freq_z
    norm_y = tau_xy * freq_x + tau_yy * freq_y + tau_yz * freq_z
    norm_z = tau_xz * freq_x + tau_yz * freq_y + tau_zz * freq_z
    square = freq_x * freq_x + freq_y * freq_y + freq_z * freq_z
    inverse = 1.0 / jnp.maximum(square, 1.0)
    along_k = (freq_x * norm_x + freq_y * norm_y + freq_z * norm_z) * inverse * inverse * green_coef

    def strain_term(first_q, second_q, first_n, second_n, plastic_part):
        total = (first_q * second_n + second_q * first_n) * inverse / (
            2.0 * shear_modulus
        ) - first_q * second_q * along_k
        return total - plastic_part

    el_xx = strain_term(freq_x, freq_x, norm_x, norm_x, strain_xx)
    el_yy = strain_term(freq_y, freq_y, norm_y, norm_y, strain_yy)
    el_zz = strain_term(freq_z, freq_z, norm_z, norm_z, strain_zz)
    el_yz = strain_term(freq_y, freq_z, norm_y, norm_z, strain_yz)
    el_xz = strain_term(freq_x, freq_z, norm_x, norm_z, strain_xz)
    el_xy = strain_term(freq_x, freq_y, norm_x, norm_y, strain_xy)
    el_trace = el_xx + el_yy + el_zz
    return jnp.stack(
        [
            lame_lambda * el_trace + 2.0 * shear_modulus * el_xx,
            lame_lambda * el_trace + 2.0 * shear_modulus * el_yy,
            lame_lambda * el_trace + 2.0 * shear_modulus * el_zz,
            2.0 * shear_modulus * el_yz,
            2.0 * shear_modulus * el_xz,
            2.0 * shear_modulus * el_xy,
        ]
    )


def advance(position, lines, burgers, sampled):
    cell_count = sampled.shape[1]
    unit_x = jnp.array([1.0, 0.0, 0.0], jnp.float32)[:, None, None]
    source = jnp.concatenate(
        [
            position[:, shifted : shifted + cell_count] + (shifted - 1.0) * unit_x
            for shifted in range(3)
        ],
        axis=2,
    )
    source_line = jnp.concatenate(
        [lines[:, shifted : shifted + cell_count] for shifted in range(3)], axis=2
    )
    source_burgers = jnp.concatenate(
        [burgers[:, shifted : shifted + cell_count] for shifted in range(3)], axis=2
    )
    target = position[:, 1 : cell_count + 1]
    own_line = lines[:, 1 : cell_count + 1]
    own_burgers = burgers[:, 1 : cell_count + 1]
    offset_vec = target[:, :, :, None] - source[:, :, None, :]
    radius = offset_vec[0] ** 2 + offset_vec[1] ** 2 + offset_vec[2] ** 2 + core_square
    weight = lax.rsqrt(radius) / radius
    line_b = source_line[:, :, None, :]
    cross = (
        jnp.stack(
            [
                offset_vec[1] * line_b[2] - offset_vec[2] * line_b[1],
                offset_vec[2] * line_b[0] - offset_vec[0] * line_b[2],
                offset_vec[0] * line_b[1] - offset_vec[1] * line_b[0],
            ]
        )
        * weight[None]
    )
    moment = jnp.einsum("acij,bcj->abci", cross, source_burgers, precision=lax.Precision.HIGHEST)
    pair_field = pair_factor * (moment + jnp.swapaxes(moment, 0, 1))
    traction = []
    for first in range(3):
        acc_row = jnp.zeros_like(target[0])
        for second in range(3):
            acc_row = (
                acc_row
                + (sampled[full_index[first][second]] + pair_field[first, second])
                * own_burgers[second]
            )
        traction.append(acc_row)
    force_x = traction[1] * own_line[2] - traction[2] * own_line[1]
    force_y = traction[2] * own_line[0] - traction[0] * own_line[2]
    force_z = traction[0] * own_line[1] - traction[1] * own_line[0]
    return target + step_size * jnp.stack([force_x, force_y, force_z])


def phases(row_index, col_index, grid_len):
    product = row_index[:, None] * col_index[None, :] % grid_len
    angle = product.astype(jnp.float32) * (2.0 * math.pi / grid_len)
    return (jnp.cos(angle), jnp.sin(angle))


def transform_last(field, matrix):
    shape = field.shape
    flat = field.reshape(-1, shape[-2] * shape[-1])
    result = jnp.dot(flat, matrix, precision=lax.Precision.HIGHEST)
    return result.reshape(shape[:-2] + (2, matrix.shape[1] // 2))


def body(plastic, offsets, lines, burgers, counts, voxels):
    grid_len = plastic.shape[3]
    pa_count = lax.axis_size("pa")
    grid_index = jnp.arange(grid_len, dtype=jnp.int32)
    bin_count = grid_len // 2 + pa_count
    bin_index = jnp.arange(bin_count, dtype=jnp.int32)
    kept_bins = (bin_index <= grid_len // 2).astype(jnp.float32)
    weights = jnp.where((bin_index == 0) | (bin_index == grid_len // 2), 1.0, 2.0) * kept_bins
    front_cos, front_sin = phases(grid_index, bin_index, grid_len)
    front_table = jnp.concatenate(
        [front_cos * kept_bins[None, :], -front_sin * kept_bins[None, :]], axis=1
    )
    final_cos, final_sin = phases(bin_index, grid_index, grid_len)
    final_table = (
        jnp.concatenate([final_cos * weights[:, None], -final_sin * weights[:, None]], axis=0)
        / grid_len
    )
    turn_cos, turn_sin = phases(grid_index, grid_index, grid_len)
    ahead_table = jnp.block([[turn_cos, -turn_sin], [turn_sin, turn_cos]])
    return_table = jnp.block([[turn_cos, turn_sin], [-turn_sin, turn_cos]]) / grid_len
    comp_count, x_local, y_local = (plastic.shape[0], plastic.shape[1], plastic.shape[2])
    field = jnp.dot(plastic.reshape(-1, grid_len), front_table, precision=lax.Precision.HIGHEST)
    field = field.reshape(comp_count, x_local, y_local, 2, bin_count)
    field = lax.all_to_all(field, "pa", split_axis=4, concat_axis=2, tiled=True)
    field = jnp.transpose(field, (0, 1, 4, 3, 2))
    field = transform_last(field, ahead_table)
    field = lax.all_to_all(field, "gx", split_axis=4, concat_axis=1, tiled=True)
    field = jnp.transpose(field, (0, 4, 2, 3, 1))
    field = transform_last(field, ahead_table)
    y_count = field.shape[1]
    z_count = field.shape[2]
    signed = jnp.where(
        grid_index < grid_len // 2,
        grid_index,
        jnp.where(grid_index == grid_len // 2, 0, grid_index - grid_len),
    ).astype(jnp.float32)
    freq_x = signed[None, None, :]
    freq_y = lax.dynamic_slice_in_dim(signed, lax.axis_index("gx") * y_count, y_count)[
        :, None, None
    ]
    freq_z = lax.dynamic_slice_in_dim(signed, lax.axis_index("pa") * z_count, z_count)[
        None, :, None
    ]
    real_part = stress_of(field[:, :, :, 0], freq_x, freq_y, freq_z)
    imag_part = stress_of(field[:, :, :, 1], freq_x, freq_y, freq_z)
    field = jnp.stack([real_part, imag_part], axis=3)
    field = transform_last(field, return_table)
    field = lax.all_to_all(field, "gx", split_axis=4, concat_axis=1, tiled=True)
    field = jnp.transpose(field, (0, 4, 2, 3, 1))
    field = transform_last(field, return_table)
    field = lax.all_to_all(field, "pa", split_axis=4, concat_axis=2, tiled=True)
    field = jnp.transpose(field, (0, 1, 4, 3, 2))
    flat = field.reshape(-1, 2 * bin_count)
    stress = jnp.dot(flat, final_table, precision=lax.Precision.HIGHEST).reshape(
        comp_count, x_local, y_local, grid_len
    )
    cell_count = offsets.shape[2]
    width_cap = offsets.shape[3]
    flat_stress = stress.reshape(6, -1)
    sampled = jnp.take(flat_stress, voxels.reshape(-1), axis=1).reshape(6, cell_count, width_cap)
    live_mask = (jnp.arange(width_cap, dtype=jnp.int32)[None, :] < counts[0][:, None]).astype(
        jnp.float32
    )
    initial = offsets[:, 0]
    line_dirs = lines[:, 0]
    masked = burgers[:, 0] * live_mask[None]
    fixed_rim = with_halo(jnp.concatenate([line_dirs, masked], axis=0), (("gx", 1),), 1)
    position = initial
    for repeat in range(SUB):
        widened = with_halo(position, (("gx", 1),), 1)
        position = advance(widened, fixed_rim[0:3], fixed_rim[3:6], sampled)
    moved = position - initial
    return (stress, moved[:, None])


LANES = 128
COMPS = 6
FEATURES = 24
SLOTS = 16
VMEM_LIMIT = 48 * 1024 * 1024
VMEM_WHOLE = 63 * 1024 * 1024


def split(value):
    high = value.astype(jnp.bfloat16)
    low = (value - high.astype(jnp.float32)).astype(jnp.bfloat16)
    return high, low


def split_table(table):
    table = np.asarray(table, np.float32)
    high = table.astype(ml_dtypes.bfloat16)
    low = (table - high.astype(np.float32)).astype(ml_dtypes.bfloat16)
    return np.stack([high, low])


def product(left, right, dims=((1,), (0,))):
    left_high, left_low = left
    right_high, right_low = right
    left_all = jnp.concatenate([left_high, left_high, left_low], axis=dims[0][0])
    right_all = jnp.concatenate([right_high, right_low, right_high], axis=dims[1][0])
    return lax.dot_general(
        left_all, right_all, (dims, ((), ())), preferred_element_type=jnp.float32
    )


def tables(grid_len, pa_count, y_local):
    index = np.arange(grid_len)
    bins = np.arange(grid_len // 2)
    angle = 2.0 * np.pi * (np.outer(bins, index) % grid_len) / grid_len
    nyquist = 1.0 - 2.0 * (index % 2)
    forward_z = np.stack([np.cos(angle), -np.sin(angle)], axis=1)
    forward_z[0, 1] = nyquist
    inverse_z = 2.0 * forward_z / grid_len
    inverse_z[0] = forward_z[0] / grid_len
    forward_z = forward_z.reshape(grid_len, grid_len)
    inverse_z = inverse_z.reshape(grid_len, grid_len)
    turn = 2.0 * np.pi * (np.outer(index, index) % grid_len) / grid_len
    cos, sin = np.cos(turn), np.sin(turn)
    ahead = np.array([[cos, sin], [-sin, cos]]).transpose(0, 2, 1, 3)
    back = np.array([[cos, -sin], [sin, cos]]).transpose(0, 2, 1, 3) / grid_len
    size = 2 * grid_len
    forward_y = ahead.reshape(2, grid_len, 2, pa_count, y_local).transpose(3, 2, 4, 0, 1)
    forward_y = forward_y.reshape(size, size)
    inverse_y = back.reshape(2, pa_count, y_local, 2, grid_len).transpose(3, 4, 1, 0, 2)
    inverse_y = inverse_y.reshape(size, size)
    forward_x = ahead.reshape(size, size)
    inverse_x = back.reshape(size, size)
    return [split_table(t) for t in (forward_z, forward_y, forward_x, inverse_x, inverse_y, inverse_z)]


def lane_iota(rows):
    return lax.broadcasted_iota(jnp.int32, (rows, LANES), 1)


def forward_z_kernel(
    x_local,
    y_local,
    plane_ref,
    table_ref,
    out_ref,
    planes,
    table,
    table_sem,
    in_sems,
):
    half = LANES // 2
    tiles = COMPS // 2
    per_comp = x_local * y_local
    first_half = lane_iota(half) < half
    fetch_table = pltpu.make_async_copy(table_ref, table, table_sem)
    fetch_table.start()
    fetches = []
    for tile in range(tiles):
        span = pl.ds(2 * tile * per_comp, 2 * per_comp)
        fetches.append(
            pltpu.make_async_copy(plane_ref.at[span], planes.at[span], in_sems.at[tile])
        )
        fetches[-1].start()
    fetch_table.wait()
    stride = tiles * y_local
    for tile in range(tiles):
        fetches[tile].wait()
        for base in range(0, y_local, 4):
            rows = [
                planes[pl.ds((2 * tile + c) * per_comp + base + y, x_local, stride=y_local), :]
                for y in range(4)
                for c in range(2)
            ]
            lines = split(jnp.concatenate(rows, axis=0))
            waves = product((table[0], table[1]), lines, ((1,), (1,)))
            for y in range(0, 4, 2):
                begin = y * LANES // 2
                low_bins = waves[:half, begin : begin + LANES]
                high_bins = waves[half:, begin : begin + LANES]
                even = jnp.where(first_half, low_bins, pltpu.roll(high_bins, half, 1))
                odd = jnp.where(first_half, pltpu.roll(low_bins, half, 1), high_bins)
                begin = tile * y_local + base + y
                out_ref[pl.ds(begin, half, stride=stride), :] = even
                out_ref[pl.ds(begin + 1, half, stride=stride), :] = odd


def spectral_kernel(
    gx_count,
    pa_count,
    y_local,
    freq_ref,
    data_ref,
    forward_y_ref,
    forward_x_ref,
    inverse_x_ref,
    inverse_y_ref,
    out_ref,
    waves,
    blocks_ref,
    sems,
):
    grid_len = LANES
    size = 2 * grid_len
    tile_count = COMPS // 2
    forward_y = (forward_y_ref[0], forward_y_ref[1])
    forward_x = (forward_x_ref[0], forward_x_ref[1])
    inverse_x = (inverse_x_ref[0], inverse_x_ref[1])
    inverse_y = (inverse_y_ref[0], inverse_y_ref[1])
    x_local = grid_len // gx_count
    for tile in range(tile_count):
        fields = [
            data_ref[pl.ds(g * pa_count, pa_count), :, tile, :, :].reshape(size, LANES).T
            for g in range(gx_count)
        ]
        lines = product(split(jnp.concatenate(fields, axis=0)), forward_y)
        planes = []
        for slot in range(4):
            rows = [
                lines[g * LANES + slot * x_local :][:x_local] for g in range(gx_count)
            ]
            plane = jnp.concatenate(rows, axis=0)
            planes.append(jnp.concatenate([plane[:, :LANES], plane[:, LANES:]], axis=0))
        waves[tile] = product(forward_x, split(jnp.concatenate(planes, axis=1)))

    def signed(index):
        plain = jnp.where(index < grid_len // 2, index, index - grid_len)
        return jnp.where(index == grid_len // 2, 0, plain).astype(jnp.float32)

    step = 16
    freq_y = signed(lax.broadcasted_iota(jnp.int32, (step, LANES), 1))
    row_index = lax.broadcasted_iota(jnp.int32, (step, LANES), 0)

    def operate(chunk, carry):
        start = pl.multiple_of(chunk * step, step)
        freq_x = signed(row_index + start)
        for j in range(2):
            freq_z = freq_ref[j]
            square = freq_x * freq_x + freq_y * freq_y + freq_z * freq_z
            inverse = 1.0 / jnp.maximum(square, 1.0)
            scaled = inverse * inverse * green_coef
            for part in range(2):
                rows = pl.ds(part * grid_len + start, step)

                def at(comp):
                    return (comp // 2, rows, pl.ds((2 * j + comp % 2) * LANES, LANES))

                e_xx, e_yy, e_zz, e_yz, e_xz, e_xy = [waves[at(c)] for c in range(COMPS)]
                trace = (0.5 * lame_lambda) * (e_xx + e_yy + e_zz)
                n_x = (trace + e_xx) * freq_x + e_xy * freq_y + e_xz * freq_z
                n_y = e_xy * freq_x + (trace + e_yy) * freq_y + e_yz * freq_z
                n_z = e_xz * freq_x + e_yz * freq_y + (trace + e_zz) * freq_z
                along = (freq_x * n_x + freq_y * n_y + freq_z * n_z) * scaled
                u_x = n_x * inverse - freq_x * along
                u_y = n_y * inverse - freq_y * along
                u_z = n_z * inverse - freq_z * along
                waves[at(0)] = 2.0 * (freq_x * u_x)
                waves[at(1)] = 2.0 * (freq_y * u_y)
                waves[at(2)] = 2.0 * (freq_z * u_z)
                waves[at(3)] = freq_y * u_z + freq_z * u_y
                waves[at(4)] = freq_x * u_z + freq_z * u_x
                waves[at(5)] = freq_x * u_y + freq_y * u_x
        return carry

    lax.fori_loop(0, grid_len // step, operate, 0)

    stores = []
    for tile in range(tile_count):
        planes = product(inverse_x, split(waves[tile]))
        rows = []
        for g in range(gx_count):
            for slot in range(4):
                lanes = slice(slot * LANES, (slot + 1) * LANES)
                parts = [
                    planes[part * grid_len + g * x_local :][:x_local, lanes] for part in range(2)
                ]
                rows.append(jnp.concatenate(parts, axis=1))
        lines = product(split(jnp.concatenate(rows, axis=0)), inverse_y)
        for g in range(gx_count):
            blocks_ref[tile, pl.ds(g * size, size), :] = lines[g * LANES : (g + 1) * LANES].T
        done = blocks_ref.at[tile].reshape(gx_count * pa_count, 2, y_local, LANES)
        stores.append(pltpu.make_async_copy(done, out_ref.at[:, :, tile], sems.at[tile]))
        stores[-1].start()
    for store in stores:
        store.wait()


def inverse_z_kernel(
    x_local,
    y_local,
    cell_count,
    voxel_ref,
    waves_ref,
    plastic_ref,
    table_ref,
    stress_ref,
    own_ref,
    low_cells_ref,
    high_cells_ref,
):
    table = (table_ref[0], table_ref[1])
    half = LANES // 2
    per_comp = x_local * y_local
    stride = (COMPS // 2) * y_local
    first_half = lane_iota(half) < half
    for pair in range(y_local // 2):
        elastic = [[None] * COMPS for _ in range(2)]
        for tile in range(COMPS // 2):
            base = tile * y_local + 2 * pair
            even = waves_ref[pl.ds(base, half, stride=stride), :]
            odd = waves_ref[pl.ds(base + 1, half, stride=stride), :]
            low_bins = jnp.where(first_half, even, pltpu.roll(odd, half, 1))
            high_bins = jnp.where(first_half, pltpu.roll(even, half, 1), odd)
            turned = jnp.concatenate([low_bins, high_bins], axis=0).T
            lines = product(split(turned), table)
            for y in range(2):
                for c in range(2):
                    begin = (2 * y + c) * x_local
                    comp = 2 * tile + c
                    own = plastic_ref[
                        pl.ds(comp * per_comp + 2 * pair + y, x_local, stride=y_local), :
                    ]
                    elastic[y][comp] = lines[begin : begin + x_local] - own
        for y in range(2):
            trace = lame_lambda * (elastic[y][0] + elastic[y][1] + elastic[y][2])
            for comp in range(COMPS):
                value = 2.0 * shear_modulus * elastic[y][comp]
                if comp < 3:
                    value = value + trace
                stress_ref[
                    pl.ds(comp * per_comp + 2 * pair + y, x_local, stride=y_local), :
                ] = value

    cell_rows = per_comp // cell_count
    place = lax.broadcasted_iota(jnp.int32, (LANES, LANES), 0)
    row = lax.broadcasted_iota(jnp.int32, (cell_rows, LANES), 0)
    unused = jnp.zeros((8 - COMPS, LANES), jnp.float32)
    for cell in range(cell_count):
        voxel = voxel_ref[pl.ds(cell, 1), :]
        picked_row = lax.shift_right_logical(voxel, LANES.bit_length() - 1)
        picked_place = lax.bitwise_and(voxel, LANES - 1)
        choose = (place == picked_place).astype(jnp.bfloat16)
        keep = row == picked_row - cell * cell_rows
        blocks = [
            jnp.concatenate(
                split(stress_ref[pl.ds(comp * per_comp + cell * cell_rows, cell_rows), :]), axis=1
            )
            for comp in range(COMPS)
        ]
        picked = jnp.dot(
            jnp.concatenate(blocks, axis=0),
            jnp.concatenate([choose, choose], axis=0),
            preferred_element_type=jnp.float32,
        )
        found = [
            jnp.sum(
                jnp.where(keep, picked[comp * cell_rows : (comp + 1) * cell_rows], 0.0),
                axis=0,
                keepdims=True,
            )
            for comp in range(COMPS)
        ]
        found = jnp.concatenate(found + [unused], axis=0)
        own_ref[cell] = found
        if cell < 2:
            low_cells_ref[cell] = found
        if cell >= cell_count - 2:
            high_cells_ref[cell - cell_count + 2] = found


def pair_moments(state, fixed, scratch, first, last):
    position = state
    columns, features, moments = scratch
    slots = position[0].shape[0]
    lines, burgers = fixed
    moved = [
        position[1] * lines[2] - position[2] * lines[1],
        position[2] * lines[0] - position[0] * lines[2],
        position[0] * lines[1] - position[1] * lines[0],
    ]
    for shift in range(3):
        offset = shift - 1.0
        shifted = [moved[0], moved[1] - offset * lines[2], moved[2] + offset * lines[1]]
        for b in range(3):
            for a in range(3):
                features[shift, pl.ds((3 * a + b) * slots, slots), :] = lines[a] * burgers[b]
                features[shift, pl.ds((9 + 3 * a + b) * slots, slots), :] = shifted[a] * burgers[b]
    for source in range(first - 1, last + 1):
        for a in range(3):
            row = position[a][source : source + 1]
            columns[source, a] = jnp.broadcast_to(row, (LANES, LANES)).T
    for target in range(first, last):
        weights = []
        sources = []
        own = [position[a][target : target + 1] for a in range(3)]
        for shift in range(3):
            source = target + shift - 1
            d_x = (own[0] - (shift - 1.0)) - columns[source, 0]
            d_y = own[1] - columns[source, 1]
            d_z = own[2] - columns[source, 2]
            inverse = lax.rsqrt(d_x * d_x + d_y * d_y + d_z * d_z + core_square)
            weights.append(inverse * inverse * inverse)
            sources.append(features[shift, pl.ds(source, FEATURES, stride=slots), :])
        total = product(
            split(jnp.concatenate(sources, axis=1)), split(jnp.concatenate(weights, axis=0))
        )
        moments[pl.ds(target * FEATURES, FEATURES), :] = total


def pair_field(position, moments):
    slots = position[0].shape[0]

    def feature(index):
        return moments[pl.ds(index, slots, stride=FEATURES), :]

    moment = [[None] * 3 for _ in range(3)]
    for b in range(3):
        g = [feature(3 * a + b) for a in range(3)]
        moment[0][b] = position[1] * g[2] - position[2] * g[1] - feature(9 + b)
        moment[1][b] = position[2] * g[0] - position[0] * g[2] - feature(12 + b)
        moment[2][b] = position[0] * g[1] - position[1] * g[0] - feature(15 + b)
    pairs = ((0, 0), (1, 1), (2, 2), (1, 2), (0, 2), (0, 1))
    return [pair_factor * (moment[a][b] + moment[b][a]) for a, b in pairs]


def load_fixed(start_ref):
    values = [start_ref[a] for a in range(9)]
    return values[0:3], values[3:6], values[6:9]


def clear(features, moments):
    features[...] = jnp.zeros_like(features)
    moments[...] = jnp.zeros_like(moments)


def first_field_kernel(last, start_ref, out_ref, columns, features, moments):
    clear(features, moments)
    position, lines, burgers = load_fixed(start_ref)
    pair_moments(position, (lines, burgers), (columns, features, moments), 1, last)
    for comp, value in enumerate(pair_field(position, moments)):
        out_ref[comp] = value


def moves_kernel(
    cell_count,
    start_ref,
    first_ref,
    left_ref,
    own_ref,
    right_ref,
    out_ref,
    columns,
    features,
    moments,
    sampled_ref,
):
    clear(features, moments)
    position, lines, burgers = load_fixed(start_ref)
    initial = position
    sampled_ref[...] = jnp.zeros_like(sampled_ref)
    sampled_ref[pl.ds(8, 16), :] = left_ref[...].reshape(16, LANES)
    sampled_ref[pl.ds(24, 8 * cell_count), :] = own_ref[...].reshape(8 * cell_count, LANES)
    sampled_ref[pl.ds(24 + 8 * cell_count, 16), :] = right_ref[...].reshape(16, LANES)
    slots = position[0].shape[0]
    sampled = [sampled_ref[pl.ds(comp, slots, stride=8), :] for comp in range(COMPS)]
    for repeat in range(SUB):
        if repeat == 0:
            field = [first_ref[comp] for comp in range(COMPS)]
        else:
            pair_moments(
                position,
                (lines, burgers),
                (columns, features, moments),
                1 + repeat,
                cell_count + 5 - repeat,
            )
            field = pair_field(position, moments)
        sigma = [sampled[comp] + field[comp] for comp in range(COMPS)]
        traction = [
            sigma[full_index[a][0]] * burgers[0]
            + sigma[full_index[a][1]] * burgers[1]
            + sigma[full_index[a][2]] * burgers[2]
            for a in range(3)
        ]
        position = [
            position[0] + step_size * (traction[1] * lines[2] - traction[2] * lines[1]),
            position[1] + step_size * (traction[2] * lines[0] - traction[0] * lines[2]),
            position[2] + step_size * (traction[0] * lines[1] - traction[1] * lines[0]),
        ]
    for a in range(3):
        out_ref[a] = (position[a] - initial[a])[3 : 3 + cell_count]


def kernel_call(kernel, outs, scratch=(), flops=0, places="", out_places="", limit=VMEM_LIMIT):
    spaces = {"s": pltpu.SMEM, "v": pltpu.VMEM, "h": pltpu.HBM}
    return pl.pallas_call(
        kernel,
        out_shape=outs,
        in_specs=[pl.BlockSpec(memory_space=spaces[p]) for p in places],
        out_specs=[pl.BlockSpec(memory_space=spaces[p]) for p in out_places],
        scratch_shapes=list(scratch),
        compiler_params=pltpu.CompilerParams(vmem_limit_bytes=limit),
        cost_estimate=pl.CostEstimate(flops=flops, bytes_accessed=1 << 20, transcendentals=0),
    )


def in_hbm(array):
    return pltpu.with_memory_space_constraint(array, pltpu.HBM)


def neighbours(low, high):
    count = lax.axis_size("gx")
    forward = [(i, (i + 1) % count) for i in range(count)]
    backward = [(target, source) for source, target in forward]
    return lax.ppermute(high, "gx", forward), lax.ppermute(low, "gx", backward)


def slab_body(plastic, offsets, lines, burgers, counts, voxels):
    f32 = jnp.float32
    comp_count, x_local, y_local, grid_len = plastic.shape
    gx_count = lax.axis_size("gx")
    pa_count = lax.axis_size("pa")
    devices = gx_count * pa_count
    cell_count, cap = voxels.shape[1:]
    tiles = comp_count // 2
    rows = devices * 2 * tiles * y_local
    blocks = (devices, rows // devices, LANES)
    parts = (devices, 2, tiles, y_local, LANES)
    forward_z, forward_y, forward_x, inverse_x, inverse_y, inverse_z = [
        jnp.asarray(t) for t in tables(grid_len, pa_count, y_local)
    ]
    axes = ("gx", "pa")
    own = lax.axis_index(axes)
    bins = (own + devices * jnp.arange(2, dtype=jnp.int32)).astype(f32)
    flat_plastic = plastic.reshape(-1, grid_len)
    tile_sems = pltpu.SemaphoreType.DMA((tiles,))

    bins, flat_plastic = lax.optimization_barrier((bins, flat_plastic))

    (waves,) = kernel_call(
        functools.partial(forward_z_kernel, x_local, y_local),
        [pltpu.VMEM((rows, LANES), f32)],
        [
            pltpu.VMEM(flat_plastic.shape, f32),
            pltpu.VMEM(forward_z.shape, jnp.bfloat16),
            pltpu.SemaphoreType.DMA,
            tile_sems,
        ],
        places="hh",
        out_places="v",
    )(in_hbm(flat_plastic), in_hbm(forward_z))
    waves = lax.all_to_all(waves.reshape(blocks), axes, 0, 0, tiled=True)
    (waves,) = kernel_call(
        functools.partial(spectral_kernel, gx_count, pa_count, y_local),
        [jax.ShapeDtypeStruct(parts, f32)],
        [
            pltpu.VMEM((tiles, 2 * grid_len, 4 * LANES), f32),
            pltpu.VMEM((tiles, rows // tiles, LANES), f32),
            tile_sems,
        ],
        places="svvvvv",
        out_places="h",
    )(bins, waves.reshape(parts), forward_y, forward_x, inverse_x, inverse_y)
    waves, offsets, lines, burgers, counts = lax.optimization_barrier(
        (waves, offsets, lines, burgers, counts)
    )
    waves = lax.all_to_all(waves.reshape(blocks), axes, 0, 0, tiled=True)

    live = (jnp.arange(cap, dtype=jnp.int32)[None, :] < counts[0][:, None]).astype(f32)
    start = jnp.concatenate([offsets[:, 0], lines[:, 0], burgers[:, 0] * live[None]], axis=0)
    below, above = neighbours(start[:, :3], start[:, cell_count - 3 :])
    padding = jnp.zeros((9, SLOTS - cell_count - 6, cap), f32)
    start = jnp.concatenate([below, start, above, padding], axis=1)
    pair_scratch = [
        pltpu.VMEM((SLOTS, 3, LANES, LANES), f32),
        pltpu.VMEM((3, FEATURES * SLOTS, LANES), f32),
        pltpu.VMEM((SLOTS * FEATURES, LANES), f32),
    ]
    (first,) = kernel_call(
        functools.partial(first_field_kernel, cell_count + 5),
        [jax.ShapeDtypeStruct((comp_count, SLOTS, cap), f32)],
        pair_scratch,
        places="v",
        out_places="v",
    )(start)

    waves, first = lax.optimization_barrier((waves, first))
    end = jax.ShapeDtypeStruct((2, 8, cap), f32)
    stress, own_cells, low_cells, high_cells = kernel_call(
        functools.partial(inverse_z_kernel, x_local, y_local, cell_count),
        [
            pltpu.VMEM(flat_plastic.shape, f32),
            jax.ShapeDtypeStruct((cell_count, 8, cap), f32),
            end,
            end,
        ],
        places="vvvv",
        out_places="vvvv",
    )(voxels[0], waves.reshape(rows, LANES), flat_plastic, inverse_z)
    left, right = neighbours(low_cells, high_cells)
    (moved,) = kernel_call(
        functools.partial(moves_kernel, cell_count),
        [jax.ShapeDtypeStruct((3, cell_count, cap), f32)],
        pair_scratch + [pltpu.VMEM((8 * SLOTS, LANES), f32)],
        places="vvvvv",
        out_places="v",
    )(start, first, left, own_cells, right)
    return (stress.reshape(plastic.shape), moved[:, None])


def fits(mesh, plastic, voxels):
    gx_count, pa_count = mesh.shape["gx"], mesh.shape["pa"]
    grid_len = plastic.shape[3]
    x_local, y_local = plastic.shape[1] // gx_count, plastic.shape[2] // pa_count
    cell_count = voxels.shape[1] // gx_count
    return (
        plastic.shape == (COMPS, LANES, LANES, LANES)
        and 4 * gx_count * pa_count == grid_len
        and 4 * x_local == LANES
        and y_local % 8 == 0
        and voxels.shape[2] == LANES
        and 3 <= cell_count <= SLOTS - 6
        and x_local % cell_count == 0
    )


def solution(mesh):
    placed = (
        P(None, "gx", "pa", None),
        P(None, "pa", "gx", None),
        P(None, "pa", "gx", None),
        P(None, "pa", "gx", None),
        P("pa", "gx"),
        P("pa", "gx", None),
    )

    def step(plastic, offsets, lines, burgers, counts, voxels):
        chosen = slab_body if fits(mesh, plastic, voxels) else body
        return jax.shard_map(
            chosen,
            mesh=mesh,
            in_specs=placed,
            out_specs=(P(None, "gx", "pa", None), P(None, "pa", "gx", None)),
            check_vma=False,
        )(plastic, offsets, lines, burgers, counts, voxels)

    return step
```

```python
import functools
import math

import jax
import jax.numpy as jnp
import ml_dtypes
import numpy as np
from jax import lax
from jax.experimental import pallas as pl
from jax.experimental.pallas import tpu as pltpu
from jax.sharding import PartitionSpec as P

SUB = 3


lame_lambda = 1.5
shear_modulus = 1.0
green_coef = 2.5 / 3.5
core_square = 0.09
pair_factor = 1.0 / (4.0 * math.pi)
step_size = 0.05
full_index = ((0, 5, 4), (5, 1, 3), (4, 3, 2))


def with_halo(block, sides, width):
    for axis, dim in sides:
        count = lax.axis_size(axis)
        forward = [(i, i + 1) for i in range(count - 1)]
        forward.append((count - 1, 0))
        backward = [(target, source) for source, target in forward]
        low = lax.ppermute(
            lax.slice_in_dim(block, block.shape[dim] - width, None, axis=dim), axis, forward
        )
        high = lax.ppermute(lax.slice_in_dim(block, 0, width, axis=dim), axis, backward)
        block = jnp.concatenate([low, block, high], axis=dim)
    return block


def stress_of(strain, freq_x, freq_y, freq_z):
    strain_xx, strain_yy, strain_zz = (strain[0], strain[1], strain[2])
    strain_yz, strain_xz, strain_xy = (strain[3], strain[4], strain[5])
    trace = strain_xx + strain_yy + strain_zz
    tau_xx = lame_lambda * trace + 2.0 * shear_modulus * strain_xx
    tau_yy = lame_lambda * trace + 2.0 * shear_modulus * strain_yy
    tau_zz = lame_lambda * trace + 2.0 * shear_modulus * strain_zz
    tau_yz = 2.0 * shear_modulus * strain_yz
    tau_xz = 2.0 * shear_modulus * strain_xz
    tau_xy = 2.0 * shear_modulus * strain_xy
    norm_x = tau_xx * freq_x + tau_xy * freq_y + tau_xz * freq_z
    norm_y = tau_xy * freq_x + tau_yy * freq_y + tau_yz * freq_z
    norm_z = tau_xz * freq_x + tau_yz * freq_y + tau_zz * freq_z
    square = freq_x * freq_x + freq_y * freq_y + freq_z * freq_z
    inverse = 1.0 / jnp.maximum(square, 1.0)
    along_k = (freq_x * norm_x + freq_y * norm_y + freq_z * norm_z) * inverse * inverse * green_coef

    def strain_term(first_q, second_q, first_n, second_n, plastic_part):
        total = (first_q * second_n + second_q * first_n) * inverse / (
            2.0 * shear_modulus
        ) - first_q * second_q * along_k
        return total - plastic_part

    el_xx = strain_term(freq_x, freq_x, norm_x, norm_x, strain_xx)
    el_yy = strain_term(freq_y, freq_y, norm_y, norm_y, strain_yy)
    el_zz = strain_term(freq_z, freq_z, norm_z, norm_z, strain_zz)
    el_yz = strain_term(freq_y, freq_z, norm_y, norm_z, strain_yz)
    el_xz = strain_term(freq_x, freq_z, norm_x, norm_z, strain_xz)
    el_xy = strain_term(freq_x, freq_y, norm_x, norm_y, strain_xy)
    el_trace = el_xx + el_yy + el_zz
    return jnp.stack(
        [
            lame_lambda * el_trace + 2.0 * shear_modulus * el_xx,
            lame_lambda * el_trace + 2.0 * shear_modulus * el_yy,
            lame_lambda * el_trace + 2.0 * shear_modulus * el_zz,
            2.0 * shear_modulus * el_yz,
            2.0 * shear_modulus * el_xz,
            2.0 * shear_modulus * el_xy,
        ]
    )


def advance(position, lines, burgers, sampled):
    cell_count = sampled.shape[1]
    unit_x = jnp.array([1.0, 0.0, 0.0], jnp.float32)[:, None, None]
    source = jnp.concatenate(
        [
            position[:, shifted : shifted + cell_count] + (shifted - 1.0) * unit_x
            for shifted in range(3)
        ],
        axis=2,
    )
    source_line = jnp.concatenate(
        [lines[:, shifted : shifted + cell_count] for shifted in range(3)], axis=2
    )
    source_burgers = jnp.concatenate(
        [burgers[:, shifted : shifted + cell_count] for shifted in range(3)], axis=2
    )
    target = position[:, 1 : cell_count + 1]
    own_line = lines[:, 1 : cell_count + 1]
    own_burgers = burgers[:, 1 : cell_count + 1]
    offset_vec = target[:, :, :, None] - source[:, :, None, :]
    radius = offset_vec[0] ** 2 + offset_vec[1] ** 2 + offset_vec[2] ** 2 + core_square
    weight = lax.rsqrt(radius) / radius
    line_b = source_line[:, :, None, :]
    cross = (
        jnp.stack(
            [
                offset_vec[1] * line_b[2] - offset_vec[2] * line_b[1],
                offset_vec[2] * line_b[0] - offset_vec[0] * line_b[2],
                offset_vec[0] * line_b[1] - offset_vec[1] * line_b[0],
            ]
        )
        * weight[None]
    )
    moment = jnp.einsum("acij,bcj->abci", cross, source_burgers, precision=lax.Precision.HIGHEST)
    pair_field = pair_factor * (moment + jnp.swapaxes(moment, 0, 1))
    traction = []
    for first in range(3):
        acc_row = jnp.zeros_like(target[0])
        for second in range(3):
            acc_row = (
                acc_row
                + (sampled[full_index[first][second]] + pair_field[first, second])
                * own_burgers[second]
            )
        traction.append(acc_row)
    force_x = traction[1] * own_line[2] - traction[2] * own_line[1]
    force_y = traction[2] * own_line[0] - traction[0] * own_line[2]
    force_z = traction[0] * own_line[1] - traction[1] * own_line[0]
    return target + step_size * jnp.stack([force_x, force_y, force_z])


def phases(row_index, col_index, grid_len):
    product = row_index[:, None] * col_index[None, :] % grid_len
    angle = product.astype(jnp.float32) * (2.0 * math.pi / grid_len)
    return (jnp.cos(angle), jnp.sin(angle))


def transform_last(field, matrix):
    shape = field.shape
    flat = field.reshape(-1, shape[-2] * shape[-1])
    result = jnp.dot(flat, matrix, precision=lax.Precision.HIGHEST)
    return result.reshape(shape[:-2] + (2, matrix.shape[1] // 2))


def body(plastic, offsets, lines, burgers, counts, voxels):
    grid_len = plastic.shape[3]
    pa_count = lax.axis_size("pa")
    grid_index = jnp.arange(grid_len, dtype=jnp.int32)
    bin_count = grid_len // 2 + pa_count
    bin_index = jnp.arange(bin_count, dtype=jnp.int32)
    kept_bins = (bin_index <= grid_len // 2).astype(jnp.float32)
    weights = jnp.where((bin_index == 0) | (bin_index == grid_len // 2), 1.0, 2.0) * kept_bins
    front_cos, front_sin = phases(grid_index, bin_index, grid_len)
    front_table = jnp.concatenate(
        [front_cos * kept_bins[None, :], -front_sin * kept_bins[None, :]], axis=1
    )
    final_cos, final_sin = phases(bin_index, grid_index, grid_len)
    final_table = (
        jnp.concatenate([final_cos * weights[:, None], -final_sin * weights[:, None]], axis=0)
        / grid_len
    )
    turn_cos, turn_sin = phases(grid_index, grid_index, grid_len)
    ahead_table = jnp.block([[turn_cos, -turn_sin], [turn_sin, turn_cos]])
    return_table = jnp.block([[turn_cos, turn_sin], [-turn_sin, turn_cos]]) / grid_len
    comp_count, x_local, y_local = (plastic.shape[0], plastic.shape[1], plastic.shape[2])
    field = jnp.dot(plastic.reshape(-1, grid_len), front_table, precision=lax.Precision.HIGHEST)
    field = field.reshape(comp_count, x_local, y_local, 2, bin_count)
    field = lax.all_to_all(field, "pa", split_axis=4, concat_axis=2, tiled=True)
    field = jnp.transpose(field, (0, 1, 4, 3, 2))
    field = transform_last(field, ahead_table)
    field = lax.all_to_all(field, "gx", split_axis=4, concat_axis=1, tiled=True)
    field = jnp.transpose(field, (0, 4, 2, 3, 1))
    field = transform_last(field, ahead_table)
    y_count = field.shape[1]
    z_count = field.shape[2]
    signed = jnp.where(
        grid_index < grid_len // 2,
        grid_index,
        jnp.where(grid_index == grid_len // 2, 0, grid_index - grid_len),
    ).astype(jnp.float32)
    freq_x = signed[None, None, :]
    freq_y = lax.dynamic_slice_in_dim(signed, lax.axis_index("gx") * y_count, y_count)[
        :, None, None
    ]
    freq_z = lax.dynamic_slice_in_dim(signed, lax.axis_index("pa") * z_count, z_count)[
        None, :, None
    ]
    real_part = stress_of(field[:, :, :, 0], freq_x, freq_y, freq_z)
    imag_part = stress_of(field[:, :, :, 1], freq_x, freq_y, freq_z)
    field = jnp.stack([real_part, imag_part], axis=3)
    field = transform_last(field, return_table)
    field = lax.all_to_all(field, "gx", split_axis=4, concat_axis=1, tiled=True)
    field = jnp.transpose(field, (0, 4, 2, 3, 1))
    field = transform_last(field, return_table)
    field = lax.all_to_all(field, "pa", split_axis=4, concat_axis=2, tiled=True)
    field = jnp.transpose(field, (0, 1, 4, 3, 2))
    flat = field.reshape(-1, 2 * bin_count)
    stress = jnp.dot(flat, final_table, precision=lax.Precision.HIGHEST).reshape(
        comp_count, x_local, y_local, grid_len
    )
    cell_count = offsets.shape[2]
    width_cap = offsets.shape[3]
    flat_stress = stress.reshape(6, -1)
    sampled = jnp.take(flat_stress, voxels.reshape(-1), axis=1).reshape(6, cell_count, width_cap)
    live_mask = (jnp.arange(width_cap, dtype=jnp.int32)[None, :] < counts[0][:, None]).astype(
        jnp.float32
    )
    initial = offsets[:, 0]
    line_dirs = lines[:, 0]
    masked = burgers[:, 0] * live_mask[None]
    fixed_rim = with_halo(jnp.concatenate([line_dirs, masked], axis=0), (("gx", 1),), 1)
    position = initial
    for repeat in range(SUB):
        widened = with_halo(position, (("gx", 1),), 1)
        position = advance(widened, fixed_rim[0:3], fixed_rim[3:6], sampled)
    moved = position - initial
    return (stress, moved[:, None])


LANES = 128
COMPS = 6
FEATURES = 24
SLOTS = 16
VMEM_LIMIT = 48 * 1024 * 1024
VMEM_WHOLE = 63 * 1024 * 1024


def split(value):
    high = value.astype(jnp.bfloat16)
    low = (value - high.astype(jnp.float32)).astype(jnp.bfloat16)
    return high, low


def split_table(table):
    table = np.asarray(table, np.float32)
    high = table.astype(ml_dtypes.bfloat16)
    low = (table - high.astype(np.float32)).astype(ml_dtypes.bfloat16)
    return np.stack([high, low])


def product(left, right, dims=((1,), (0,))):
    left_high, left_low = left
    right_high, right_low = right
    left_all = jnp.concatenate([left_high, left_high, left_low], axis=dims[0][0])
    right_all = jnp.concatenate([right_high, right_low, right_high], axis=dims[1][0])
    return lax.dot_general(
        left_all, right_all, (dims, ((), ())), preferred_element_type=jnp.float32
    )


def tables(grid_len, pa_count, y_local):
    index = np.arange(grid_len)
    bins = np.arange(grid_len // 2)
    angle = 2.0 * np.pi * (np.outer(bins, index) % grid_len) / grid_len
    nyquist = 1.0 - 2.0 * (index % 2)
    forward_z = np.stack([np.cos(angle), -np.sin(angle)], axis=1)
    forward_z[0, 1] = nyquist
    inverse_z = 2.0 * forward_z / grid_len
    inverse_z[0] = forward_z[0] / grid_len
    forward_z = forward_z.reshape(grid_len, grid_len)
    inverse_z = inverse_z.reshape(grid_len, grid_len)
    turn = 2.0 * np.pi * (np.outer(index, index) % grid_len) / grid_len
    cos, sin = np.cos(turn), np.sin(turn)
    ahead = np.array([[cos, sin], [-sin, cos]]).transpose(0, 2, 1, 3)
    back = np.array([[cos, -sin], [sin, cos]]).transpose(0, 2, 1, 3) / grid_len
    size = 2 * grid_len
    forward_y = ahead.reshape(2, grid_len, 2, pa_count, y_local).transpose(3, 2, 4, 0, 1)
    forward_y = forward_y.reshape(size, size)
    inverse_y = back.reshape(2, pa_count, y_local, 2, grid_len).transpose(3, 4, 1, 0, 2)
    inverse_y = inverse_y.reshape(size, size)
    forward_x = ahead.reshape(size, size)
    inverse_x = back.reshape(size, size)
    return [split_table(t) for t in (forward_z, forward_y, forward_x, inverse_x, inverse_y, inverse_z)]


def lane_iota(rows):
    return lax.broadcasted_iota(jnp.int32, (rows, LANES), 1)


def forward_z_kernel(
    x_local,
    y_local,
    plane_ref,
    table_ref,
    out_ref,
    planes,
    table,
    table_sem,
    in_sems,
):
    half = LANES // 2
    tiles = COMPS // 2
    per_comp = x_local * y_local
    first_half = lane_iota(half) < half
    fetch_table = pltpu.make_async_copy(table_ref, table, table_sem)
    fetch_table.start()
    fetches = []
    for tile in range(tiles):
        span = pl.ds(2 * tile * per_comp, 2 * per_comp)
        fetches.append(
            pltpu.make_async_copy(plane_ref.at[span], planes.at[span], in_sems.at[tile])
        )
        fetches[-1].start()
    fetch_table.wait()
    stride = tiles * y_local
    for tile in range(tiles):
        fetches[tile].wait()
        for base in range(0, y_local, 4):
            rows = [
                planes[pl.ds((2 * tile + c) * per_comp + base + y, x_local, stride=y_local), :]
                for y in range(4)
                for c in range(2)
            ]
            lines = split(jnp.concatenate(rows, axis=0))
            waves = product((table[0], table[1]), lines, ((1,), (1,)))
            for y in range(0, 4, 2):
                begin = y * LANES // 2
                low_bins = waves[:half, begin : begin + LANES]
                high_bins = waves[half:, begin : begin + LANES]
                even = jnp.where(first_half, low_bins, pltpu.roll(high_bins, half, 1))
                odd = jnp.where(first_half, pltpu.roll(low_bins, half, 1), high_bins)
                begin = tile * y_local + base + y
                out_ref[pl.ds(begin, half, stride=stride), :] = even
                out_ref[pl.ds(begin + 1, half, stride=stride), :] = odd


def spectral_kernel(
    gx_count,
    pa_count,
    y_local,
    freq_ref,
    data_ref,
    forward_y_ref,
    forward_x_ref,
    inverse_x_ref,
    inverse_y_ref,
    out_ref,
    waves,
    blocks_ref,
    sems,
):
    grid_len = LANES
    size = 2 * grid_len
    tile_count = COMPS // 2
    forward_y = (forward_y_ref[0], forward_y_ref[1])
    forward_x = (forward_x_ref[0], forward_x_ref[1])
    inverse_x = (inverse_x_ref[0], inverse_x_ref[1])
    inverse_y = (inverse_y_ref[0], inverse_y_ref[1])
    x_local = grid_len // gx_count
    for tile in range(tile_count):
        fields = [
            data_ref[pl.ds(g * pa_count, pa_count), :, tile, :, :].reshape(size, LANES).T
            for g in range(gx_count)
        ]
        lines = product(split(jnp.concatenate(fields, axis=0)), forward_y)
        planes = []
        for slot in range(4):
            rows = [
                lines[g * LANES + slot * x_local :][:x_local] for g in range(gx_count)
            ]
            plane = jnp.concatenate(rows, axis=0)
            planes.append(jnp.concatenate([plane[:, :LANES], plane[:, LANES:]], axis=0))
        waves[tile] = product(forward_x, split(jnp.concatenate(planes, axis=1)))

    def signed(index):
        plain = jnp.where(index < grid_len // 2, index, index - grid_len)
        return jnp.where(index == grid_len // 2, 0, plain).astype(jnp.float32)

    step = 16
    freq_y = signed(lax.broadcasted_iota(jnp.int32, (step, LANES), 1))
    row_index = lax.broadcasted_iota(jnp.int32, (step, LANES), 0)

    def operate(chunk, carry):
        start = pl.multiple_of(chunk * step, step)
        freq_x = signed(row_index + start)
        for j in range(2):
            freq_z = freq_ref[j]
            square = freq_x * freq_x + freq_y * freq_y + freq_z * freq_z
            inverse = 1.0 / jnp.maximum(square, 1.0)
            scaled = inverse * inverse * green_coef
            for part in range(2):
                rows = pl.ds(part * grid_len + start, step)

                def at(comp):
                    return (comp // 2, rows, pl.ds((2 * j + comp % 2) * LANES, LANES))

                e_xx, e_yy, e_zz, e_yz, e_xz, e_xy = [waves[at(c)] for c in range(COMPS)]
                trace = (0.5 * lame_lambda) * (e_xx + e_yy + e_zz)
                n_x = (trace + e_xx) * freq_x + e_xy * freq_y + e_xz * freq_z
                n_y = e_xy * freq_x + (trace + e_yy) * freq_y + e_yz * freq_z
                n_z = e_xz * freq_x + e_yz * freq_y + (trace + e_zz) * freq_z
                along = (freq_x * n_x + freq_y * n_y + freq_z * n_z) * scaled
                u_x = n_x * inverse - freq_x * along
                u_y = n_y * inverse - freq_y * along
                u_z = n_z * inverse - freq_z * along
                waves[at(0)] = 2.0 * (freq_x * u_x)
                waves[at(1)] = 2.0 * (freq_y * u_y)
                waves[at(2)] = 2.0 * (freq_z * u_z)
                waves[at(3)] = freq_y * u_z + freq_z * u_y
                waves[at(4)] = freq_x * u_z + freq_z * u_x
                waves[at(5)] = freq_x * u_y + freq_y * u_x
        return carry

    lax.fori_loop(0, grid_len // step, operate, 0, unroll=True)

    stores = []
    for tile in range(tile_count):
        planes = product(inverse_x, split(waves[tile]))
        rows = []
        for g in range(gx_count):
            for slot in range(4):
                lanes = slice(slot * LANES, (slot + 1) * LANES)
                parts = [
                    planes[part * grid_len + g * x_local :][:x_local, lanes] for part in range(2)
                ]
                rows.append(jnp.concatenate(parts, axis=1))
        lines = product(split(jnp.concatenate(rows, axis=0)), inverse_y)
        for g in range(gx_count):
            blocks_ref[tile, pl.ds(g * size, size), :] = lines[g * LANES : (g + 1) * LANES].T
        done = blocks_ref.at[tile].reshape(gx_count * pa_count, 2, y_local, LANES)
        stores.append(pltpu.make_async_copy(done, out_ref.at[:, :, tile], sems.at[tile]))
        stores[-1].start()
    for store in stores:
        store.wait()


def inverse_z_kernel(
    x_local,
    y_local,
    cell_count,
    voxel_ref,
    waves_ref,
    plastic_ref,
    table_ref,
    stress_ref,
    own_ref,
    low_cells_ref,
    high_cells_ref,
):
    table = (table_ref[0], table_ref[1])
    half = LANES // 2
    per_comp = x_local * y_local
    stride = (COMPS // 2) * y_local
    first_half = lane_iota(half) < half
    for pair in range(y_local // 2):
        elastic = [[None] * COMPS for _ in range(2)]
        for tile in range(COMPS // 2):
            base = tile * y_local + 2 * pair
            even = waves_ref[pl.ds(base, half, stride=stride), :]
            odd = waves_ref[pl.ds(base + 1, half, stride=stride), :]
            low_bins = jnp.where(first_half, even, pltpu.roll(odd, half, 1))
            high_bins = jnp.where(first_half, pltpu.roll(even, half, 1), odd)
            turned = jnp.concatenate([low_bins, high_bins], axis=0).T
            lines = product(split(turned), table)
            for y in range(2):
                for c in range(2):
                    begin = (2 * y + c) * x_local
                    comp = 2 * tile + c
                    own = plastic_ref[
                        pl.ds(comp * per_comp + 2 * pair + y, x_local, stride=y_local), :
                    ]
                    elastic[y][comp] = lines[begin : begin + x_local] - own
        for y in range(2):
            trace = lame_lambda * (elastic[y][0] + elastic[y][1] + elastic[y][2])
            for comp in range(COMPS):
                value = 2.0 * shear_modulus * elastic[y][comp]
                if comp < 3:
                    value = value + trace
                stress_ref[
                    pl.ds(comp * per_comp + 2 * pair + y, x_local, stride=y_local), :
                ] = value

    cell_rows = per_comp // cell_count
    place = lax.broadcasted_iota(jnp.int32, (LANES, LANES), 0)
    row = lax.broadcasted_iota(jnp.int32, (cell_rows, LANES), 0)
    unused = jnp.zeros((8 - COMPS, LANES), jnp.float32)
    for cell in range(cell_count):
        voxel = voxel_ref[pl.ds(cell, 1), :]
        picked_row = lax.shift_right_logical(voxel, LANES.bit_length() - 1)
        picked_place = lax.bitwise_and(voxel, LANES - 1)
        choose = (place == picked_place).astype(jnp.bfloat16)
        keep = row == picked_row - cell * cell_rows
        blocks = [
            jnp.concatenate(
                split(stress_ref[pl.ds(comp * per_comp + cell * cell_rows, cell_rows), :]), axis=1
            )
            for comp in range(COMPS)
        ]
        picked = jnp.dot(
            jnp.concatenate(blocks, axis=0),
            jnp.concatenate([choose, choose], axis=0),
            preferred_element_type=jnp.float32,
        )
        found = [
            jnp.sum(
                jnp.where(keep, picked[comp * cell_rows : (comp + 1) * cell_rows], 0.0),
                axis=0,
                keepdims=True,
            )
            for comp in range(COMPS)
        ]
        found = jnp.concatenate(found + [unused], axis=0)
        own_ref[cell] = found
        if cell < 2:
            low_cells_ref[cell] = found
        if cell >= cell_count - 2:
            high_cells_ref[cell - cell_count + 2] = found


def pair_moments(position, fixed, scratch, pairs, add=()):
    columns, features, moments = scratch
    slots = position[0].shape[0]
    lines, burgers = fixed
    moved = [
        position[1] * lines[2] - position[2] * lines[1],
        position[2] * lines[0] - position[0] * lines[2],
        position[0] * lines[1] - position[1] * lines[0],
    ]
    for shift in range(3):
        offset = shift - 1.0
        shifted = [moved[0], moved[1] - offset * lines[2], moved[2] + offset * lines[1]]
        for b in range(3):
            for a in range(3):
                features[shift, pl.ds((3 * a + b) * slots, slots), :] = lines[a] * burgers[b]
                features[shift, pl.ds((9 + 3 * a + b) * slots, slots), :] = shifted[a] * burgers[b]
    for source in sorted({target + shift - 1 for target in pairs for shift in pairs[target]}):
        for a in range(3):
            row = position[a][source : source + 1]
            columns[source, a] = jnp.broadcast_to(row, (LANES, LANES)).T
    for target, shifts in pairs.items():
        weights = []
        sources = []
        own = [position[a][target : target + 1] for a in range(3)]
        for shift in shifts:
            source = target + shift - 1
            d_x = (own[0] - (shift - 1.0)) - columns[source, 0]
            d_y = own[1] - columns[source, 1]
            d_z = own[2] - columns[source, 2]
            inverse = lax.rsqrt(d_x * d_x + d_y * d_y + d_z * d_z + core_square)
            weights.append(inverse * inverse * inverse)
            sources.append(features[shift, pl.ds(source, FEATURES, stride=slots), :])
        total = product(
            split(jnp.concatenate(sources, axis=1)), split(jnp.concatenate(weights, axis=0))
        )
        rows = pl.ds(target * FEATURES, FEATURES)
        moments[rows, :] = moments[rows, :] + total if target in add else total


def every_pair(first, last):
    return {target: (0, 1, 2) for target in range(first, last)}


def pair_field(position, moments):
    slots = position[0].shape[0]

    def feature(index):
        return moments[pl.ds(index, slots, stride=FEATURES), :]

    moment = [[None] * 3 for _ in range(3)]
    for b in range(3):
        g = [feature(3 * a + b) for a in range(3)]
        moment[0][b] = position[1] * g[2] - position[2] * g[1] - feature(9 + b)
        moment[1][b] = position[2] * g[0] - position[0] * g[2] - feature(12 + b)
        moment[2][b] = position[0] * g[1] - position[1] * g[0] - feature(15 + b)
    pairs = ((0, 0), (1, 1), (2, 2), (1, 2), (0, 2), (0, 1))
    return [pair_factor * (moment[a][b] + moment[b][a]) for a, b in pairs]


def load_fixed(start_ref):
    values = [start_ref[a] for a in range(9)]
    return values[0:3], values[3:6], values[6:9]


def clear(features, moments):
    features[...] = jnp.zeros_like(features)
    moments[...] = jnp.zeros_like(moments)


def first_field_kernel(last, start_ref, out_ref, columns, features, moments):
    clear(features, moments)
    position, lines, burgers = load_fixed(start_ref)
    pair_moments(
        position, (lines, burgers), (columns, features, moments), every_pair(1, last)
    )
    for comp, value in enumerate(pair_field(position, moments)):
        out_ref[comp] = value


def moved_on(position, lines, burgers, sampled, field):
    sigma = [sampled[comp] + field[comp] for comp in range(COMPS)]
    traction = [
        sigma[full_index[a][0]] * burgers[0]
        + sigma[full_index[a][1]] * burgers[1]
        + sigma[full_index[a][2]] * burgers[2]
        for a in range(3)
    ]
    return [
        position[0] + step_size * (traction[1] * lines[2] - traction[2] * lines[1]),
        position[1] + step_size * (traction[2] * lines[0] - traction[0] * lines[2]),
        position[2] + step_size * (traction[0] * lines[1] - traction[1] * lines[0]),
    ]


def spread(sampled_ref, parts):
    sampled_ref[...] = jnp.zeros_like(sampled_ref)
    for begin, part in parts:
        sampled_ref[pl.ds(8 * begin, 8 * part.shape[0]), :] = part[...].reshape(-1, LANES)
    return [sampled_ref[pl.ds(comp, SLOTS, stride=8), :] for comp in range(COMPS)]


def own_moves_kernel(
    cell_count,
    start_ref,
    first_ref,
    own_ref,
    stress_ref,
    stress_out_ref,
    part_ref,
    columns,
    features,
    moments,
    sampled_ref,
    sem,
):
    store = pltpu.make_async_copy(stress_ref, stress_out_ref, sem)
    store.start()
    clear(features, moments)
    position, lines, burgers = load_fixed(start_ref)
    sampled = spread(sampled_ref, [(3, own_ref)])
    field = [first_ref[comp] for comp in range(COMPS)]
    position = moved_on(position, lines, burgers, sampled, field)
    first, last = 3, cell_count + 3
    pairs = {
        target: [s for s in range(3) if first <= target + s - 1 < last]
        for target in range(first, last)
    }
    pair_moments(position, (lines, burgers), (columns, features, moments), pairs)
    part_ref[...] = moments[...]
    store.wait()


def moves_kernel(
    cell_count,
    start_ref,
    first_ref,
    left_ref,
    own_ref,
    right_ref,
    part_ref,
    out_ref,
    columns,
    features,
    moments,
    sampled_ref,
):
    features[...] = jnp.zeros_like(features)
    moments[...] = part_ref[...]
    position, lines, burgers = load_fixed(start_ref)
    initial = position
    first, last = 3, cell_count + 3
    sampled = spread(sampled_ref, [(1, left_ref), (first, own_ref), (last, right_ref)])
    rest = {first - 1: (0, 1, 2), first: (0,), last - 1: (2,), last: (0, 1, 2)}
    for repeat in range(SUB):
        if repeat == 0:
            field = [first_ref[comp] for comp in range(COMPS)]
        else:
            pair_moments(
                position,
                (lines, burgers),
                (columns, features, moments),
                rest if repeat == 1 else every_pair(first, last),
                (first, last - 1) if repeat == 1 else (),
            )
            field = pair_field(position, moments)
        position = moved_on(position, lines, burgers, sampled, field)
    for a in range(3):
        out_ref[a] = (position[a] - initial[a])[first:last]


def kernel_call(kernel, outs, scratch=(), flops=0, places="", out_places="", limit=VMEM_LIMIT):
    spaces = {"s": pltpu.SMEM, "v": pltpu.VMEM, "h": pltpu.HBM}
    return pl.pallas_call(
        kernel,
        out_shape=outs,
        in_specs=[pl.BlockSpec(memory_space=spaces[p]) for p in places],
        out_specs=[pl.BlockSpec(memory_space=spaces[p]) for p in out_places],
        scratch_shapes=list(scratch),
        compiler_params=pltpu.CompilerParams(vmem_limit_bytes=limit),
        cost_estimate=pl.CostEstimate(flops=flops, bytes_accessed=1 << 20, transcendentals=0),
    )


def in_hbm(array):
    return pltpu.with_memory_space_constraint(array, pltpu.HBM)


def neighbours(low, high):
    count = lax.axis_size("gx")
    forward = [(i, (i + 1) % count) for i in range(count)]
    backward = [(target, source) for source, target in forward]
    return lax.ppermute(high, "gx", forward), lax.ppermute(low, "gx", backward)


def slab_body(plastic, offsets, lines, burgers, counts, voxels):
    f32 = jnp.float32
    comp_count, x_local, y_local, grid_len = plastic.shape
    gx_count = lax.axis_size("gx")
    pa_count = lax.axis_size("pa")
    devices = gx_count * pa_count
    cell_count, cap = voxels.shape[1:]
    tiles = comp_count // 2
    rows = devices * 2 * tiles * y_local
    blocks = (devices, rows // devices, LANES)
    parts = (devices, 2, tiles, y_local, LANES)
    forward_z, forward_y, forward_x, inverse_x, inverse_y, inverse_z = [
        jnp.asarray(t) for t in tables(grid_len, pa_count, y_local)
    ]
    axes = ("gx", "pa")
    own = lax.axis_index(axes)
    bins = (own + devices * jnp.arange(2, dtype=jnp.int32)).astype(f32)
    flat_plastic = plastic.reshape(-1, grid_len)
    tile_sems = pltpu.SemaphoreType.DMA((tiles,))

    bins, flat_plastic = lax.optimization_barrier((bins, flat_plastic))

    (waves,) = kernel_call(
        functools.partial(forward_z_kernel, x_local, y_local),
        [pltpu.VMEM((rows, LANES), f32)],
        [
            pltpu.VMEM(flat_plastic.shape, f32),
            pltpu.VMEM(forward_z.shape, jnp.bfloat16),
            pltpu.SemaphoreType.DMA,
            tile_sems,
        ],
        places="hh",
        out_places="v",
    )(in_hbm(flat_plastic), in_hbm(forward_z))
    waves = lax.all_to_all(waves.reshape(blocks), axes, 0, 0, tiled=True)
    (waves,) = kernel_call(
        functools.partial(spectral_kernel, gx_count, pa_count, y_local),
        [jax.ShapeDtypeStruct(parts, f32)],
        [
            pltpu.VMEM((tiles, 2 * grid_len, 4 * LANES), f32),
            pltpu.VMEM((tiles, rows // tiles, LANES), f32),
            tile_sems,
        ],
        places="svvvvv",
        out_places="h",
    )(bins, waves.reshape(parts), forward_y, forward_x, inverse_x, inverse_y)
    waves, offsets, lines, burgers, counts = lax.optimization_barrier(
        (waves, offsets, lines, burgers, counts)
    )
    waves = lax.all_to_all(waves.reshape(blocks), axes, 0, 0, tiled=True)

    live = (jnp.arange(cap, dtype=jnp.int32)[None, :] < counts[0][:, None]).astype(f32)
    start = jnp.concatenate([offsets[:, 0], lines[:, 0], burgers[:, 0] * live[None]], axis=0)
    below, above = neighbours(start[:, :3], start[:, cell_count - 3 :])
    padding = jnp.zeros((9, SLOTS - cell_count - 6, cap), f32)
    start = jnp.concatenate([below, start, above, padding], axis=1)
    pair_scratch = [
        pltpu.VMEM((SLOTS, 3, LANES, LANES), f32),
        pltpu.VMEM((3, FEATURES * SLOTS, LANES), f32),
        pltpu.VMEM((SLOTS * FEATURES, LANES), f32),
    ]
    (first,) = kernel_call(
        functools.partial(first_field_kernel, cell_count + 5),
        [jax.ShapeDtypeStruct((comp_count, SLOTS, cap), f32)],
        pair_scratch,
        places="v",
        out_places="v",
    )(start)

    waves, first = lax.optimization_barrier((waves, first))
    end = jax.ShapeDtypeStruct((2, 8, cap), f32)
    stress, own_cells, low_cells, high_cells = kernel_call(
        functools.partial(inverse_z_kernel, x_local, y_local, cell_count),
        [
            pltpu.VMEM(flat_plastic.shape, f32),
            jax.ShapeDtypeStruct((cell_count, 8, cap), f32),
            end,
            end,
        ],
        places="vvvv",
        out_places="vvvv",
    )(voxels[0], waves.reshape(rows, LANES), flat_plastic, inverse_z)
    left, right = neighbours(low_cells, high_cells)
    sampled = pltpu.VMEM((8 * SLOTS, LANES), f32)
    stress, part = kernel_call(
        functools.partial(own_moves_kernel, cell_count),
        [
            jax.ShapeDtypeStruct(stress.shape, f32),
            jax.ShapeDtypeStruct((SLOTS * FEATURES, cap), f32),
        ],
        pair_scratch + [sampled, pltpu.SemaphoreType.DMA],
        places="vvvv",
        out_places="hv",
    )(start, first, own_cells, stress)
    (moved,) = kernel_call(
        functools.partial(moves_kernel, cell_count),
        [jax.ShapeDtypeStruct((3, cell_count, cap), f32)],
        pair_scratch + [sampled],
        places="vvvvvv",
        out_places="v",
    )(start, first, left, own_cells, right, part)
    return (stress.reshape(plastic.shape), moved[:, None])


def fits(mesh, plastic, voxels):
    gx_count, pa_count = mesh.shape["gx"], mesh.shape["pa"]
    grid_len = plastic.shape[3]
    x_local, y_local = plastic.shape[1] // gx_count, plastic.shape[2] // pa_count
    cell_count = voxels.shape[1] // gx_count
    return (
        plastic.shape == (COMPS, LANES, LANES, LANES)
        and 4 * gx_count * pa_count == grid_len
        and 4 * x_local == LANES
        and y_local % 8 == 0
        and voxels.shape[2] == LANES
        and 3 <= cell_count <= SLOTS - 6
        and x_local % cell_count == 0
    )


def solution(mesh):
    placed = (
        P(None, "gx", "pa", None),
        P(None, "pa", "gx", None),
        P(None, "pa", "gx", None),
        P(None, "pa", "gx", None),
        P("pa", "gx"),
        P("pa", "gx", None),
    )

    def step(plastic, offsets, lines, burgers, counts, voxels):
        chosen = slab_body if fits(mesh, plastic, voxels) else body
        return jax.shard_map(
            chosen,
            mesh=mesh,
            in_specs=placed,
            out_specs=(P(None, "gx", "pa", None), P(None, "pa", "gx", None)),
            check_vma=False,
        )(plastic, offsets, lines, burgers, counts, voxels)

    return step
```

```python
import functools
import math

import jax
import jax.numpy as jnp
import ml_dtypes
import numpy as np
from jax import lax
from jax.experimental import pallas as pl
from jax.experimental.pallas import tpu as pltpu
from jax.sharding import PartitionSpec as P

SUB = 3


lame_lambda = 1.5
shear_modulus = 1.0
green_coef = 2.5 / 3.5
core_square = 0.09
pair_factor = 1.0 / (4.0 * math.pi)
step_size = 0.05
full_index = ((0, 5, 4), (5, 1, 3), (4, 3, 2))


def with_halo(block, sides, width):
    for axis, dim in sides:
        count = lax.axis_size(axis)
        forward = [(i, i + 1) for i in range(count - 1)]
        forward.append((count - 1, 0))
        backward = [(target, source) for source, target in forward]
        low = lax.ppermute(
            lax.slice_in_dim(block, block.shape[dim] - width, None, axis=dim), axis, forward
        )
        high = lax.ppermute(lax.slice_in_dim(block, 0, width, axis=dim), axis, backward)
        block = jnp.concatenate([low, block, high], axis=dim)
    return block


def stress_of(strain, freq_x, freq_y, freq_z):
    strain_xx, strain_yy, strain_zz = (strain[0], strain[1], strain[2])
    strain_yz, strain_xz, strain_xy = (strain[3], strain[4], strain[5])
    trace = strain_xx + strain_yy + strain_zz
    tau_xx = lame_lambda * trace + 2.0 * shear_modulus * strain_xx
    tau_yy = lame_lambda * trace + 2.0 * shear_modulus * strain_yy
    tau_zz = lame_lambda * trace + 2.0 * shear_modulus * strain_zz
    tau_yz = 2.0 * shear_modulus * strain_yz
    tau_xz = 2.0 * shear_modulus * strain_xz
    tau_xy = 2.0 * shear_modulus * strain_xy
    norm_x = tau_xx * freq_x + tau_xy * freq_y + tau_xz * freq_z
    norm_y = tau_xy * freq_x + tau_yy * freq_y + tau_yz * freq_z
    norm_z = tau_xz * freq_x + tau_yz * freq_y + tau_zz * freq_z
    square = freq_x * freq_x + freq_y * freq_y + freq_z * freq_z
    inverse = 1.0 / jnp.maximum(square, 1.0)
    along_k = (freq_x * norm_x + freq_y * norm_y + freq_z * norm_z) * inverse * inverse * green_coef

    def strain_term(first_q, second_q, first_n, second_n, plastic_part):
        total = (first_q * second_n + second_q * first_n) * inverse / (
            2.0 * shear_modulus
        ) - first_q * second_q * along_k
        return total - plastic_part

    el_xx = strain_term(freq_x, freq_x, norm_x, norm_x, strain_xx)
    el_yy = strain_term(freq_y, freq_y, norm_y, norm_y, strain_yy)
    el_zz = strain_term(freq_z, freq_z, norm_z, norm_z, strain_zz)
    el_yz = strain_term(freq_y, freq_z, norm_y, norm_z, strain_yz)
    el_xz = strain_term(freq_x, freq_z, norm_x, norm_z, strain_xz)
    el_xy = strain_term(freq_x, freq_y, norm_x, norm_y, strain_xy)
    el_trace = el_xx + el_yy + el_zz
    return jnp.stack(
        [
            lame_lambda * el_trace + 2.0 * shear_modulus * el_xx,
            lame_lambda * el_trace + 2.0 * shear_modulus * el_yy,
            lame_lambda * el_trace + 2.0 * shear_modulus * el_zz,
            2.0 * shear_modulus * el_yz,
            2.0 * shear_modulus * el_xz,
            2.0 * shear_modulus * el_xy,
        ]
    )


def advance(position, lines, burgers, sampled):
    cell_count = sampled.shape[1]
    unit_x = jnp.array([1.0, 0.0, 0.0], jnp.float32)[:, None, None]
    source = jnp.concatenate(
        [
            position[:, shifted : shifted + cell_count] + (shifted - 1.0) * unit_x
            for shifted in range(3)
        ],
        axis=2,
    )
    source_line = jnp.concatenate(
        [lines[:, shifted : shifted + cell_count] for shifted in range(3)], axis=2
    )
    source_burgers = jnp.concatenate(
        [burgers[:, shifted : shifted + cell_count] for shifted in range(3)], axis=2
    )
    target = position[:, 1 : cell_count + 1]
    own_line = lines[:, 1 : cell_count + 1]
    own_burgers = burgers[:, 1 : cell_count + 1]
    offset_vec = target[:, :, :, None] - source[:, :, None, :]
    radius = offset_vec[0] ** 2 + offset_vec[1] ** 2 + offset_vec[2] ** 2 + core_square
    weight = lax.rsqrt(radius) / radius
    line_b = source_line[:, :, None, :]
    cross = (
        jnp.stack(
            [
                offset_vec[1] * line_b[2] - offset_vec[2] * line_b[1],
                offset_vec[2] * line_b[0] - offset_vec[0] * line_b[2],
                offset_vec[0] * line_b[1] - offset_vec[1] * line_b[0],
            ]
        )
        * weight[None]
    )
    moment = jnp.einsum("acij,bcj->abci", cross, source_burgers, precision=lax.Precision.HIGHEST)
    pair_field = pair_factor * (moment + jnp.swapaxes(moment, 0, 1))
    traction = []
    for first in range(3):
        acc_row = jnp.zeros_like(target[0])
        for second in range(3):
            acc_row = (
                acc_row
                + (sampled[full_index[first][second]] + pair_field[first, second])
                * own_burgers[second]
            )
        traction.append(acc_row)
    force_x = traction[1] * own_line[2] - traction[2] * own_line[1]
    force_y = traction[2] * own_line[0] - traction[0] * own_line[2]
    force_z = traction[0] * own_line[1] - traction[1] * own_line[0]
    return target + step_size * jnp.stack([force_x, force_y, force_z])


def phases(row_index, col_index, grid_len):
    product = row_index[:, None] * col_index[None, :] % grid_len
    angle = product.astype(jnp.float32) * (2.0 * math.pi / grid_len)
    return (jnp.cos(angle), jnp.sin(angle))


def transform_last(field, matrix):
    shape = field.shape
    flat = field.reshape(-1, shape[-2] * shape[-1])
    result = jnp.dot(flat, matrix, precision=lax.Precision.HIGHEST)
    return result.reshape(shape[:-2] + (2, matrix.shape[1] // 2))


def body(plastic, offsets, lines, burgers, counts, voxels):
    grid_len = plastic.shape[3]
    pa_count = lax.axis_size("pa")
    grid_index = jnp.arange(grid_len, dtype=jnp.int32)
    bin_count = grid_len // 2 + pa_count
    bin_index = jnp.arange(bin_count, dtype=jnp.int32)
    kept_bins = (bin_index <= grid_len // 2).astype(jnp.float32)
    weights = jnp.where((bin_index == 0) | (bin_index == grid_len // 2), 1.0, 2.0) * kept_bins
    front_cos, front_sin = phases(grid_index, bin_index, grid_len)
    front_table = jnp.concatenate(
        [front_cos * kept_bins[None, :], -front_sin * kept_bins[None, :]], axis=1
    )
    final_cos, final_sin = phases(bin_index, grid_index, grid_len)
    final_table = (
        jnp.concatenate([final_cos * weights[:, None], -final_sin * weights[:, None]], axis=0)
        / grid_len
    )
    turn_cos, turn_sin = phases(grid_index, grid_index, grid_len)
    ahead_table = jnp.block([[turn_cos, -turn_sin], [turn_sin, turn_cos]])
    return_table = jnp.block([[turn_cos, turn_sin], [-turn_sin, turn_cos]]) / grid_len
    comp_count, x_local, y_local = (plastic.shape[0], plastic.shape[1], plastic.shape[2])
    field = jnp.dot(plastic.reshape(-1, grid_len), front_table, precision=lax.Precision.HIGHEST)
    field = field.reshape(comp_count, x_local, y_local, 2, bin_count)
    field = lax.all_to_all(field, "pa", split_axis=4, concat_axis=2, tiled=True)
    field = jnp.transpose(field, (0, 1, 4, 3, 2))
    field = transform_last(field, ahead_table)
    field = lax.all_to_all(field, "gx", split_axis=4, concat_axis=1, tiled=True)
    field = jnp.transpose(field, (0, 4, 2, 3, 1))
    field = transform_last(field, ahead_table)
    y_count = field.shape[1]
    z_count = field.shape[2]
    signed = jnp.where(
        grid_index < grid_len // 2,
        grid_index,
        jnp.where(grid_index == grid_len // 2, 0, grid_index - grid_len),
    ).astype(jnp.float32)
    freq_x = signed[None, None, :]
    freq_y = lax.dynamic_slice_in_dim(signed, lax.axis_index("gx") * y_count, y_count)[
        :, None, None
    ]
    freq_z = lax.dynamic_slice_in_dim(signed, lax.axis_index("pa") * z_count, z_count)[
        None, :, None
    ]
    real_part = stress_of(field[:, :, :, 0], freq_x, freq_y, freq_z)
    imag_part = stress_of(field[:, :, :, 1], freq_x, freq_y, freq_z)
    field = jnp.stack([real_part, imag_part], axis=3)
    field = transform_last(field, return_table)
    field = lax.all_to_all(field, "gx", split_axis=4, concat_axis=1, tiled=True)
    field = jnp.transpose(field, (0, 4, 2, 3, 1))
    field = transform_last(field, return_table)
    field = lax.all_to_all(field, "pa", split_axis=4, concat_axis=2, tiled=True)
    field = jnp.transpose(field, (0, 1, 4, 3, 2))
    flat = field.reshape(-1, 2 * bin_count)
    stress = jnp.dot(flat, final_table, precision=lax.Precision.HIGHEST).reshape(
        comp_count, x_local, y_local, grid_len
    )
    cell_count = offsets.shape[2]
    width_cap = offsets.shape[3]
    flat_stress = stress.reshape(6, -1)
    sampled = jnp.take(flat_stress, voxels.reshape(-1), axis=1).reshape(6, cell_count, width_cap)
    live_mask = (jnp.arange(width_cap, dtype=jnp.int32)[None, :] < counts[0][:, None]).astype(
        jnp.float32
    )
    initial = offsets[:, 0]
    line_dirs = lines[:, 0]
    masked = burgers[:, 0] * live_mask[None]
    fixed_rim = with_halo(jnp.concatenate([line_dirs, masked], axis=0), (("gx", 1),), 1)
    position = initial
    for repeat in range(SUB):
        widened = with_halo(position, (("gx", 1),), 1)
        position = advance(widened, fixed_rim[0:3], fixed_rim[3:6], sampled)
    moved = position - initial
    return (stress, moved[:, None])


LANES = 128
COMPS = 6
FEATURES = 24
SLOTS = 16
VMEM_LIMIT = 48 * 1024 * 1024
VMEM_WHOLE = 63 * 1024 * 1024


def split(value):
    high = value.astype(jnp.bfloat16)
    low = (value - high.astype(jnp.float32)).astype(jnp.bfloat16)
    return high, low


def split_table(table):
    table = np.asarray(table, np.float32)
    high = table.astype(ml_dtypes.bfloat16)
    low = (table - high.astype(np.float32)).astype(ml_dtypes.bfloat16)
    return np.stack([high, low])


def product(left, right, dims=((1,), (0,))):
    left_high, left_low = left
    right_high, right_low = right
    left_all = jnp.concatenate([left_high, left_high, left_low], axis=dims[0][0])
    right_all = jnp.concatenate([right_high, right_low, right_high], axis=dims[1][0])
    return lax.dot_general(
        left_all, right_all, (dims, ((), ())), preferred_element_type=jnp.float32
    )


def tables(grid_len, pa_count, y_local):
    index = np.arange(grid_len)
    bins = np.arange(grid_len // 2)
    angle = 2.0 * np.pi * (np.outer(bins, index) % grid_len) / grid_len
    nyquist = 1.0 - 2.0 * (index % 2)
    forward_z = np.stack([np.cos(angle), -np.sin(angle)], axis=1)
    forward_z[0, 1] = nyquist
    inverse_z = 2.0 * forward_z / grid_len
    inverse_z[0] = forward_z[0] / grid_len
    forward_z = forward_z.reshape(grid_len, grid_len)
    inverse_z = inverse_z.reshape(grid_len, grid_len)
    turn = 2.0 * np.pi * (np.outer(index, index) % grid_len) / grid_len
    cos, sin = np.cos(turn), np.sin(turn)
    ahead = np.array([[cos, sin], [-sin, cos]]).transpose(0, 2, 1, 3)
    back = np.array([[cos, -sin], [sin, cos]]).transpose(0, 2, 1, 3) / grid_len
    size = 2 * grid_len
    forward_y = ahead.reshape(2, grid_len, 2, pa_count, y_local).transpose(3, 2, 4, 0, 1)
    forward_y = forward_y.reshape(size, size)
    inverse_y = back.reshape(2, pa_count, y_local, 2, grid_len).transpose(3, 4, 1, 0, 2)
    inverse_y = inverse_y.reshape(size, size)
    forward_x = ahead.reshape(size, size)
    inverse_x = back.reshape(size, size)
    return [split_table(t) for t in (forward_z, forward_y, forward_x, inverse_x, inverse_y, inverse_z)]


def lane_iota(rows):
    return lax.broadcasted_iota(jnp.int32, (rows, LANES), 1)


def forward_z_kernel(
    x_local,
    y_local,
    plane_ref,
    table_ref,
    out_ref,
    planes,
    table,
    table_sem,
    in_sems,
):
    half = LANES // 2
    tiles = COMPS // 2
    per_comp = x_local * y_local
    first_half = lane_iota(half) < half
    fetch_table = pltpu.make_async_copy(table_ref, table, table_sem)
    fetch_table.start()
    fetches = []
    for tile in range(tiles):
        span = pl.ds(2 * tile * per_comp, 2 * per_comp)
        fetches.append(
            pltpu.make_async_copy(plane_ref.at[span], planes.at[span], in_sems.at[tile])
        )
        fetches[-1].start()
    fetch_table.wait()
    stride = tiles * y_local
    for tile in range(tiles):
        fetches[tile].wait()
        for base in range(0, y_local, 4):
            rows = [
                planes[pl.ds((2 * tile + c) * per_comp + base + y, x_local, stride=y_local), :]
                for y in range(4)
                for c in range(2)
            ]
            lines = split(jnp.concatenate(rows, axis=0))
            waves = product((table[0], table[1]), lines, ((1,), (1,)))
            for y in range(0, 4, 2):
                begin = y * LANES // 2
                low_bins = waves[:half, begin : begin + LANES]
                high_bins = waves[half:, begin : begin + LANES]
                even = jnp.where(first_half, low_bins, pltpu.roll(high_bins, half, 1))
                odd = jnp.where(first_half, pltpu.roll(low_bins, half, 1), high_bins)
                begin = tile * y_local + base + y
                out_ref[pl.ds(begin, half, stride=stride), :] = even
                out_ref[pl.ds(begin + 1, half, stride=stride), :] = odd


def spectral_kernel(
    gx_count,
    pa_count,
    y_local,
    freq_ref,
    data_ref,
    forward_y_ref,
    forward_x_ref,
    inverse_x_ref,
    inverse_y_ref,
    out_ref,
    waves,
    blocks_ref,
    sems,
):
    grid_len = LANES
    size = 2 * grid_len
    tile_count = COMPS // 2
    forward_y = (forward_y_ref[0], forward_y_ref[1])
    forward_x = (forward_x_ref[0], forward_x_ref[1])
    inverse_x = (inverse_x_ref[0], inverse_x_ref[1])
    inverse_y = (inverse_y_ref[0], inverse_y_ref[1])
    x_local = grid_len // gx_count
    for tile in range(tile_count):
        fields = [
            data_ref[:, g, :, :, tile].reshape(size, LANES).T
            for g in range(gx_count)
        ]
        lines = product(split(jnp.concatenate(fields, axis=0)), forward_y)
        planes = []
        for slot in range(4):
            rows = [
                lines[g * LANES + slot * x_local :][:x_local] for g in range(gx_count)
            ]
            plane = jnp.concatenate(rows, axis=0)
            planes.append(jnp.concatenate([plane[:, :LANES], plane[:, LANES:]], axis=0))
        waves[tile] = product(forward_x, split(jnp.concatenate(planes, axis=1)))

    def signed(index):
        plain = jnp.where(index < grid_len // 2, index, index - grid_len)
        return jnp.where(index == grid_len // 2, 0, plain).astype(jnp.float32)

    step = 16
    freq_y = signed(lax.broadcasted_iota(jnp.int32, (step, LANES), 1))
    row_index = lax.broadcasted_iota(jnp.int32, (step, LANES), 0)

    def operate(chunk, carry):
        start = pl.multiple_of(chunk * step, step)
        freq_x = signed(row_index + start)
        for j in range(2):
            freq_z = freq_ref[j]
            square = freq_x * freq_x + freq_y * freq_y + freq_z * freq_z
            inverse = 1.0 / jnp.maximum(square, 1.0)
            scaled = inverse * inverse * green_coef
            for part in range(2):
                rows = pl.ds(part * grid_len + start, step)

                def at(comp):
                    return (comp // 2, rows, pl.ds((2 * j + comp % 2) * LANES, LANES))

                e_xx, e_yy, e_zz, e_yz, e_xz, e_xy = [waves[at(c)] for c in range(COMPS)]
                trace = (0.5 * lame_lambda) * (e_xx + e_yy + e_zz)
                n_x = (trace + e_xx) * freq_x + e_xy * freq_y + e_xz * freq_z
                n_y = e_xy * freq_x + (trace + e_yy) * freq_y + e_yz * freq_z
                n_z = e_xz * freq_x + e_yz * freq_y + (trace + e_zz) * freq_z
                along = (freq_x * n_x + freq_y * n_y + freq_z * n_z) * scaled
                u_x = n_x * inverse - freq_x * along
                u_y = n_y * inverse - freq_y * along
                u_z = n_z * inverse - freq_z * along
                waves[at(0)] = 2.0 * (freq_x * u_x)
                waves[at(1)] = 2.0 * (freq_y * u_y)
                waves[at(2)] = 2.0 * (freq_z * u_z)
                waves[at(3)] = freq_y * u_z + freq_z * u_y
                waves[at(4)] = freq_x * u_z + freq_z * u_x
                waves[at(5)] = freq_x * u_y + freq_y * u_x
        return carry

    lax.fori_loop(0, grid_len // step, operate, 0, unroll=True)

    stores = []
    for tile in range(tile_count):
        planes = product(inverse_x, split(waves[tile]))
        rows = []
        for g in range(gx_count):
            for slot in range(4):
                lanes = slice(slot * LANES, (slot + 1) * LANES)
                parts = [
                    planes[part * grid_len + g * x_local :][:x_local, lanes] for part in range(2)
                ]
                rows.append(jnp.concatenate(parts, axis=1))
        lines = product(split(jnp.concatenate(rows, axis=0)), inverse_y)
        for g in range(gx_count):
            field = lines[g * LANES : (g + 1) * LANES].T
            blocks_ref[tile, :, g] = field.reshape(pa_count // 2, 2, 2, y_local, LANES)
        place = out_ref.at[:, :, :, :, tile]
        stores.append(pltpu.make_async_copy(blocks_ref.at[tile], place, sems.at[tile]))
        stores[-1].start()
    for store in stores:
        store.wait()


def inverse_z_kernel(
    x_local,
    y_local,
    cell_count,
    voxel_ref,
    waves_ref,
    plastic_ref,
    table_ref,
    stress_ref,
    own_ref,
    low_cells_ref,
    high_cells_ref,
):
    table = (table_ref[0], table_ref[1])
    half = LANES // 2
    per_comp = x_local * y_local
    stride = (COMPS // 2) * y_local
    first_half = lane_iota(half) < half
    for pair in range(y_local // 2):
        elastic = [[None] * COMPS for _ in range(2)]
        for tile in range(COMPS // 2):
            base = tile * y_local + 2 * pair
            even = waves_ref[pl.ds(base, half, stride=stride), :]
            odd = waves_ref[pl.ds(base + 1, half, stride=stride), :]
            low_bins = jnp.where(first_half, even, pltpu.roll(odd, half, 1))
            high_bins = jnp.where(first_half, pltpu.roll(even, half, 1), odd)
            turned = jnp.concatenate([low_bins, high_bins], axis=0).T
            lines = product(split(turned), table)
            for y in range(2):
                for c in range(2):
                    begin = (2 * y + c) * x_local
                    comp = 2 * tile + c
                    own = plastic_ref[
                        pl.ds(comp * per_comp + 2 * pair + y, x_local, stride=y_local), :
                    ]
                    elastic[y][comp] = lines[begin : begin + x_local] - own
        for y in range(2):
            trace = lame_lambda * (elastic[y][0] + elastic[y][1] + elastic[y][2])
            for comp in range(COMPS):
                value = 2.0 * shear_modulus * elastic[y][comp]
                if comp < 3:
                    value = value + trace
                stress_ref[
                    pl.ds(comp * per_comp + 2 * pair + y, x_local, stride=y_local), :
                ] = value

    cell_rows = per_comp // cell_count
    place = lax.broadcasted_iota(jnp.int32, (LANES, LANES), 0)
    row = lax.broadcasted_iota(jnp.int32, (cell_rows, LANES), 0)
    unused = jnp.zeros((8 - COMPS, LANES), jnp.float32)
    for cell in range(cell_count):
        voxel = voxel_ref[pl.ds(cell, 1), :]
        picked_row = lax.shift_right_logical(voxel, LANES.bit_length() - 1)
        picked_place = lax.bitwise_and(voxel, LANES - 1)
        choose = (place == picked_place).astype(jnp.bfloat16)
        keep = row == picked_row - cell * cell_rows
        blocks = [
            jnp.concatenate(
                split(stress_ref[pl.ds(comp * per_comp + cell * cell_rows, cell_rows), :]), axis=1
            )
            for comp in range(COMPS)
        ]
        picked = jnp.dot(
            jnp.concatenate(blocks, axis=0),
            jnp.concatenate([choose, choose], axis=0),
            preferred_element_type=jnp.float32,
        )
        found = [
            jnp.sum(
                jnp.where(keep, picked[comp * cell_rows : (comp + 1) * cell_rows], 0.0),
                axis=0,
                keepdims=True,
            )
            for comp in range(COMPS)
        ]
        found = jnp.concatenate(found + [unused], axis=0)
        own_ref[cell] = found
        if cell < 2:
            low_cells_ref[cell] = found
        if cell >= cell_count - 2:
            high_cells_ref[cell - cell_count + 2] = found


def pair_moments(position, fixed, scratch, pairs, add=()):
    columns, features, moments = scratch
    slots = position[0].shape[0]
    lines, burgers = fixed
    moved = [
        position[1] * lines[2] - position[2] * lines[1],
        position[2] * lines[0] - position[0] * lines[2],
        position[0] * lines[1] - position[1] * lines[0],
    ]
    for shift in range(3):
        offset = shift - 1.0
        shifted = [moved[0], moved[1] - offset * lines[2], moved[2] + offset * lines[1]]
        for b in range(3):
            for a in range(3):
                features[shift, pl.ds((3 * a + b) * slots, slots), :] = lines[a] * burgers[b]
                features[shift, pl.ds((9 + 3 * a + b) * slots, slots), :] = shifted[a] * burgers[b]
    for source in sorted({target + shift - 1 for target in pairs for shift in pairs[target]}):
        for a in range(3):
            row = position[a][source : source + 1]
            columns[source, a] = jnp.broadcast_to(row, (LANES, LANES)).T
    for target, shifts in pairs.items():
        weights = []
        sources = []
        own = [position[a][target : target + 1] for a in range(3)]
        for shift in shifts:
            source = target + shift - 1
            d_x = (own[0] - (shift - 1.0)) - columns[source, 0]
            d_y = own[1] - columns[source, 1]
            d_z = own[2] - columns[source, 2]
            inverse = lax.rsqrt(d_x * d_x + d_y * d_y + d_z * d_z + core_square)
            weights.append(inverse * inverse * inverse)
            sources.append(features[shift, pl.ds(source, FEATURES, stride=slots), :])
        source = jnp.concatenate(sources, axis=1)
        high, rest = split(source)
        low = (source - high.astype(jnp.float32) - rest.astype(jnp.float32)).astype(jnp.bfloat16)
        parts = jnp.concatenate([high, rest, low], axis=0)
        total = jnp.dot(
            jnp.concatenate([parts, parts], axis=1),
            jnp.concatenate(split(jnp.concatenate(weights, axis=0)), axis=0),
            preferred_element_type=jnp.float32,
        )
        total = total[:FEATURES] + (total[FEATURES : 2 * FEATURES] + total[2 * FEATURES :])
        rows = pl.ds(target * FEATURES, FEATURES)
        moments[rows, :] = moments[rows, :] + total if target in add else total


def every_pair(first, last):
    return {target: (0, 1, 2) for target in range(first, last)}


def pair_field(position, moments):
    slots = position[0].shape[0]

    def feature(index):
        return moments[pl.ds(index, slots, stride=FEATURES), :]

    moment = [[None] * 3 for _ in range(3)]
    for b in range(3):
        g = [feature(3 * a + b) for a in range(3)]
        moment[0][b] = position[1] * g[2] - position[2] * g[1] - feature(9 + b)
        moment[1][b] = position[2] * g[0] - position[0] * g[2] - feature(12 + b)
        moment[2][b] = position[0] * g[1] - position[1] * g[0] - feature(15 + b)
    pairs = ((0, 0), (1, 1), (2, 2), (1, 2), (0, 2), (0, 1))
    return [pair_factor * (moment[a][b] + moment[b][a]) for a, b in pairs]


def load_fixed(start_ref):
    values = [start_ref[a] for a in range(9)]
    return values[0:3], values[3:6], values[6:9]


def clear(features, moments):
    features[...] = jnp.zeros_like(features)
    moments[...] = jnp.zeros_like(moments)


def first_field_kernel(last, start_ref, out_ref, columns, features, moments):
    clear(features, moments)
    position, lines, burgers = load_fixed(start_ref)
    pair_moments(
        position, (lines, burgers), (columns, features, moments), every_pair(1, last)
    )
    for comp, value in enumerate(pair_field(position, moments)):
        out_ref[comp] = value


def moved_on(position, lines, burgers, sampled, field):
    sigma = [sampled[comp] + field[comp] for comp in range(COMPS)]
    traction = [
        sigma[full_index[a][0]] * burgers[0]
        + sigma[full_index[a][1]] * burgers[1]
        + sigma[full_index[a][2]] * burgers[2]
        for a in range(3)
    ]
    return [
        position[0] + step_size * (traction[1] * lines[2] - traction[2] * lines[1]),
        position[1] + step_size * (traction[2] * lines[0] - traction[0] * lines[2]),
        position[2] + step_size * (traction[0] * lines[1] - traction[1] * lines[0]),
    ]


def spread(sampled_ref, parts):
    sampled_ref[...] = jnp.zeros_like(sampled_ref)
    for begin, part in parts:
        sampled_ref[pl.ds(8 * begin, 8 * part.shape[0]), :] = part[...].reshape(-1, LANES)
    return [sampled_ref[pl.ds(comp, SLOTS, stride=8), :] for comp in range(COMPS)]


def own_moves_kernel(
    cell_count,
    start_ref,
    first_ref,
    own_ref,
    stress_ref,
    stress_out_ref,
    part_ref,
    columns,
    features,
    moments,
    sampled_ref,
    sem,
):
    store = pltpu.make_async_copy(stress_ref, stress_out_ref, sem)
    store.start()
    clear(features, moments)
    position, lines, burgers = load_fixed(start_ref)
    sampled = spread(sampled_ref, [(3, own_ref)])
    field = [first_ref[comp] for comp in range(COMPS)]
    position = moved_on(position, lines, burgers, sampled, field)
    first, last = 3, cell_count + 3
    pairs = {
        target: [s for s in range(3) if first <= target + s - 1 < last]
        for target in range(first, last)
    }
    pair_moments(position, (lines, burgers), (columns, features, moments), pairs)
    part_ref[...] = moments[...]
    store.wait()


def moves_kernel(
    cell_count,
    start_ref,
    first_ref,
    left_ref,
    own_ref,
    right_ref,
    part_ref,
    out_ref,
    columns,
    features,
    moments,
    sampled_ref,
):
    features[...] = jnp.zeros_like(features)
    moments[...] = part_ref[...]
    position, lines, burgers = load_fixed(start_ref)
    initial = position
    first, last = 3, cell_count + 3
    sampled = spread(sampled_ref, [(1, left_ref), (first, own_ref), (last, right_ref)])
    rest = {first - 1: (0, 1, 2), first: (0,), last - 1: (2,), last: (0, 1, 2)}
    for repeat in range(SUB):
        if repeat == 0:
            field = [first_ref[comp] for comp in range(COMPS)]
        else:
            pair_moments(
                position,
                (lines, burgers),
                (columns, features, moments),
                rest if repeat == 1 else every_pair(first, last),
                (first, last - 1) if repeat == 1 else (),
            )
            field = pair_field(position, moments)
        position = moved_on(position, lines, burgers, sampled, field)
    for a in range(3):
        out_ref[a] = (position[a] - initial[a])[first:last]


def kernel_call(kernel, outs, scratch=(), flops=0, places="", out_places="", limit=VMEM_LIMIT):
    spaces = {"s": pltpu.SMEM, "v": pltpu.VMEM, "h": pltpu.HBM}
    return pl.pallas_call(
        kernel,
        out_shape=outs,
        in_specs=[pl.BlockSpec(memory_space=spaces[p]) for p in places],
        out_specs=[pl.BlockSpec(memory_space=spaces[p]) for p in out_places],
        scratch_shapes=list(scratch),
        compiler_params=pltpu.CompilerParams(vmem_limit_bytes=limit),
        cost_estimate=pl.CostEstimate(flops=flops, bytes_accessed=1 << 20, transcendentals=0),
    )


def in_hbm(array):
    return pltpu.with_memory_space_constraint(array, pltpu.HBM)


def neighbours(low, high):
    count = lax.axis_size("gx")
    forward = [(i, (i + 1) % count) for i in range(count)]
    backward = [(target, source) for source, target in forward]
    return lax.ppermute(high, "gx", forward), lax.ppermute(low, "gx", backward)


def slab_body(plastic, offsets, lines, burgers, counts, voxels):
    f32 = jnp.float32
    comp_count, x_local, y_local, grid_len = plastic.shape
    gx_count = lax.axis_size("gx")
    pa_count = lax.axis_size("pa")
    devices = gx_count * pa_count
    cell_count, cap = voxels.shape[1:]
    tiles = comp_count // 2
    rows = devices * 2 * tiles * y_local
    blocks = (devices, rows // devices, LANES)
    parts = (pa_count // 2, gx_count, 2, 2, tiles, y_local, LANES)
    forward_z, forward_y, forward_x, inverse_x, inverse_y, inverse_z = [
        jnp.asarray(t) for t in tables(grid_len, pa_count, y_local)
    ]
    order = [
        [
            g * pa_count + 2 * z + core
            for z in range(pa_count // 2)
            for g in range(gx_count)
            for core in range(2)
        ]
    ]
    exchange = functools.partial(
        lax.all_to_all,
        axis_name=("gx", "pa"),
        split_axis=0,
        concat_axis=0,
        axis_index_groups=order,
        tiled=True,
    )
    pa_index = lax.axis_index("pa")
    own = (pa_index // 2 * gx_count + lax.axis_index("gx")) * 2 + pa_index % 2
    bins = (own + devices * jnp.arange(2, dtype=jnp.int32)).astype(f32)
    flat_plastic = plastic.reshape(-1, grid_len)
    tile_sems = pltpu.SemaphoreType.DMA((tiles,))

    bins, flat_plastic = lax.optimization_barrier((bins, flat_plastic))

    (waves,) = kernel_call(
        functools.partial(forward_z_kernel, x_local, y_local),
        [pltpu.VMEM((rows, LANES), f32)],
        [
            pltpu.VMEM(flat_plastic.shape, f32),
            pltpu.VMEM(forward_z.shape, jnp.bfloat16),
            pltpu.SemaphoreType.DMA,
            tile_sems,
        ],
        places="hh",
        out_places="v",
    )(in_hbm(flat_plastic), in_hbm(forward_z))
    waves = exchange(waves.reshape(blocks))
    (waves,) = kernel_call(
        functools.partial(spectral_kernel, gx_count, pa_count, y_local),
        [jax.ShapeDtypeStruct(parts, f32)],
        [
            pltpu.VMEM((tiles, 2 * grid_len, 4 * LANES), f32),
            pltpu.VMEM((tiles, pa_count // 2, gx_count, 2, 2, y_local, LANES), f32),
            tile_sems,
        ],
        places="svvvvv",
        out_places="h",
    )(bins, waves.reshape(parts), forward_y, forward_x, inverse_x, inverse_y)
    waves, offsets, lines, burgers, counts = lax.optimization_barrier(
        (waves, offsets, lines, burgers, counts)
    )
    waves = exchange(waves.reshape(blocks))

    live = (jnp.arange(cap, dtype=jnp.int32)[None, :] < counts[0][:, None]).astype(f32)
    start = jnp.concatenate([offsets[:, 0], lines[:, 0], burgers[:, 0] * live[None]], axis=0)
    below, above = neighbours(start[:, :3], start[:, cell_count - 3 :])
    padding = jnp.zeros((9, SLOTS - cell_count - 6, cap), f32)
    start = jnp.concatenate([below, start, above, padding], axis=1)
    pair_scratch = [
        pltpu.VMEM((SLOTS, 3, LANES, LANES), f32),
        pltpu.VMEM((3, FEATURES * SLOTS, LANES), f32),
        pltpu.VMEM((SLOTS * FEATURES, LANES), f32),
    ]
    (first,) = kernel_call(
        functools.partial(first_field_kernel, cell_count + 5),
        [jax.ShapeDtypeStruct((comp_count, SLOTS, cap), f32)],
        pair_scratch,
        places="v",
        out_places="v",
    )(start)

    waves, first = lax.optimization_barrier((waves, first))
    end = jax.ShapeDtypeStruct((2, 8, cap), f32)
    stress, own_cells, low_cells, high_cells = kernel_call(
        functools.partial(inverse_z_kernel, x_local, y_local, cell_count),
        [
            pltpu.VMEM(flat_plastic.shape, f32),
            jax.ShapeDtypeStruct((cell_count, 8, cap), f32),
            end,
            end,
        ],
        places="vvvv",
        out_places="vvvv",
    )(voxels[0], waves.reshape(rows, LANES), flat_plastic, inverse_z)
    left, right = neighbours(low_cells, high_cells)
    sampled = pltpu.VMEM((8 * SLOTS, LANES), f32)
    stress, part = kernel_call(
        functools.partial(own_moves_kernel, cell_count),
        [
            jax.ShapeDtypeStruct(stress.shape, f32),
            jax.ShapeDtypeStruct((SLOTS * FEATURES, cap), f32),
        ],
        pair_scratch + [sampled, pltpu.SemaphoreType.DMA],
        places="vvvv",
        out_places="hv",
    )(start, first, own_cells, stress)
    (moved,) = kernel_call(
        functools.partial(moves_kernel, cell_count),
        [jax.ShapeDtypeStruct((3, cell_count, cap), f32)],
        pair_scratch + [sampled],
        places="vvvvvv",
        out_places="v",
    )(start, first, left, own_cells, right, part)
    return (stress.reshape(plastic.shape), moved[:, None])


def fits(mesh, plastic, voxels):
    gx_count, pa_count = mesh.shape["gx"], mesh.shape["pa"]
    grid_len = plastic.shape[3]
    x_local, y_local = plastic.shape[1] // gx_count, plastic.shape[2] // pa_count
    cell_count = voxels.shape[1] // gx_count
    return (
        plastic.shape == (COMPS, LANES, LANES, LANES)
        and 4 * gx_count * pa_count == grid_len
        and 4 * x_local == LANES
        and pa_count % 2 == 0
        and y_local % 8 == 0
        and voxels.shape[2] == LANES
        and 3 <= cell_count <= SLOTS - 6
        and x_local % cell_count == 0
    )


def solution(mesh):
    placed = (
        P(None, "gx", "pa", None),
        P(None, "pa", "gx", None),
        P(None, "pa", "gx", None),
        P(None, "pa", "gx", None),
        P("pa", "gx"),
        P("pa", "gx", None),
    )

    def step(plastic, offsets, lines, burgers, counts, voxels):
        chosen = slab_body if fits(mesh, plastic, voxels) else body
        return jax.shard_map(
            chosen,
            mesh=mesh,
            in_specs=placed,
            out_specs=(P(None, "gx", "pa", None), P(None, "pa", "gx", None)),
            check_vma=False,
        )(plastic, offsets, lines, burgers, counts, voxels)

    return step
```

```python
import functools
import math

import jax
import jax.numpy as jnp
import ml_dtypes
import numpy as np
from jax import lax
from jax.experimental import pallas as pl
from jax.experimental.pallas import tpu as pltpu
from jax.sharding import PartitionSpec as P

SUB = 3


lame_lambda = 1.5
shear_modulus = 1.0
green_coef = 2.5 / 3.5
core_square = 0.09
pair_factor = 1.0 / (4.0 * math.pi)
step_size = 0.05
full_index = ((0, 5, 4), (5, 1, 3), (4, 3, 2))


def with_halo(block, sides, width):
    for axis, dim in sides:
        count = lax.axis_size(axis)
        forward = [(i, i + 1) for i in range(count - 1)]
        forward.append((count - 1, 0))
        backward = [(target, source) for source, target in forward]
        low = lax.ppermute(
            lax.slice_in_dim(block, block.shape[dim] - width, None, axis=dim), axis, forward
        )
        high = lax.ppermute(lax.slice_in_dim(block, 0, width, axis=dim), axis, backward)
        block = jnp.concatenate([low, block, high], axis=dim)
    return block


def stress_of(strain, freq_x, freq_y, freq_z):
    strain_xx, strain_yy, strain_zz = (strain[0], strain[1], strain[2])
    strain_yz, strain_xz, strain_xy = (strain[3], strain[4], strain[5])
    trace = strain_xx + strain_yy + strain_zz
    tau_xx = lame_lambda * trace + 2.0 * shear_modulus * strain_xx
    tau_yy = lame_lambda * trace + 2.0 * shear_modulus * strain_yy
    tau_zz = lame_lambda * trace + 2.0 * shear_modulus * strain_zz
    tau_yz = 2.0 * shear_modulus * strain_yz
    tau_xz = 2.0 * shear_modulus * strain_xz
    tau_xy = 2.0 * shear_modulus * strain_xy
    norm_x = tau_xx * freq_x + tau_xy * freq_y + tau_xz * freq_z
    norm_y = tau_xy * freq_x + tau_yy * freq_y + tau_yz * freq_z
    norm_z = tau_xz * freq_x + tau_yz * freq_y + tau_zz * freq_z
    square = freq_x * freq_x + freq_y * freq_y + freq_z * freq_z
    inverse = 1.0 / jnp.maximum(square, 1.0)
    along_k = (freq_x * norm_x + freq_y * norm_y + freq_z * norm_z) * inverse * inverse * green_coef

    def strain_term(first_q, second_q, first_n, second_n, plastic_part):
        total = (first_q * second_n + second_q * first_n) * inverse / (
            2.0 * shear_modulus
        ) - first_q * second_q * along_k
        return total - plastic_part

    el_xx = strain_term(freq_x, freq_x, norm_x, norm_x, strain_xx)
    el_yy = strain_term(freq_y, freq_y, norm_y, norm_y, strain_yy)
    el_zz = strain_term(freq_z, freq_z, norm_z, norm_z, strain_zz)
    el_yz = strain_term(freq_y, freq_z, norm_y, norm_z, strain_yz)
    el_xz = strain_term(freq_x, freq_z, norm_x, norm_z, strain_xz)
    el_xy = strain_term(freq_x, freq_y, norm_x, norm_y, strain_xy)
    el_trace = el_xx + el_yy + el_zz
    return jnp.stack(
        [
            lame_lambda * el_trace + 2.0 * shear_modulus * el_xx,
            lame_lambda * el_trace + 2.0 * shear_modulus * el_yy,
            lame_lambda * el_trace + 2.0 * shear_modulus * el_zz,
            2.0 * shear_modulus * el_yz,
            2.0 * shear_modulus * el_xz,
            2.0 * shear_modulus * el_xy,
        ]
    )


def advance(position, lines, burgers, sampled):
    cell_count = sampled.shape[1]
    unit_x = jnp.array([1.0, 0.0, 0.0], jnp.float32)[:, None, None]
    source = jnp.concatenate(
        [
            position[:, shifted : shifted + cell_count] + (shifted - 1.0) * unit_x
            for shifted in range(3)
        ],
        axis=2,
    )
    source_line = jnp.concatenate(
        [lines[:, shifted : shifted + cell_count] for shifted in range(3)], axis=2
    )
    source_burgers = jnp.concatenate(
        [burgers[:, shifted : shifted + cell_count] for shifted in range(3)], axis=2
    )
    target = position[:, 1 : cell_count + 1]
    own_line = lines[:, 1 : cell_count + 1]
    own_burgers = burgers[:, 1 : cell_count + 1]
    offset_vec = target[:, :, :, None] - source[:, :, None, :]
    radius = offset_vec[0] ** 2 + offset_vec[1] ** 2 + offset_vec[2] ** 2 + core_square
    weight = lax.rsqrt(radius) / radius
    line_b = source_line[:, :, None, :]
    cross = (
        jnp.stack(
            [
                offset_vec[1] * line_b[2] - offset_vec[2] * line_b[1],
                offset_vec[2] * line_b[0] - offset_vec[0] * line_b[2],
                offset_vec[0] * line_b[1] - offset_vec[1] * line_b[0],
            ]
        )
        * weight[None]
    )
    moment = jnp.einsum("acij,bcj->abci", cross, source_burgers, precision=lax.Precision.HIGHEST)
    pair_field = pair_factor * (moment + jnp.swapaxes(moment, 0, 1))
    traction = []
    for first in range(3):
        acc_row = jnp.zeros_like(target[0])
        for second in range(3):
            acc_row = (
                acc_row
                + (sampled[full_index[first][second]] + pair_field[first, second])
                * own_burgers[second]
            )
        traction.append(acc_row)
    force_x = traction[1] * own_line[2] - traction[2] * own_line[1]
    force_y = traction[2] * own_line[0] - traction[0] * own_line[2]
    force_z = traction[0] * own_line[1] - traction[1] * own_line[0]
    return target + step_size * jnp.stack([force_x, force_y, force_z])


def phases(row_index, col_index, grid_len):
    product = row_index[:, None] * col_index[None, :] % grid_len
    angle = product.astype(jnp.float32) * (2.0 * math.pi / grid_len)
    return (jnp.cos(angle), jnp.sin(angle))


def transform_last(field, matrix):
    shape = field.shape
    flat = field.reshape(-1, shape[-2] * shape[-1])
    result = jnp.dot(flat, matrix, precision=lax.Precision.HIGHEST)
    return result.reshape(shape[:-2] + (2, matrix.shape[1] // 2))


def body(plastic, offsets, lines, burgers, counts, voxels):
    grid_len = plastic.shape[3]
    pa_count = lax.axis_size("pa")
    grid_index = jnp.arange(grid_len, dtype=jnp.int32)
    bin_count = grid_len // 2 + pa_count
    bin_index = jnp.arange(bin_count, dtype=jnp.int32)
    kept_bins = (bin_index <= grid_len // 2).astype(jnp.float32)
    weights = jnp.where((bin_index == 0) | (bin_index == grid_len // 2), 1.0, 2.0) * kept_bins
    front_cos, front_sin = phases(grid_index, bin_index, grid_len)
    front_table = jnp.concatenate(
        [front_cos * kept_bins[None, :], -front_sin * kept_bins[None, :]], axis=1
    )
    final_cos, final_sin = phases(bin_index, grid_index, grid_len)
    final_table = (
        jnp.concatenate([final_cos * weights[:, None], -final_sin * weights[:, None]], axis=0)
        / grid_len
    )
    turn_cos, turn_sin = phases(grid_index, grid_index, grid_len)
    ahead_table = jnp.block([[turn_cos, -turn_sin], [turn_sin, turn_cos]])
    return_table = jnp.block([[turn_cos, turn_sin], [-turn_sin, turn_cos]]) / grid_len
    comp_count, x_local, y_local = (plastic.shape[0], plastic.shape[1], plastic.shape[2])
    field = jnp.dot(plastic.reshape(-1, grid_len), front_table, precision=lax.Precision.HIGHEST)
    field = field.reshape(comp_count, x_local, y_local, 2, bin_count)
    field = lax.all_to_all(field, "pa", split_axis=4, concat_axis=2, tiled=True)
    field = jnp.transpose(field, (0, 1, 4, 3, 2))
    field = transform_last(field, ahead_table)
    field = lax.all_to_all(field, "gx", split_axis=4, concat_axis=1, tiled=True)
    field = jnp.transpose(field, (0, 4, 2, 3, 1))
    field = transform_last(field, ahead_table)
    y_count = field.shape[1]
    z_count = field.shape[2]
    signed = jnp.where(
        grid_index < grid_len // 2,
        grid_index,
        jnp.where(grid_index == grid_len // 2, 0, grid_index - grid_len),
    ).astype(jnp.float32)
    freq_x = signed[None, None, :]
    freq_y = lax.dynamic_slice_in_dim(signed, lax.axis_index("gx") * y_count, y_count)[
        :, None, None
    ]
    freq_z = lax.dynamic_slice_in_dim(signed, lax.axis_index("pa") * z_count, z_count)[
        None, :, None
    ]
    real_part = stress_of(field[:, :, :, 0], freq_x, freq_y, freq_z)
    imag_part = stress_of(field[:, :, :, 1], freq_x, freq_y, freq_z)
    field = jnp.stack([real_part, imag_part], axis=3)
    field = transform_last(field, return_table)
    field = lax.all_to_all(field, "gx", split_axis=4, concat_axis=1, tiled=True)
    field = jnp.transpose(field, (0, 4, 2, 3, 1))
    field = transform_last(field, return_table)
    field = lax.all_to_all(field, "pa", split_axis=4, concat_axis=2, tiled=True)
    field = jnp.transpose(field, (0, 1, 4, 3, 2))
    flat = field.reshape(-1, 2 * bin_count)
    stress = jnp.dot(flat, final_table, precision=lax.Precision.HIGHEST).reshape(
        comp_count, x_local, y_local, grid_len
    )
    cell_count = offsets.shape[2]
    width_cap = offsets.shape[3]
    flat_stress = stress.reshape(6, -1)
    sampled = jnp.take(flat_stress, voxels.reshape(-1), axis=1).reshape(6, cell_count, width_cap)
    live_mask = (jnp.arange(width_cap, dtype=jnp.int32)[None, :] < counts[0][:, None]).astype(
        jnp.float32
    )
    initial = offsets[:, 0]
    line_dirs = lines[:, 0]
    masked = burgers[:, 0] * live_mask[None]
    fixed_rim = with_halo(jnp.concatenate([line_dirs, masked], axis=0), (("gx", 1),), 1)
    position = initial
    for repeat in range(SUB):
        widened = with_halo(position, (("gx", 1),), 1)
        position = advance(widened, fixed_rim[0:3], fixed_rim[3:6], sampled)
    moved = position - initial
    return (stress, moved[:, None])


LANES = 128
COMPS = 6
FEATURES = 24
SLOTS = 16
VMEM_LIMIT = 48 * 1024 * 1024
VMEM_WHOLE = 63 * 1024 * 1024


def split(value):
    high = value.astype(jnp.bfloat16)
    low = (value - high.astype(jnp.float32)).astype(jnp.bfloat16)
    return high, low


def split_table(table):
    table = np.asarray(table, np.float32)
    high = table.astype(ml_dtypes.bfloat16)
    low = (table - high.astype(np.float32)).astype(ml_dtypes.bfloat16)
    return np.stack([high, low])


def product(left, right, dims=((1,), (0,))):
    left_high, left_low = left
    right_high, right_low = right
    left_all = jnp.concatenate([left_high, left_high, left_low], axis=dims[0][0])
    right_all = jnp.concatenate([right_high, right_low, right_high], axis=dims[1][0])
    return lax.dot_general(
        left_all, right_all, (dims, ((), ())), preferred_element_type=jnp.float32
    )


def tables(grid_len, pa_count, y_local):
    index = np.arange(grid_len)
    bins = np.arange(grid_len // 2)
    angle = 2.0 * np.pi * (np.outer(bins, index) % grid_len) / grid_len
    nyquist = 1.0 - 2.0 * (index % 2)
    forward_z = np.stack([np.cos(angle), -np.sin(angle)], axis=1)
    forward_z[0, 1] = nyquist
    inverse_z = 2.0 * forward_z / grid_len
    inverse_z[0] = forward_z[0] / grid_len
    forward_z = forward_z.reshape(grid_len, grid_len)
    inverse_z = inverse_z.reshape(grid_len, grid_len)
    turn = 2.0 * np.pi * (np.outer(index, index) % grid_len) / grid_len
    cos, sin = np.cos(turn), np.sin(turn)
    ahead = np.array([[cos, sin], [-sin, cos]]).transpose(0, 2, 1, 3)
    back = np.array([[cos, -sin], [sin, cos]]).transpose(0, 2, 1, 3) / grid_len
    size = 2 * grid_len
    forward_y = ahead.reshape(2, grid_len, 2, pa_count, y_local).transpose(3, 2, 4, 0, 1)
    forward_y = forward_y.reshape(size, size)
    inverse_y = back.reshape(2, pa_count, y_local, 2, grid_len).transpose(3, 4, 1, 0, 2)
    inverse_y = inverse_y.reshape(size, size)
    forward_x = ahead.reshape(size, size)
    inverse_x = back.reshape(size, size)
    return [split_table(t) for t in (forward_z, forward_y, forward_x, inverse_x, inverse_y, inverse_z)]


def lane_iota(rows):
    return lax.broadcasted_iota(jnp.int32, (rows, LANES), 1)


def forward_z_kernel(
    x_local,
    y_local,
    plane_ref,
    table_ref,
    out_ref,
    planes,
    table,
    table_sem,
    in_sems,
):
    half = LANES // 2
    tiles = COMPS // 2
    per_comp = x_local * y_local
    first_half = lane_iota(half) < half
    fetch_table = pltpu.make_async_copy(table_ref, table, table_sem)
    fetch_table.start()
    fetches = []
    for tile in range(tiles):
        span = pl.ds(2 * tile * per_comp, 2 * per_comp)
        fetches.append(
            pltpu.make_async_copy(plane_ref.at[span], planes.at[span], in_sems.at[tile])
        )
        fetches[-1].start()
    fetch_table.wait()
    stride = tiles * y_local
    for tile in range(tiles):
        fetches[tile].wait()
        for base in range(0, y_local, 4):
            rows = [
                planes[pl.ds((2 * tile + c) * per_comp + base + y, x_local, stride=y_local), :]
                for y in range(4)
                for c in range(2)
            ]
            lines = split(jnp.concatenate(rows, axis=0))
            waves = product((table[0], table[1]), lines, ((1,), (1,)))
            for y in range(0, 4, 2):
                begin = y * LANES // 2
                low_bins = waves[:half, begin : begin + LANES]
                high_bins = waves[half:, begin : begin + LANES]
                even = jnp.where(first_half, low_bins, pltpu.roll(high_bins, half, 1))
                odd = jnp.where(first_half, pltpu.roll(low_bins, half, 1), high_bins)
                begin = tile * y_local + base + y
                out_ref[pl.ds(begin, half, stride=stride), :] = even
                out_ref[pl.ds(begin + 1, half, stride=stride), :] = odd


def spectral_kernel(
    gx_count,
    pa_count,
    y_local,
    freq_ref,
    data_ref,
    forward_y_ref,
    forward_x_ref,
    inverse_x_ref,
    inverse_y_ref,
    out_ref,
    waves,
    blocks_ref,
    sems,
):
    grid_len = LANES
    size = 2 * grid_len
    tile_count = COMPS // 2
    forward_y = (forward_y_ref[0], forward_y_ref[1])
    forward_x = (forward_x_ref[0], forward_x_ref[1])
    inverse_x = (inverse_x_ref[0], inverse_x_ref[1])
    inverse_y = (inverse_y_ref[0], inverse_y_ref[1])
    x_local = grid_len // gx_count
    def along_y(tile):
        fields = [
            data_ref[:, g, :, :, tile].reshape(size, LANES).T for g in range(gx_count)
        ]
        return product(split(jnp.concatenate(fields, axis=0)), forward_y)

    def along_x(tile, lines):
        planes = []
        for slot in range(4):
            rows = [
                lines[g * LANES + slot * x_local :][:x_local] for g in range(gx_count)
            ]
            plane = jnp.concatenate(rows, axis=0)
            planes.append(jnp.concatenate([plane[:, :LANES], plane[:, LANES:]], axis=0))
        waves[tile] = product(forward_x, split(jnp.concatenate(planes, axis=1)))

    lines = along_y(0)
    for tile in range(tile_count):
        later = along_y(tile + 1) if tile + 1 < tile_count else None
        along_x(tile, lines)
        lines = later

    def signed(index):
        plain = jnp.where(index < grid_len // 2, index, index - grid_len)
        return jnp.where(index == grid_len // 2, 0, plain).astype(jnp.float32)

    step = 16
    freq_y = signed(lax.broadcasted_iota(jnp.int32, (step, LANES), 1))
    row_index = lax.broadcasted_iota(jnp.int32, (step, LANES), 0)

    def operate(chunk, carry):
        start = pl.multiple_of(chunk * step, step)
        freq_x = signed(row_index + start)
        for j in range(2):
            freq_z = freq_ref[j]
            square = freq_x * freq_x + freq_y * freq_y + freq_z * freq_z
            inverse = 1.0 / jnp.maximum(square, 1.0)
            scaled = inverse * inverse * green_coef
            for part in range(2):
                rows = pl.ds(part * grid_len + start, step)

                def at(comp):
                    return (comp // 2, rows, pl.ds((2 * j + comp % 2) * LANES, LANES))

                e_xx, e_yy, e_zz, e_yz, e_xz, e_xy = [waves[at(c)] for c in range(COMPS)]
                trace = (0.5 * lame_lambda) * (e_xx + e_yy + e_zz)
                n_x = (trace + e_xx) * freq_x + e_xy * freq_y + e_xz * freq_z
                n_y = e_xy * freq_x + (trace + e_yy) * freq_y + e_yz * freq_z
                n_z = e_xz * freq_x + e_yz * freq_y + (trace + e_zz) * freq_z
                along = (freq_x * n_x + freq_y * n_y + freq_z * n_z) * scaled
                u_x = n_x * inverse - freq_x * along
                u_y = n_y * inverse - freq_y * along
                u_z = n_z * inverse - freq_z * along
                waves[at(0)] = 2.0 * (freq_x * u_x)
                waves[at(1)] = 2.0 * (freq_y * u_y)
                waves[at(2)] = 2.0 * (freq_z * u_z)
                waves[at(3)] = freq_y * u_z + freq_z * u_y
                waves[at(4)] = freq_x * u_z + freq_z * u_x
                waves[at(5)] = freq_x * u_y + freq_y * u_x
        return carry

    lax.fori_loop(0, grid_len // step, operate, 0, unroll=True)

    stores = []
    for tile in range(tile_count):
        planes = product(inverse_x, split(waves[tile]))
        rows = []
        for g in range(gx_count):
            for slot in range(4):
                lanes = slice(slot * LANES, (slot + 1) * LANES)
                parts = [
                    planes[part * grid_len + g * x_local :][:x_local, lanes] for part in range(2)
                ]
                rows.append(jnp.concatenate(parts, axis=1))
        lines = product(split(jnp.concatenate(rows, axis=0)), inverse_y)
        for g in range(gx_count):
            field = lines[g * LANES : (g + 1) * LANES].T
            blocks_ref[tile, :, g] = field.reshape(pa_count // 2, 2, 2, y_local, LANES)
        place = out_ref.at[:, :, :, :, tile]
        stores.append(pltpu.make_async_copy(blocks_ref.at[tile], place, sems.at[tile]))
        stores[-1].start()
    for store in stores:
        store.wait()


def sample(field_ref, voxel_ref, per_comp, cell_count, cell):
    cell_rows = per_comp // cell_count
    place = lax.broadcasted_iota(jnp.int32, (LANES, LANES), 0)
    row = lax.broadcasted_iota(jnp.int32, (cell_rows, LANES), 0)
    voxel = voxel_ref[pl.ds(cell, 1), :]
    picked_row = lax.shift_right_logical(voxel, LANES.bit_length() - 1)
    picked_place = lax.bitwise_and(voxel, LANES - 1)
    choose = (place == picked_place).astype(jnp.bfloat16)
    keep = row == picked_row - cell * cell_rows
    blocks = [
        jnp.concatenate(
            split(field_ref[pl.ds(comp * per_comp + cell * cell_rows, cell_rows), :]), axis=1
        )
        for comp in range(COMPS)
    ]
    picked = jnp.dot(
        jnp.concatenate(blocks, axis=0),
        jnp.concatenate([choose, choose], axis=0),
        preferred_element_type=jnp.float32,
    )
    found = [
        jnp.sum(
            jnp.where(keep, picked[comp * cell_rows : (comp + 1) * cell_rows], 0.0),
            axis=0,
            keepdims=True,
        )
        for comp in range(COMPS)
    ]
    return jnp.concatenate(found + [jnp.zeros((8 - COMPS, LANES), jnp.float32)], axis=0)


def stress_from(elastic):
    trace = lame_lambda * (elastic[0] + elastic[1] + elastic[2])
    return [
        2.0 * shear_modulus * value + (trace if comp < 3 else 0.0)
        for comp, value in enumerate(elastic)
    ]


def inverse_z_kernel(
    x_local,
    y_local,
    cell_count,
    voxel_ref,
    waves_ref,
    local_ref,
    table_ref,
    strain_ref,
    own_ref,
    low_cells_ref,
    high_cells_ref,
):
    table = (table_ref[0], table_ref[1])
    half = LANES // 2
    per_comp = x_local * y_local
    stride = (COMPS // 2) * y_local
    first_half = lane_iota(half) < half
    for pair in range(y_local // 2):
        for tile in range(COMPS // 2):
            base = tile * y_local + 2 * pair
            even = waves_ref[pl.ds(base, half, stride=stride), :]
            odd = waves_ref[pl.ds(base + 1, half, stride=stride), :]
            low_bins = jnp.where(first_half, even, pltpu.roll(odd, half, 1))
            high_bins = jnp.where(first_half, pltpu.roll(even, half, 1), odd)
            turned = jnp.concatenate([low_bins, high_bins], axis=0).T
            lines = product(split(turned), table)
            for y in range(2):
                for c in range(2):
                    begin = (2 * y + c) * x_local
                    place = (2 * tile + c) * per_comp + 2 * pair + y
                    strain_ref[pl.ds(place, x_local, stride=y_local), :] = lines[begin:][:x_local]
    for cell in range(cell_count):
        found = sample(strain_ref, voxel_ref, per_comp, cell_count, cell) - local_ref[cell]
        own_ref[cell] = found
        if cell < 2:
            low_cells_ref[cell] = found
        if cell >= cell_count - 2:
            high_cells_ref[cell - cell_count + 2] = found


def pair_moments(position, fixed, scratch, pairs, add=()):
    columns, features, moments = scratch
    slots = position[0].shape[0]
    lines, burgers = fixed
    moved = [
        position[1] * lines[2] - position[2] * lines[1],
        position[2] * lines[0] - position[0] * lines[2],
        position[0] * lines[1] - position[1] * lines[0],
    ]
    for shift in range(3):
        offset = shift - 1.0
        shifted = [moved[0], moved[1] - offset * lines[2], moved[2] + offset * lines[1]]
        for b in range(3):
            for a in range(3):
                features[shift, pl.ds((3 * a + b) * slots, slots), :] = lines[a] * burgers[b]
                features[shift, pl.ds((9 + 3 * a + b) * slots, slots), :] = shifted[a] * burgers[b]
    for source in sorted({target + shift - 1 for target in pairs for shift in pairs[target]}):
        for a in range(3):
            row = position[a][source : source + 1]
            columns[source, a] = jnp.broadcast_to(row, (LANES, LANES)).T
    for target, shifts in pairs.items():
        weights = []
        sources = []
        own = [position[a][target : target + 1] for a in range(3)]
        for shift in shifts:
            source = target + shift - 1
            d_x = (own[0] - (shift - 1.0)) - columns[source, 0]
            d_y = own[1] - columns[source, 1]
            d_z = own[2] - columns[source, 2]
            inverse = lax.rsqrt(d_x * d_x + d_y * d_y + d_z * d_z + core_square)
            weights.append(inverse * inverse * inverse)
            sources.append(features[shift, pl.ds(source, FEATURES, stride=slots), :])
        source = jnp.concatenate(sources, axis=1)
        high, rest = split(source)
        low = (source - high.astype(jnp.float32) - rest.astype(jnp.float32)).astype(jnp.bfloat16)
        parts = jnp.concatenate([high, rest, low], axis=0)
        total = jnp.dot(
            jnp.concatenate([parts, parts], axis=1),
            jnp.concatenate(split(jnp.concatenate(weights, axis=0)), axis=0),
            preferred_element_type=jnp.float32,
        )
        total = total[:FEATURES] + (total[FEATURES : 2 * FEATURES] + total[2 * FEATURES :])
        rows = pl.ds(target * FEATURES, FEATURES)
        moments[rows, :] = moments[rows, :] + total if target in add else total


def every_pair(first, last):
    return {target: (0, 1, 2) for target in range(first, last)}


def pair_field(position, moments):
    slots = position[0].shape[0]

    def feature(index):
        return moments[pl.ds(index, slots, stride=FEATURES), :]

    moment = [[None] * 3 for _ in range(3)]
    for b in range(3):
        g = [feature(3 * a + b) for a in range(3)]
        moment[0][b] = position[1] * g[2] - position[2] * g[1] - feature(9 + b)
        moment[1][b] = position[2] * g[0] - position[0] * g[2] - feature(12 + b)
        moment[2][b] = position[0] * g[1] - position[1] * g[0] - feature(15 + b)
    pairs = ((0, 0), (1, 1), (2, 2), (1, 2), (0, 2), (0, 1))
    return [pair_factor * (moment[a][b] + moment[b][a]) for a, b in pairs]


def load_fixed(start_ref):
    values = [start_ref[a] for a in range(9)]
    return values[0:3], values[3:6], values[6:9]


def clear(features, moments):
    features[...] = jnp.zeros_like(features)
    moments[...] = jnp.zeros_like(moments)


def first_field_kernel(
    per_comp,
    cell_count,
    start_ref,
    voxel_ref,
    plastic_ref,
    out_ref,
    local_ref,
    columns,
    features,
    moments,
):
    for cell in range(cell_count):
        local_ref[cell] = sample(plastic_ref, voxel_ref, per_comp, cell_count, cell)
    clear(features, moments)
    position, lines, burgers = load_fixed(start_ref)
    pair_moments(
        position, (lines, burgers), (columns, features, moments), every_pair(1, cell_count + 5)
    )
    for comp, value in enumerate(pair_field(position, moments)):
        out_ref[comp] = value


def moved_on(position, lines, burgers, sampled, field):
    sigma = [sampled[comp] + field[comp] for comp in range(COMPS)]
    traction = [
        sigma[full_index[a][0]] * burgers[0]
        + sigma[full_index[a][1]] * burgers[1]
        + sigma[full_index[a][2]] * burgers[2]
        for a in range(3)
    ]
    return [
        position[0] + step_size * (traction[1] * lines[2] - traction[2] * lines[1]),
        position[1] + step_size * (traction[2] * lines[0] - traction[0] * lines[2]),
        position[2] + step_size * (traction[0] * lines[1] - traction[1] * lines[0]),
    ]


def spread(sampled_ref, parts):
    sampled_ref[...] = jnp.zeros_like(sampled_ref)
    for begin, part in parts:
        sampled_ref[pl.ds(8 * begin, 8 * part.shape[0]), :] = part[...].reshape(-1, LANES)
    return stress_from([sampled_ref[pl.ds(comp, SLOTS, stride=8), :] for comp in range(COMPS)])


def own_moves_kernel(
    cell_count,
    start_ref,
    first_ref,
    own_ref,
    strain_ref,
    plastic_ref,
    stress_ref,
    part_ref,
    columns,
    features,
    moments,
    sampled_ref,
    block,
    sems,
):
    rows = stress_ref.shape[1] // cell_count
    stores = []
    for cell in range(cell_count):
        span = pl.ds(cell * rows, rows)
        elastic = [strain_ref[c, span, :] - plastic_ref[c, span, :] for c in range(COMPS)]
        for comp, value in enumerate(stress_from(elastic)):
            block[comp, span, :] = value
        stores.append(
            pltpu.make_async_copy(block.at[:, span], stress_ref.at[:, span], sems.at[cell])
        )
        stores[-1].start()
    clear(features, moments)
    position, lines, burgers = load_fixed(start_ref)
    sampled = spread(sampled_ref, [(3, own_ref)])
    field = [first_ref[comp] for comp in range(COMPS)]
    position = moved_on(position, lines, burgers, sampled, field)
    first, last = 3, cell_count + 3
    pairs = {
        target: [s for s in range(3) if first <= target + s - 1 < last]
        for target in range(first, last)
    }
    pair_moments(position, (lines, burgers), (columns, features, moments), pairs)
    part_ref[...] = moments[...]
    for store in stores:
        store.wait()


def moves_kernel(
    cell_count,
    start_ref,
    first_ref,
    left_ref,
    own_ref,
    right_ref,
    part_ref,
    out_ref,
    columns,
    features,
    moments,
    sampled_ref,
):
    features[...] = jnp.zeros_like(features)
    moments[...] = part_ref[...]
    position, lines, burgers = load_fixed(start_ref)
    initial = position
    first, last = 3, cell_count + 3
    sampled = spread(sampled_ref, [(1, left_ref), (first, own_ref), (last, right_ref)])
    rest = {first - 1: (0, 1, 2), first: (0,), last - 1: (2,), last: (0, 1, 2)}
    for repeat in range(SUB):
        if repeat == 0:
            field = [first_ref[comp] for comp in range(COMPS)]
        else:
            pair_moments(
                position,
                (lines, burgers),
                (columns, features, moments),
                rest if repeat == 1 else every_pair(first, last),
                (first, last - 1) if repeat == 1 else (),
            )
            field = pair_field(position, moments)
        position = moved_on(position, lines, burgers, sampled, field)
    for a in range(3):
        out_ref[a] = (position[a] - initial[a])[first:last]


def kernel_call(kernel, outs, scratch=(), flops=0, places="", out_places="", limit=VMEM_LIMIT):
    spaces = {"s": pltpu.SMEM, "v": pltpu.VMEM, "h": pltpu.HBM}
    return pl.pallas_call(
        kernel,
        out_shape=outs,
        in_specs=[pl.BlockSpec(memory_space=spaces[p]) for p in places],
        out_specs=[pl.BlockSpec(memory_space=spaces[p]) for p in out_places],
        scratch_shapes=list(scratch),
        compiler_params=pltpu.CompilerParams(vmem_limit_bytes=limit),
        cost_estimate=pl.CostEstimate(flops=flops, bytes_accessed=1 << 20, transcendentals=0),
    )


def in_hbm(array):
    return pltpu.with_memory_space_constraint(array, pltpu.HBM)


def neighbours(low, high):
    count = lax.axis_size("gx")
    forward = [(i, (i + 1) % count) for i in range(count)]
    backward = [(target, source) for source, target in forward]
    return lax.ppermute(high, "gx", forward), lax.ppermute(low, "gx", backward)


def slab_body(plastic, offsets, lines, burgers, counts, voxels):
    f32 = jnp.float32
    comp_count, x_local, y_local, grid_len = plastic.shape
    gx_count = lax.axis_size("gx")
    pa_count = lax.axis_size("pa")
    devices = gx_count * pa_count
    cell_count, cap = voxels.shape[1:]
    tiles = comp_count // 2
    rows = devices * 2 * tiles * y_local
    blocks = (devices, rows // devices, LANES)
    parts = (pa_count // 2, gx_count, 2, 2, tiles, y_local, LANES)
    forward_z, forward_y, forward_x, inverse_x, inverse_y, inverse_z = [
        jnp.asarray(t) for t in tables(grid_len, pa_count, y_local)
    ]
    order = [
        [
            g * pa_count + 2 * z + core
            for z in range(pa_count // 2)
            for g in range(gx_count)
            for core in range(2)
        ]
    ]
    exchange = functools.partial(
        lax.all_to_all,
        axis_name=("gx", "pa"),
        split_axis=0,
        concat_axis=0,
        axis_index_groups=order,
        tiled=True,
    )
    pa_index = lax.axis_index("pa")
    own = (pa_index // 2 * gx_count + lax.axis_index("gx")) * 2 + pa_index % 2
    bins = (own + devices * jnp.arange(2, dtype=jnp.int32)).astype(f32)
    flat_plastic = plastic.reshape(-1, grid_len)
    tile_sems = pltpu.SemaphoreType.DMA((tiles,))

    bins, flat_plastic = lax.optimization_barrier((bins, flat_plastic))

    (waves,) = kernel_call(
        functools.partial(forward_z_kernel, x_local, y_local),
        [pltpu.VMEM((rows, LANES), f32)],
        [
            pltpu.VMEM(flat_plastic.shape, f32),
            pltpu.VMEM(forward_z.shape, jnp.bfloat16),
            pltpu.SemaphoreType.DMA,
            tile_sems,
        ],
        places="hh",
        out_places="v",
    )(in_hbm(flat_plastic), in_hbm(forward_z))
    waves = exchange(waves.reshape(blocks))
    (waves,) = kernel_call(
        functools.partial(spectral_kernel, gx_count, pa_count, y_local),
        [pltpu.HBM(parts, f32)],
        [
            pltpu.VMEM((tiles, 2 * grid_len, 4 * LANES), f32),
            pltpu.VMEM((tiles, pa_count // 2, gx_count, 2, 2, y_local, LANES), f32),
            tile_sems,
        ],
        places="svvvvv",
        out_places="h",
    )(bins, waves.reshape(parts), forward_y, forward_x, inverse_x, inverse_y)
    waves, offsets, lines, burgers, counts = lax.optimization_barrier(
        (waves, offsets, lines, burgers, counts)
    )
    waves = exchange(waves.reshape(blocks))

    live = (jnp.arange(cap, dtype=jnp.int32)[None, :] < counts[0][:, None]).astype(f32)
    start = jnp.concatenate([offsets[:, 0], lines[:, 0], burgers[:, 0] * live[None]], axis=0)
    below, above = neighbours(start[:, :3], start[:, cell_count - 3 :])
    padding = jnp.zeros((9, SLOTS - cell_count - 6, cap), f32)
    start = jnp.concatenate([below, start, above, padding], axis=1)
    pair_scratch = [
        pltpu.VMEM((SLOTS, 3, LANES, LANES), f32),
        pltpu.VMEM((3, FEATURES * SLOTS, LANES), f32),
        pltpu.VMEM((SLOTS * FEATURES, LANES), f32),
    ]
    per_comp = x_local * y_local
    cells = jax.ShapeDtypeStruct((cell_count, 8, cap), f32)
    first, local = kernel_call(
        functools.partial(first_field_kernel, per_comp, cell_count),
        [jax.ShapeDtypeStruct((comp_count, SLOTS, cap), f32), cells],
        pair_scratch,
        places="vvv",
        out_places="vv",
    )(start, voxels[0], flat_plastic)

    waves, first, local = lax.optimization_barrier((waves, first, local))
    end = jax.ShapeDtypeStruct((2, 8, cap), f32)
    strain, own_cells, low_cells, high_cells = kernel_call(
        functools.partial(inverse_z_kernel, x_local, y_local, cell_count),
        [pltpu.VMEM(flat_plastic.shape, f32), cells, end, end],
        places="vvvv",
        out_places="vvvv",
    )(voxels[0], waves.reshape(rows, LANES), local, inverse_z)
    left, right = neighbours(low_cells, high_cells)
    sampled = pltpu.VMEM((8 * SLOTS, LANES), f32)
    whole = (comp_count, per_comp, LANES)
    stress, part = kernel_call(
        functools.partial(own_moves_kernel, cell_count),
        [
            jax.ShapeDtypeStruct(whole, f32),
            jax.ShapeDtypeStruct((SLOTS * FEATURES, cap), f32),
        ],
        pair_scratch
        + [sampled, pltpu.VMEM(whole, f32), pltpu.SemaphoreType.DMA((cell_count,))],
        places="vvvvv",
        out_places="hv",
    )(start, first, own_cells, strain.reshape(whole), plastic.reshape(whole))
    (moved,) = kernel_call(
        functools.partial(moves_kernel, cell_count),
        [jax.ShapeDtypeStruct((3, cell_count, cap), f32)],
        pair_scratch + [sampled],
        places="vvvvvv",
        out_places="v",
    )(start, first, left, own_cells, right, part)
    return (stress.reshape(plastic.shape), moved[:, None])


def fits(mesh, plastic, voxels):
    gx_count, pa_count = mesh.shape["gx"], mesh.shape["pa"]
    grid_len = plastic.shape[3]
    x_local, y_local = plastic.shape[1] // gx_count, plastic.shape[2] // pa_count
    cell_count = voxels.shape[1] // gx_count
    return (
        plastic.shape == (COMPS, LANES, LANES, LANES)
        and 4 * gx_count * pa_count == grid_len
        and 4 * x_local == LANES
        and pa_count % 2 == 0
        and y_local % 8 == 0
        and voxels.shape[2] == LANES
        and 3 <= cell_count <= SLOTS - 6
        and x_local % cell_count == 0
    )


def solution(mesh):
    placed = (
        P(None, "gx", "pa", None),
        P(None, "pa", "gx", None),
        P(None, "pa", "gx", None),
        P(None, "pa", "gx", None),
        P("pa", "gx"),
        P("pa", "gx", None),
    )

    def step(plastic, offsets, lines, burgers, counts, voxels):
        chosen = slab_body if fits(mesh, plastic, voxels) else body
        return jax.shard_map(
            chosen,
            mesh=mesh,
            in_specs=placed,
            out_specs=(P(None, "gx", "pa", None), P(None, "pa", "gx", None)),
            check_vma=False,
        )(plastic, offsets, lines, burgers, counts, voxels)

    return step
```

```python
import functools
import math

import jax
import jax.numpy as jnp
import ml_dtypes
import numpy as np
from jax import lax
from jax.experimental import pallas as pl
from jax.experimental.pallas import tpu as pltpu
from jax.sharding import PartitionSpec as P

SUB = 3


lame_lambda = 1.5
shear_modulus = 1.0
green_coef = 2.5 / 3.5
core_square = 0.09
pair_factor = 1.0 / (4.0 * math.pi)
step_size = 0.05
full_index = ((0, 5, 4), (5, 1, 3), (4, 3, 2))


def with_halo(block, sides, width):
    for axis, dim in sides:
        count = lax.axis_size(axis)
        forward = [(i, i + 1) for i in range(count - 1)]
        forward.append((count - 1, 0))
        backward = [(target, source) for source, target in forward]
        low = lax.ppermute(
            lax.slice_in_dim(block, block.shape[dim] - width, None, axis=dim), axis, forward
        )
        high = lax.ppermute(lax.slice_in_dim(block, 0, width, axis=dim), axis, backward)
        block = jnp.concatenate([low, block, high], axis=dim)
    return block


def stress_of(strain, freq_x, freq_y, freq_z):
    strain_xx, strain_yy, strain_zz = (strain[0], strain[1], strain[2])
    strain_yz, strain_xz, strain_xy = (strain[3], strain[4], strain[5])
    trace = strain_xx + strain_yy + strain_zz
    tau_xx = lame_lambda * trace + 2.0 * shear_modulus * strain_xx
    tau_yy = lame_lambda * trace + 2.0 * shear_modulus * strain_yy
    tau_zz = lame_lambda * trace + 2.0 * shear_modulus * strain_zz
    tau_yz = 2.0 * shear_modulus * strain_yz
    tau_xz = 2.0 * shear_modulus * strain_xz
    tau_xy = 2.0 * shear_modulus * strain_xy
    norm_x = tau_xx * freq_x + tau_xy * freq_y + tau_xz * freq_z
    norm_y = tau_xy * freq_x + tau_yy * freq_y + tau_yz * freq_z
    norm_z = tau_xz * freq_x + tau_yz * freq_y + tau_zz * freq_z
    square = freq_x * freq_x + freq_y * freq_y + freq_z * freq_z
    inverse = 1.0 / jnp.maximum(square, 1.0)
    along_k = (freq_x * norm_x + freq_y * norm_y + freq_z * norm_z) * inverse * inverse * green_coef

    def strain_term(first_q, second_q, first_n, second_n, plastic_part):
        total = (first_q * second_n + second_q * first_n) * inverse / (
            2.0 * shear_modulus
        ) - first_q * second_q * along_k
        return total - plastic_part

    el_xx = strain_term(freq_x, freq_x, norm_x, norm_x, strain_xx)
    el_yy = strain_term(freq_y, freq_y, norm_y, norm_y, strain_yy)
    el_zz = strain_term(freq_z, freq_z, norm_z, norm_z, strain_zz)
    el_yz = strain_term(freq_y, freq_z, norm_y, norm_z, strain_yz)
    el_xz = strain_term(freq_x, freq_z, norm_x, norm_z, strain_xz)
    el_xy = strain_term(freq_x, freq_y, norm_x, norm_y, strain_xy)
    el_trace = el_xx + el_yy + el_zz
    return jnp.stack(
        [
            lame_lambda * el_trace + 2.0 * shear_modulus * el_xx,
            lame_lambda * el_trace + 2.0 * shear_modulus * el_yy,
            lame_lambda * el_trace + 2.0 * shear_modulus * el_zz,
            2.0 * shear_modulus * el_yz,
            2.0 * shear_modulus * el_xz,
            2.0 * shear_modulus * el_xy,
        ]
    )


def advance(position, lines, burgers, sampled):
    cell_count = sampled.shape[1]
    unit_x = jnp.array([1.0, 0.0, 0.0], jnp.float32)[:, None, None]
    source = jnp.concatenate(
        [
            position[:, shifted : shifted + cell_count] + (shifted - 1.0) * unit_x
            for shifted in range(3)
        ],
        axis=2,
    )
    source_line = jnp.concatenate(
        [lines[:, shifted : shifted + cell_count] for shifted in range(3)], axis=2
    )
    source_burgers = jnp.concatenate(
        [burgers[:, shifted : shifted + cell_count] for shifted in range(3)], axis=2
    )
    target = position[:, 1 : cell_count + 1]
    own_line = lines[:, 1 : cell_count + 1]
    own_burgers = burgers[:, 1 : cell_count + 1]
    offset_vec = target[:, :, :, None] - source[:, :, None, :]
    radius = offset_vec[0] ** 2 + offset_vec[1] ** 2 + offset_vec[2] ** 2 + core_square
    weight = lax.rsqrt(radius) / radius
    line_b = source_line[:, :, None, :]
    cross = (
        jnp.stack(
            [
                offset_vec[1] * line_b[2] - offset_vec[2] * line_b[1],
                offset_vec[2] * line_b[0] - offset_vec[0] * line_b[2],
                offset_vec[0] * line_b[1] - offset_vec[1] * line_b[0],
            ]
        )
        * weight[None]
    )
    moment = jnp.einsum("acij,bcj->abci", cross, source_burgers, precision=lax.Precision.HIGHEST)
    pair_field = pair_factor * (moment + jnp.swapaxes(moment, 0, 1))
    traction = []
    for first in range(3):
        acc_row = jnp.zeros_like(target[0])
        for second in range(3):
            acc_row = (
                acc_row
                + (sampled[full_index[first][second]] + pair_field[first, second])
                * own_burgers[second]
            )
        traction.append(acc_row)
    force_x = traction[1] * own_line[2] - traction[2] * own_line[1]
    force_y = traction[2] * own_line[0] - traction[0] * own_line[2]
    force_z = traction[0] * own_line[1] - traction[1] * own_line[0]
    return target + step_size * jnp.stack([force_x, force_y, force_z])


def phases(row_index, col_index, grid_len):
    product = row_index[:, None] * col_index[None, :] % grid_len
    angle = product.astype(jnp.float32) * (2.0 * math.pi / grid_len)
    return (jnp.cos(angle), jnp.sin(angle))


def transform_last(field, matrix):
    shape = field.shape
    flat = field.reshape(-1, shape[-2] * shape[-1])
    result = jnp.dot(flat, matrix, precision=lax.Precision.HIGHEST)
    return result.reshape(shape[:-2] + (2, matrix.shape[1] // 2))


def body(plastic, offsets, lines, burgers, counts, voxels):
    grid_len = plastic.shape[3]
    pa_count = lax.axis_size("pa")
    grid_index = jnp.arange(grid_len, dtype=jnp.int32)
    bin_count = grid_len // 2 + pa_count
    bin_index = jnp.arange(bin_count, dtype=jnp.int32)
    kept_bins = (bin_index <= grid_len // 2).astype(jnp.float32)
    weights = jnp.where((bin_index == 0) | (bin_index == grid_len // 2), 1.0, 2.0) * kept_bins
    front_cos, front_sin = phases(grid_index, bin_index, grid_len)
    front_table = jnp.concatenate(
        [front_cos * kept_bins[None, :], -front_sin * kept_bins[None, :]], axis=1
    )
    final_cos, final_sin = phases(bin_index, grid_index, grid_len)
    final_table = (
        jnp.concatenate([final_cos * weights[:, None], -final_sin * weights[:, None]], axis=0)
        / grid_len
    )
    turn_cos, turn_sin = phases(grid_index, grid_index, grid_len)
    ahead_table = jnp.block([[turn_cos, -turn_sin], [turn_sin, turn_cos]])
    return_table = jnp.block([[turn_cos, turn_sin], [-turn_sin, turn_cos]]) / grid_len
    comp_count, x_local, y_local = (plastic.shape[0], plastic.shape[1], plastic.shape[2])
    field = jnp.dot(plastic.reshape(-1, grid_len), front_table, precision=lax.Precision.HIGHEST)
    field = field.reshape(comp_count, x_local, y_local, 2, bin_count)
    field = lax.all_to_all(field, "pa", split_axis=4, concat_axis=2, tiled=True)
    field = jnp.transpose(field, (0, 1, 4, 3, 2))
    field = transform_last(field, ahead_table)
    field = lax.all_to_all(field, "gx", split_axis=4, concat_axis=1, tiled=True)
    field = jnp.transpose(field, (0, 4, 2, 3, 1))
    field = transform_last(field, ahead_table)
    y_count = field.shape[1]
    z_count = field.shape[2]
    signed = jnp.where(
        grid_index < grid_len // 2,
        grid_index,
        jnp.where(grid_index == grid_len // 2, 0, grid_index - grid_len),
    ).astype(jnp.float32)
    freq_x = signed[None, None, :]
    freq_y = lax.dynamic_slice_in_dim(signed, lax.axis_index("gx") * y_count, y_count)[
        :, None, None
    ]
    freq_z = lax.dynamic_slice_in_dim(signed, lax.axis_index("pa") * z_count, z_count)[
        None, :, None
    ]
    real_part = stress_of(field[:, :, :, 0], freq_x, freq_y, freq_z)
    imag_part = stress_of(field[:, :, :, 1], freq_x, freq_y, freq_z)
    field = jnp.stack([real_part, imag_part], axis=3)
    field = transform_last(field, return_table)
    field = lax.all_to_all(field, "gx", split_axis=4, concat_axis=1, tiled=True)
    field = jnp.transpose(field, (0, 4, 2, 3, 1))
    field = transform_last(field, return_table)
    field = lax.all_to_all(field, "pa", split_axis=4, concat_axis=2, tiled=True)
    field = jnp.transpose(field, (0, 1, 4, 3, 2))
    flat = field.reshape(-1, 2 * bin_count)
    stress = jnp.dot(flat, final_table, precision=lax.Precision.HIGHEST).reshape(
        comp_count, x_local, y_local, grid_len
    )
    cell_count = offsets.shape[2]
    width_cap = offsets.shape[3]
    flat_stress = stress.reshape(6, -1)
    sampled = jnp.take(flat_stress, voxels.reshape(-1), axis=1).reshape(6, cell_count, width_cap)
    live_mask = (jnp.arange(width_cap, dtype=jnp.int32)[None, :] < counts[0][:, None]).astype(
        jnp.float32
    )
    initial = offsets[:, 0]
    line_dirs = lines[:, 0]
    masked = burgers[:, 0] * live_mask[None]
    fixed_rim = with_halo(jnp.concatenate([line_dirs, masked], axis=0), (("gx", 1),), 1)
    position = initial
    for repeat in range(SUB):
        widened = with_halo(position, (("gx", 1),), 1)
        position = advance(widened, fixed_rim[0:3], fixed_rim[3:6], sampled)
    moved = position - initial
    return (stress, moved[:, None])


LANES = 128
COMPS = 6
FEATURES = 24
SLOTS = 16
VMEM_LIMIT = 48 * 1024 * 1024
VMEM_WHOLE = 63 * 1024 * 1024


def split(value):
    high = value.astype(jnp.bfloat16)
    low = (value - high.astype(jnp.float32)).astype(jnp.bfloat16)
    return high, low


def split_table(table):
    table = np.asarray(table, np.float32)
    high = table.astype(ml_dtypes.bfloat16)
    low = (table - high.astype(np.float32)).astype(ml_dtypes.bfloat16)
    return np.stack([high, low])


def product(left, right, dims=((1,), (0,))):
    left_high, left_low = left
    right_high, right_low = right
    left_all = jnp.concatenate([left_high, left_high, left_low], axis=dims[0][0])
    right_all = jnp.concatenate([right_high, right_low, right_high], axis=dims[1][0])
    return lax.dot_general(
        left_all, right_all, (dims, ((), ())), preferred_element_type=jnp.float32
    )


def gray(count):
    return [i ^ (i >> 1) for i in range(count)]


def tables(grid_len, pa_count, y_local):
    index = np.arange(grid_len)
    bins = np.arange(grid_len // 2)
    angle = 2.0 * np.pi * (np.outer(bins, index) % grid_len) / grid_len
    nyquist = 1.0 - 2.0 * (index % 2)
    forward_z = np.stack([np.cos(angle), -np.sin(angle)], axis=1)
    forward_z[0, 1] = nyquist
    inverse_z = 2.0 * forward_z / grid_len
    inverse_z[0] = forward_z[0] / grid_len
    forward_z = forward_z.reshape(grid_len, grid_len)
    inverse_z = inverse_z.reshape(grid_len, grid_len)
    turn = 2.0 * np.pi * (np.outer(index, index) % grid_len) / grid_len
    cos, sin = np.cos(turn), np.sin(turn)
    ahead = np.array([[cos, sin], [-sin, cos]]).transpose(0, 2, 1, 3)
    back = np.array([[cos, -sin], [sin, cos]]).transpose(0, 2, 1, 3) / grid_len
    size = 2 * grid_len
    chips = gray(pa_count // 2)
    forward_y = ahead.reshape(2, grid_len, 2, pa_count // 2, 2, y_local)
    forward_y = forward_y.transpose(3, 4, 2, 5, 0, 1)[chips]
    forward_y = forward_y.reshape(size, size)
    inverse_y = back.reshape(2, pa_count // 2, 2, y_local, 2, grid_len)
    inverse_y = inverse_y.transpose(4, 5, 1, 2, 0, 3)[:, :, chips]
    inverse_y = inverse_y.reshape(size, size)
    forward_x = ahead.reshape(size, size)
    inverse_x = back.reshape(size, size)
    return [split_table(t) for t in (forward_z, forward_y, forward_x, inverse_x, inverse_y, inverse_z)]


def lane_iota(rows):
    return lax.broadcasted_iota(jnp.int32, (rows, LANES), 1)


def forward_z_kernel(
    x_local,
    y_local,
    plane_ref,
    table_ref,
    out_ref,
    planes,
    table,
    table_sem,
    in_sems,
):
    half = LANES // 2
    tiles = COMPS // 2
    per_comp = x_local * y_local
    first_half = lane_iota(half) < half
    fetch_table = pltpu.make_async_copy(table_ref, table, table_sem)
    fetch_table.start()
    fetches = []
    for tile in range(tiles):
        span = pl.ds(2 * tile * per_comp, 2 * per_comp)
        fetches.append(
            pltpu.make_async_copy(plane_ref.at[span], planes.at[span], in_sems.at[tile])
        )
        fetches[-1].start()
    fetch_table.wait()
    stride = tiles * y_local
    for tile in range(tiles):
        fetches[tile].wait()
        for base in range(0, y_local, 4):
            rows = [
                planes[pl.ds((2 * tile + c) * per_comp + base + y, x_local, stride=y_local), :]
                for y in range(4)
                for c in range(2)
            ]
            lines = split(jnp.concatenate(rows, axis=0))
            waves = product((table[0], table[1]), lines, ((1,), (1,)))
            for y in range(0, 4, 2):
                begin = y * LANES // 2
                low_bins = waves[:half, begin : begin + LANES]
                high_bins = waves[half:, begin : begin + LANES]
                even = jnp.where(first_half, low_bins, pltpu.roll(high_bins, half, 1))
                odd = jnp.where(first_half, pltpu.roll(low_bins, half, 1), high_bins)
                begin = tile * y_local + base + y
                out_ref[pl.ds(begin, half, stride=stride), :] = even
                out_ref[pl.ds(begin + 1, half, stride=stride), :] = odd


def spectral_kernel(
    gx_count,
    pa_count,
    y_local,
    freq_ref,
    data_ref,
    forward_y_ref,
    forward_x_ref,
    inverse_x_ref,
    inverse_y_ref,
    out_ref,
    waves,
    blocks_ref,
    sems,
):
    grid_len = LANES
    size = 2 * grid_len
    tile_count = COMPS // 2
    forward_y = (forward_y_ref[0], forward_y_ref[1])
    forward_x = (forward_x_ref[0], forward_x_ref[1])
    inverse_x = (inverse_x_ref[0], inverse_x_ref[1])
    inverse_y = (inverse_y_ref[0], inverse_y_ref[1])
    x_local = grid_len // gx_count
    def along_y(tile):
        fields = [
            data_ref[:, g, :, :, tile].reshape(size, LANES).T for g in range(gx_count)
        ]
        return product(split(jnp.concatenate(fields, axis=0)), forward_y)

    def along_x(tile, lines):
        planes = []
        for slot in range(4):
            rows = [
                lines[g * LANES + slot * x_local :][:x_local] for g in range(gx_count)
            ]
            plane = jnp.concatenate(rows, axis=0)
            planes.append(jnp.concatenate([plane[:, :LANES], plane[:, LANES:]], axis=0))
        waves[tile] = product(forward_x, split(jnp.concatenate(planes, axis=1)))

    lines = along_y(0)
    for tile in range(tile_count):
        later = along_y(tile + 1) if tile + 1 < tile_count else None
        along_x(tile, lines)
        lines = later

    def signed(index):
        plain = jnp.where(index < grid_len // 2, index, index - grid_len)
        return jnp.where(index == grid_len // 2, 0, plain).astype(jnp.float32)

    step = 16
    freq_y = signed(lax.broadcasted_iota(jnp.int32, (step, LANES), 1))
    row_index = lax.broadcasted_iota(jnp.int32, (step, LANES), 0)

    def operate(chunk, carry):
        start = pl.multiple_of(chunk * step, step)
        freq_x = signed(row_index + start)
        for j in range(2):
            freq_z = freq_ref[j]
            square = freq_x * freq_x + freq_y * freq_y + freq_z * freq_z
            inverse = 1.0 / jnp.maximum(square, 1.0)
            scaled = inverse * inverse * green_coef
            for part in range(2):
                rows = pl.ds(part * grid_len + start, step)

                def at(comp):
                    return (comp // 2, rows, pl.ds((2 * j + comp % 2) * LANES, LANES))

                e_xx, e_yy, e_zz, e_yz, e_xz, e_xy = [waves[at(c)] for c in range(COMPS)]
                trace = (0.5 * lame_lambda) * (e_xx + e_yy + e_zz)
                n_x = (trace + e_xx) * freq_x + e_xy * freq_y + e_xz * freq_z
                n_y = e_xy * freq_x + (trace + e_yy) * freq_y + e_yz * freq_z
                n_z = e_xz * freq_x + e_yz * freq_y + (trace + e_zz) * freq_z
                along = (freq_x * n_x + freq_y * n_y + freq_z * n_z) * scaled
                u_x = n_x * inverse - freq_x * along
                u_y = n_y * inverse - freq_y * along
                u_z = n_z * inverse - freq_z * along
                waves[at(0)] = 2.0 * (freq_x * u_x)
                waves[at(1)] = 2.0 * (freq_y * u_y)
                waves[at(2)] = 2.0 * (freq_z * u_z)
                waves[at(3)] = freq_y * u_z + freq_z * u_y
                waves[at(4)] = freq_x * u_z + freq_z * u_x
                waves[at(5)] = freq_x * u_y + freq_y * u_x
        return carry

    lax.fori_loop(0, grid_len // step, operate, 0, unroll=True)

    stores = []
    for tile in range(tile_count):
        planes = product(inverse_x, split(waves[tile]))
        rows = []
        for g in range(gx_count):
            for slot in range(4):
                lanes = slice(slot * LANES, (slot + 1) * LANES)
                parts = [
                    planes[part * grid_len + g * x_local :][:x_local, lanes] for part in range(2)
                ]
                rows.append(jnp.concatenate(parts, axis=1))
        lines = product(split(jnp.concatenate(rows, axis=0)), inverse_y)
        for g in range(gx_count):
            field = lines[g * LANES : (g + 1) * LANES].T
            blocks_ref[tile, :, g] = field.reshape(pa_count // 2, 2, 2, y_local, LANES)
        place = out_ref.at[:, :, :, :, tile]
        stores.append(pltpu.make_async_copy(blocks_ref.at[tile], place, sems.at[tile]))
        stores[-1].start()
    for store in stores:
        store.wait()


def sample(field_ref, voxel_ref, per_comp, cell_count, cell):
    cell_rows = per_comp // cell_count
    place = lax.broadcasted_iota(jnp.int32, (LANES, LANES), 0)
    row = lax.broadcasted_iota(jnp.int32, (cell_rows, LANES), 0)
    voxel = voxel_ref[pl.ds(cell, 1), :]
    picked_row = lax.shift_right_logical(voxel, LANES.bit_length() - 1)
    picked_place = lax.bitwise_and(voxel, LANES - 1)
    choose = (place == picked_place).astype(jnp.bfloat16)
    keep = row == picked_row - cell * cell_rows
    blocks = [
        jnp.concatenate(
            split(field_ref[pl.ds(comp * per_comp + cell * cell_rows, cell_rows), :]), axis=1
        )
        for comp in range(COMPS)
    ]
    picked = jnp.dot(
        jnp.concatenate(blocks, axis=0),
        jnp.concatenate([choose, choose], axis=0),
        preferred_element_type=jnp.float32,
    )
    found = [
        jnp.sum(
            jnp.where(keep, picked[comp * cell_rows : (comp + 1) * cell_rows], 0.0),
            axis=0,
            keepdims=True,
        )
        for comp in range(COMPS)
    ]
    return jnp.concatenate(found + [jnp.zeros((8 - COMPS, LANES), jnp.float32)], axis=0)


def stress_from(elastic):
    trace = lame_lambda * (elastic[0] + elastic[1] + elastic[2])
    return [
        2.0 * shear_modulus * value + (trace if comp < 3 else 0.0)
        for comp, value in enumerate(elastic)
    ]


def inverse_z_kernel(
    x_local,
    y_local,
    cell_count,
    voxel_ref,
    waves_ref,
    local_ref,
    table_ref,
    strain_ref,
    own_ref,
    low_cells_ref,
    high_cells_ref,
):
    table = (table_ref[0], table_ref[1])
    half = LANES // 2
    per_comp = x_local * y_local
    stride = (COMPS // 2) * y_local
    first_half = lane_iota(half) < half
    for pair in range(y_local // 2):
        for tile in range(COMPS // 2):
            base = tile * y_local + 2 * pair
            even = waves_ref[pl.ds(base, half, stride=stride), :]
            odd = waves_ref[pl.ds(base + 1, half, stride=stride), :]
            low_bins = jnp.where(first_half, even, pltpu.roll(odd, half, 1))
            high_bins = jnp.where(first_half, pltpu.roll(even, half, 1), odd)
            turned = jnp.concatenate([low_bins, high_bins], axis=0).T
            lines = product(split(turned), table)
            for y in range(2):
                for c in range(2):
                    begin = (2 * y + c) * x_local
                    place = (2 * tile + c) * per_comp + 2 * pair + y
                    strain_ref[pl.ds(place, x_local, stride=y_local), :] = lines[begin:][:x_local]
    for cell in range(cell_count):
        found = sample(strain_ref, voxel_ref, per_comp, cell_count, cell) - local_ref[cell]
        own_ref[cell] = found
        if cell < 2:
            low_cells_ref[cell] = found
        if cell >= cell_count - 2:
            high_cells_ref[cell - cell_count + 2] = found


def pair_moments(position, fixed, scratch, pairs, add=()):
    columns, features, moments = scratch
    slots = position[0].shape[0]
    lines, burgers = fixed
    moved = [
        position[1] * lines[2] - position[2] * lines[1],
        position[2] * lines[0] - position[0] * lines[2],
        position[0] * lines[1] - position[1] * lines[0],
    ]
    for shift in range(3):
        offset = shift - 1.0
        shifted = [moved[0], moved[1] - offset * lines[2], moved[2] + offset * lines[1]]
        for b in range(3):
            for a in range(3):
                features[shift, pl.ds((3 * a + b) * slots, slots), :] = lines[a] * burgers[b]
                features[shift, pl.ds((9 + 3 * a + b) * slots, slots), :] = shifted[a] * burgers[b]
    for source in sorted({target + shift - 1 for target in pairs for shift in pairs[target]}):
        for a in range(3):
            row = position[a][source : source + 1]
            columns[source, a] = jnp.broadcast_to(row, (LANES, LANES)).T
    for target, shifts in pairs.items():
        weights = []
        sources = []
        own = [position[a][target : target + 1] for a in range(3)]
        for shift in shifts:
            source = target + shift - 1
            d_x = (own[0] - (shift - 1.0)) - columns[source, 0]
            d_y = own[1] - columns[source, 1]
            d_z = own[2] - columns[source, 2]
            inverse = lax.rsqrt(d_x * d_x + d_y * d_y + d_z * d_z + core_square)
            weights.append(inverse * inverse * inverse)
            sources.append(features[shift, pl.ds(source, FEATURES, stride=slots), :])
        source = jnp.concatenate(sources, axis=1)
        high, rest = split(source)
        low = (source - high.astype(jnp.float32) - rest.astype(jnp.float32)).astype(jnp.bfloat16)
        parts = jnp.concatenate([high, rest, low], axis=0)
        total = jnp.dot(
            jnp.concatenate([parts, parts], axis=1),
            jnp.concatenate(split(jnp.concatenate(weights, axis=0)), axis=0),
            preferred_element_type=jnp.float32,
        )
        total = total[:FEATURES] + (total[FEATURES : 2 * FEATURES] + total[2 * FEATURES :])
        rows = pl.ds(target * FEATURES, FEATURES)
        moments[rows, :] = moments[rows, :] + total if target in add else total


def every_pair(first, last):
    return {target: (0, 1, 2) for target in range(first, last)}


def pair_field(position, moments):
    slots = position[0].shape[0]

    def feature(index):
        return moments[pl.ds(index, slots, stride=FEATURES), :]

    moment = [[None] * 3 for _ in range(3)]
    for b in range(3):
        g = [feature(3 * a + b) for a in range(3)]
        moment[0][b] = position[1] * g[2] - position[2] * g[1] - feature(9 + b)
        moment[1][b] = position[2] * g[0] - position[0] * g[2] - feature(12 + b)
        moment[2][b] = position[0] * g[1] - position[1] * g[0] - feature(15 + b)
    pairs = ((0, 0), (1, 1), (2, 2), (1, 2), (0, 2), (0, 1))
    return [pair_factor * (moment[a][b] + moment[b][a]) for a, b in pairs]


def load_fixed(start_ref):
    values = [start_ref[a] for a in range(9)]
    return values[0:3], values[3:6], values[6:9]


def clear(features, moments):
    features[...] = jnp.zeros_like(features)
    moments[...] = jnp.zeros_like(moments)


def first_field_kernel(
    per_comp,
    cell_count,
    start_ref,
    voxel_ref,
    plastic_ref,
    out_ref,
    local_ref,
    columns,
    features,
    moments,
):
    for cell in range(cell_count):
        local_ref[cell] = sample(plastic_ref, voxel_ref, per_comp, cell_count, cell)
    clear(features, moments)
    position, lines, burgers = load_fixed(start_ref)
    pair_moments(
        position, (lines, burgers), (columns, features, moments), every_pair(1, cell_count + 5)
    )
    for comp, value in enumerate(pair_field(position, moments)):
        out_ref[comp] = value


def moved_on(position, lines, burgers, sampled, field):
    sigma = [sampled[comp] + field[comp] for comp in range(COMPS)]
    traction = [
        sigma[full_index[a][0]] * burgers[0]
        + sigma[full_index[a][1]] * burgers[1]
        + sigma[full_index[a][2]] * burgers[2]
        for a in range(3)
    ]
    return [
        position[0] + step_size * (traction[1] * lines[2] - traction[2] * lines[1]),
        position[1] + step_size * (traction[2] * lines[0] - traction[0] * lines[2]),
        position[2] + step_size * (traction[0] * lines[1] - traction[1] * lines[0]),
    ]


def spread(sampled_ref, parts):
    sampled_ref[...] = jnp.zeros_like(sampled_ref)
    for begin, part in parts:
        sampled_ref[pl.ds(8 * begin, 8 * part.shape[0]), :] = part[...].reshape(-1, LANES)
    return stress_from([sampled_ref[pl.ds(comp, SLOTS, stride=8), :] for comp in range(COMPS)])


def own_moves_kernel(
    cell_count,
    start_ref,
    first_ref,
    own_ref,
    strain_ref,
    plastic_ref,
    stress_ref,
    part_ref,
    columns,
    features,
    moments,
    sampled_ref,
    block,
    sems,
):
    rows = stress_ref.shape[1] // cell_count
    stores = []
    for cell in range(cell_count):
        span = pl.ds(cell * rows, rows)
        elastic = [strain_ref[c, span, :] - plastic_ref[c, span, :] for c in range(COMPS)]
        for comp, value in enumerate(stress_from(elastic)):
            block[comp, span, :] = value
        stores.append(
            pltpu.make_async_copy(block.at[:, span], stress_ref.at[:, span], sems.at[cell])
        )
        stores[-1].start()
    clear(features, moments)
    position, lines, burgers = load_fixed(start_ref)
    sampled = spread(sampled_ref, [(3, own_ref)])
    field = [first_ref[comp] for comp in range(COMPS)]
    position = moved_on(position, lines, burgers, sampled, field)
    first, last = 3, cell_count + 3
    pairs = {
        target: [s for s in range(3) if first <= target + s - 1 < last]
        for target in range(first, last)
    }
    pair_moments(position, (lines, burgers), (columns, features, moments), pairs)
    part_ref[...] = moments[...]
    for store in stores:
        store.wait()


def moves_kernel(
    cell_count,
    start_ref,
    first_ref,
    left_ref,
    own_ref,
    right_ref,
    part_ref,
    out_ref,
    columns,
    features,
    moments,
    sampled_ref,
):
    features[...] = jnp.zeros_like(features)
    moments[...] = part_ref[...]
    position, lines, burgers = load_fixed(start_ref)
    initial = position
    first, last = 3, cell_count + 3
    sampled = spread(sampled_ref, [(1, left_ref), (first, own_ref), (last, right_ref)])
    rest = {first - 1: (0, 1, 2), first: (0,), last - 1: (2,), last: (0, 1, 2)}
    for repeat in range(SUB):
        if repeat == 0:
            field = [first_ref[comp] for comp in range(COMPS)]
        else:
            pair_moments(
                position,
                (lines, burgers),
                (columns, features, moments),
                rest if repeat == 1 else every_pair(first, last),
                (first, last - 1) if repeat == 1 else (),
            )
            field = pair_field(position, moments)
        position = moved_on(position, lines, burgers, sampled, field)
    for a in range(3):
        out_ref[a] = (position[a] - initial[a])[first:last]


def kernel_call(kernel, outs, scratch=(), flops=0, places="", out_places="", limit=VMEM_LIMIT):
    spaces = {"s": pltpu.SMEM, "v": pltpu.VMEM, "h": pltpu.HBM}
    return pl.pallas_call(
        kernel,
        out_shape=outs,
        in_specs=[pl.BlockSpec(memory_space=spaces[p]) for p in places],
        out_specs=[pl.BlockSpec(memory_space=spaces[p]) for p in out_places],
        scratch_shapes=list(scratch),
        compiler_params=pltpu.CompilerParams(vmem_limit_bytes=limit),
        cost_estimate=pl.CostEstimate(flops=flops, bytes_accessed=1 << 20, transcendentals=0),
    )


def in_hbm(array):
    return pltpu.with_memory_space_constraint(array, pltpu.HBM)


def neighbours(low, high):
    count = lax.axis_size("gx")
    forward = [(i, (i + 1) % count) for i in range(count)]
    backward = [(target, source) for source, target in forward]
    return lax.ppermute(high, "gx", forward), lax.ppermute(low, "gx", backward)


def slab_body(plastic, offsets, lines, burgers, counts, voxels):
    f32 = jnp.float32
    comp_count, x_local, y_local, grid_len = plastic.shape
    gx_count = lax.axis_size("gx")
    pa_count = lax.axis_size("pa")
    devices = gx_count * pa_count
    cell_count, cap = voxels.shape[1:]
    tiles = comp_count // 2
    rows = devices * 2 * tiles * y_local
    blocks = (devices, rows // devices, LANES)
    parts = (pa_count // 2, gx_count, 2, 2, tiles, y_local, LANES)
    forward_z, forward_y, forward_x, inverse_x, inverse_y, inverse_z = [
        jnp.asarray(t) for t in tables(grid_len, pa_count, y_local)
    ]
    order = [
        [
            g * pa_count + 2 * z + core
            for z in gray(pa_count // 2)
            for g in range(gx_count)
            for core in range(2)
        ]
    ]
    exchange = functools.partial(
        lax.all_to_all,
        axis_name=("gx", "pa"),
        split_axis=0,
        concat_axis=0,
        axis_index_groups=order,
        tiled=True,
    )
    pa_index = lax.axis_index("pa")
    place = pa_index // 2
    for shift in (1, 2, 4, 8):
        place = place ^ (pa_index // 2 >> shift)
    own = (place * gx_count + lax.axis_index("gx")) * 2 + pa_index % 2
    bins = (own + devices * jnp.arange(2, dtype=jnp.int32)).astype(f32)
    flat_plastic = plastic.reshape(-1, grid_len)
    tile_sems = pltpu.SemaphoreType.DMA((tiles,))

    bins, flat_plastic = lax.optimization_barrier((bins, flat_plastic))

    (waves,) = kernel_call(
        functools.partial(forward_z_kernel, x_local, y_local),
        [pltpu.VMEM((rows, LANES), f32)],
        [
            pltpu.VMEM(flat_plastic.shape, f32),
            pltpu.VMEM(forward_z.shape, jnp.bfloat16),
            pltpu.SemaphoreType.DMA,
            tile_sems,
        ],
        places="hh",
        out_places="v",
    )(in_hbm(flat_plastic), in_hbm(forward_z))
    waves = exchange(waves.reshape(blocks))
    (waves,) = kernel_call(
        functools.partial(spectral_kernel, gx_count, pa_count, y_local),
        [pltpu.HBM(parts, f32)],
        [
            pltpu.VMEM((tiles, 2 * grid_len, 4 * LANES), f32),
            pltpu.VMEM((tiles, pa_count // 2, gx_count, 2, 2, y_local, LANES), f32),
            tile_sems,
        ],
        places="svvvvv",
        out_places="h",
    )(bins, waves.reshape(parts), forward_y, forward_x, inverse_x, inverse_y)
    waves, offsets, lines, burgers, counts = lax.optimization_barrier(
        (waves, offsets, lines, burgers, counts)
    )
    waves = exchange(waves.reshape(blocks))

    live = (jnp.arange(cap, dtype=jnp.int32)[None, :] < counts[0][:, None]).astype(f32)
    start = jnp.concatenate([offsets[:, 0], lines[:, 0], burgers[:, 0] * live[None]], axis=0)
    below, above = neighbours(start[:, :3], start[:, cell_count - 3 :])
    padding = jnp.zeros((9, SLOTS - cell_count - 6, cap), f32)
    start = jnp.concatenate([below, start, above, padding], axis=1)
    pair_scratch = [
        pltpu.VMEM((SLOTS, 3, LANES, LANES), f32),
        pltpu.VMEM((3, FEATURES * SLOTS, LANES), f32),
        pltpu.VMEM((SLOTS * FEATURES, LANES), f32),
    ]
    per_comp = x_local * y_local
    cells = jax.ShapeDtypeStruct((cell_count, 8, cap), f32)
    first, local = kernel_call(
        functools.partial(first_field_kernel, per_comp, cell_count),
        [jax.ShapeDtypeStruct((comp_count, SLOTS, cap), f32), cells],
        pair_scratch,
        places="vvv",
        out_places="vv",
    )(start, voxels[0], flat_plastic)

    waves, first, local = lax.optimization_barrier((waves, first, local))
    end = jax.ShapeDtypeStruct((2, 8, cap), f32)
    strain, own_cells, low_cells, high_cells = kernel_call(
        functools.partial(inverse_z_kernel, x_local, y_local, cell_count),
        [pltpu.VMEM(flat_plastic.shape, f32), cells, end, end],
        places="vvvv",
        out_places="vvvv",
    )(voxels[0], waves.reshape(rows, LANES), local, inverse_z)
    left, right = neighbours(low_cells, high_cells)
    sampled = pltpu.VMEM((8 * SLOTS, LANES), f32)
    whole = (comp_count, per_comp, LANES)
    stress, part = kernel_call(
        functools.partial(own_moves_kernel, cell_count),
        [
            jax.ShapeDtypeStruct(whole, f32),
            jax.ShapeDtypeStruct((SLOTS * FEATURES, cap), f32),
        ],
        pair_scratch
        + [sampled, pltpu.VMEM(whole, f32), pltpu.SemaphoreType.DMA((cell_count,))],
        places="vvvvv",
        out_places="hv",
    )(start, first, own_cells, strain.reshape(whole), plastic.reshape(whole))
    (moved,) = kernel_call(
        functools.partial(moves_kernel, cell_count),
        [jax.ShapeDtypeStruct((3, cell_count, cap), f32)],
        pair_scratch + [sampled],
        places="vvvvvv",
        out_places="v",
    )(start, first, left, own_cells, right, part)
    return (stress.reshape(plastic.shape), moved[:, None])


def fits(mesh, plastic, voxels):
    gx_count, pa_count = mesh.shape["gx"], mesh.shape["pa"]
    grid_len = plastic.shape[3]
    x_local, y_local = plastic.shape[1] // gx_count, plastic.shape[2] // pa_count
    cell_count = voxels.shape[1] // gx_count
    return (
        plastic.shape == (COMPS, LANES, LANES, LANES)
        and 4 * gx_count * pa_count == grid_len
        and 4 * x_local == LANES
        and pa_count % 2 == 0
        and y_local % 8 == 0
        and voxels.shape[2] == LANES
        and 3 <= cell_count <= SLOTS - 6
        and x_local % cell_count == 0
    )


def solution(mesh):
    placed = (
        P(None, "gx", "pa", None),
        P(None, "pa", "gx", None),
        P(None, "pa", "gx", None),
        P(None, "pa", "gx", None),
        P("pa", "gx"),
        P("pa", "gx", None),
    )

    def step(plastic, offsets, lines, burgers, counts, voxels):
        chosen = slab_body if fits(mesh, plastic, voxels) else body
        return jax.shard_map(
            chosen,
            mesh=mesh,
            in_specs=placed,
            out_specs=(P(None, "gx", "pa", None), P(None, "pa", "gx", None)),
            check_vma=False,
        )(plastic, offsets, lines, burgers, counts, voxels)

    return step
```

```python
import functools
import math

import jax
import jax.numpy as jnp
import ml_dtypes
import numpy as np
from jax import lax
from jax.experimental import pallas as pl
from jax.experimental.pallas import tpu as pltpu
from jax.sharding import PartitionSpec as P

SUB = 3


lame_lambda = 1.5
shear_modulus = 1.0
green_coef = 2.5 / 3.5
core_square = 0.09
pair_factor = 1.0 / (4.0 * math.pi)
step_size = 0.05
full_index = ((0, 5, 4), (5, 1, 3), (4, 3, 2))


def with_halo(block, sides, width):
    for axis, dim in sides:
        count = lax.axis_size(axis)
        forward = [(i, i + 1) for i in range(count - 1)]
        forward.append((count - 1, 0))
        backward = [(target, source) for source, target in forward]
        low = lax.ppermute(
            lax.slice_in_dim(block, block.shape[dim] - width, None, axis=dim), axis, forward
        )
        high = lax.ppermute(lax.slice_in_dim(block, 0, width, axis=dim), axis, backward)
        block = jnp.concatenate([low, block, high], axis=dim)
    return block


def stress_of(strain, freq_x, freq_y, freq_z):
    strain_xx, strain_yy, strain_zz = (strain[0], strain[1], strain[2])
    strain_yz, strain_xz, strain_xy = (strain[3], strain[4], strain[5])
    trace = strain_xx + strain_yy + strain_zz
    tau_xx = lame_lambda * trace + 2.0 * shear_modulus * strain_xx
    tau_yy = lame_lambda * trace + 2.0 * shear_modulus * strain_yy
    tau_zz = lame_lambda * trace + 2.0 * shear_modulus * strain_zz
    tau_yz = 2.0 * shear_modulus * strain_yz
    tau_xz = 2.0 * shear_modulus * strain_xz
    tau_xy = 2.0 * shear_modulus * strain_xy
    norm_x = tau_xx * freq_x + tau_xy * freq_y + tau_xz * freq_z
    norm_y = tau_xy * freq_x + tau_yy * freq_y + tau_yz * freq_z
    norm_z = tau_xz * freq_x + tau_yz * freq_y + tau_zz * freq_z
    square = freq_x * freq_x + freq_y * freq_y + freq_z * freq_z
    inverse = 1.0 / jnp.maximum(square, 1.0)
    along_k = (freq_x * norm_x + freq_y * norm_y + freq_z * norm_z) * inverse * inverse * green_coef

    def strain_term(first_q, second_q, first_n, second_n, plastic_part):
        total = (first_q * second_n + second_q * first_n) * inverse / (
            2.0 * shear_modulus
        ) - first_q * second_q * along_k
        return total - plastic_part

    el_xx = strain_term(freq_x, freq_x, norm_x, norm_x, strain_xx)
    el_yy = strain_term(freq_y, freq_y, norm_y, norm_y, strain_yy)
    el_zz = strain_term(freq_z, freq_z, norm_z, norm_z, strain_zz)
    el_yz = strain_term(freq_y, freq_z, norm_y, norm_z, strain_yz)
    el_xz = strain_term(freq_x, freq_z, norm_x, norm_z, strain_xz)
    el_xy = strain_term(freq_x, freq_y, norm_x, norm_y, strain_xy)
    el_trace = el_xx + el_yy + el_zz
    return jnp.stack(
        [
            lame_lambda * el_trace + 2.0 * shear_modulus * el_xx,
            lame_lambda * el_trace + 2.0 * shear_modulus * el_yy,
            lame_lambda * el_trace + 2.0 * shear_modulus * el_zz,
            2.0 * shear_modulus * el_yz,
            2.0 * shear_modulus * el_xz,
            2.0 * shear_modulus * el_xy,
        ]
    )


def advance(position, lines, burgers, sampled):
    cell_count = sampled.shape[1]
    unit_x = jnp.array([1.0, 0.0, 0.0], jnp.float32)[:, None, None]
    source = jnp.concatenate(
        [
            position[:, shifted : shifted + cell_count] + (shifted - 1.0) * unit_x
            for shifted in range(3)
        ],
        axis=2,
    )
    source_line = jnp.concatenate(
        [lines[:, shifted : shifted + cell_count] for shifted in range(3)], axis=2
    )
    source_burgers = jnp.concatenate(
        [burgers[:, shifted : shifted + cell_count] for shifted in range(3)], axis=2
    )
    target = position[:, 1 : cell_count + 1]
    own_line = lines[:, 1 : cell_count + 1]
    own_burgers = burgers[:, 1 : cell_count + 1]
    offset_vec = target[:, :, :, None] - source[:, :, None, :]
    radius = offset_vec[0] ** 2 + offset_vec[1] ** 2 + offset_vec[2] ** 2 + core_square
    weight = lax.rsqrt(radius) / radius
    line_b = source_line[:, :, None, :]
    cross = (
        jnp.stack(
            [
                offset_vec[1] * line_b[2] - offset_vec[2] * line_b[1],
                offset_vec[2] * line_b[0] - offset_vec[0] * line_b[2],
                offset_vec[0] * line_b[1] - offset_vec[1] * line_b[0],
            ]
        )
        * weight[None]
    )
    moment = jnp.einsum("acij,bcj->abci", cross, source_burgers, precision=lax.Precision.HIGHEST)
    pair_field = pair_factor * (moment + jnp.swapaxes(moment, 0, 1))
    traction = []
    for first in range(3):
        acc_row = jnp.zeros_like(target[0])
        for second in range(3):
            acc_row = (
                acc_row
                + (sampled[full_index[first][second]] + pair_field[first, second])
                * own_burgers[second]
            )
        traction.append(acc_row)
    force_x = traction[1] * own_line[2] - traction[2] * own_line[1]
    force_y = traction[2] * own_line[0] - traction[0] * own_line[2]
    force_z = traction[0] * own_line[1] - traction[1] * own_line[0]
    return target + step_size * jnp.stack([force_x, force_y, force_z])


def phases(row_index, col_index, grid_len):
    product = row_index[:, None] * col_index[None, :] % grid_len
    angle = product.astype(jnp.float32) * (2.0 * math.pi / grid_len)
    return (jnp.cos(angle), jnp.sin(angle))


def transform_last(field, matrix):
    shape = field.shape
    flat = field.reshape(-1, shape[-2] * shape[-1])
    result = jnp.dot(flat, matrix, precision=lax.Precision.HIGHEST)
    return result.reshape(shape[:-2] + (2, matrix.shape[1] // 2))


def body(plastic, offsets, lines, burgers, counts, voxels):
    grid_len = plastic.shape[3]
    pa_count = lax.axis_size("pa")
    grid_index = jnp.arange(grid_len, dtype=jnp.int32)
    bin_count = grid_len // 2 + pa_count
    bin_index = jnp.arange(bin_count, dtype=jnp.int32)
    kept_bins = (bin_index <= grid_len // 2).astype(jnp.float32)
    weights = jnp.where((bin_index == 0) | (bin_index == grid_len // 2), 1.0, 2.0) * kept_bins
    front_cos, front_sin = phases(grid_index, bin_index, grid_len)
    front_table = jnp.concatenate(
        [front_cos * kept_bins[None, :], -front_sin * kept_bins[None, :]], axis=1
    )
    final_cos, final_sin = phases(bin_index, grid_index, grid_len)
    final_table = (
        jnp.concatenate([final_cos * weights[:, None], -final_sin * weights[:, None]], axis=0)
        / grid_len
    )
    turn_cos, turn_sin = phases(grid_index, grid_index, grid_len)
    ahead_table = jnp.block([[turn_cos, -turn_sin], [turn_sin, turn_cos]])
    return_table = jnp.block([[turn_cos, turn_sin], [-turn_sin, turn_cos]]) / grid_len
    comp_count, x_local, y_local = (plastic.shape[0], plastic.shape[1], plastic.shape[2])
    field = jnp.dot(plastic.reshape(-1, grid_len), front_table, precision=lax.Precision.HIGHEST)
    field = field.reshape(comp_count, x_local, y_local, 2, bin_count)
    field = lax.all_to_all(field, "pa", split_axis=4, concat_axis=2, tiled=True)
    field = jnp.transpose(field, (0, 1, 4, 3, 2))
    field = transform_last(field, ahead_table)
    field = lax.all_to_all(field, "gx", split_axis=4, concat_axis=1, tiled=True)
    field = jnp.transpose(field, (0, 4, 2, 3, 1))
    field = transform_last(field, ahead_table)
    y_count = field.shape[1]
    z_count = field.shape[2]
    signed = jnp.where(
        grid_index < grid_len // 2,
        grid_index,
        jnp.where(grid_index == grid_len // 2, 0, grid_index - grid_len),
    ).astype(jnp.float32)
    freq_x = signed[None, None, :]
    freq_y = lax.dynamic_slice_in_dim(signed, lax.axis_index("gx") * y_count, y_count)[
        :, None, None
    ]
    freq_z = lax.dynamic_slice_in_dim(signed, lax.axis_index("pa") * z_count, z_count)[
        None, :, None
    ]
    real_part = stress_of(field[:, :, :, 0], freq_x, freq_y, freq_z)
    imag_part = stress_of(field[:, :, :, 1], freq_x, freq_y, freq_z)
    field = jnp.stack([real_part, imag_part], axis=3)
    field = transform_last(field, return_table)
    field = lax.all_to_all(field, "gx", split_axis=4, concat_axis=1, tiled=True)
    field = jnp.transpose(field, (0, 4, 2, 3, 1))
    field = transform_last(field, return_table)
    field = lax.all_to_all(field, "pa", split_axis=4, concat_axis=2, tiled=True)
    field = jnp.transpose(field, (0, 1, 4, 3, 2))
    flat = field.reshape(-1, 2 * bin_count)
    stress = jnp.dot(flat, final_table, precision=lax.Precision.HIGHEST).reshape(
        comp_count, x_local, y_local, grid_len
    )
    cell_count = offsets.shape[2]
    width_cap = offsets.shape[3]
    flat_stress = stress.reshape(6, -1)
    sampled = jnp.take(flat_stress, voxels.reshape(-1), axis=1).reshape(6, cell_count, width_cap)
    live_mask = (jnp.arange(width_cap, dtype=jnp.int32)[None, :] < counts[0][:, None]).astype(
        jnp.float32
    )
    initial = offsets[:, 0]
    line_dirs = lines[:, 0]
    masked = burgers[:, 0] * live_mask[None]
    fixed_rim = with_halo(jnp.concatenate([line_dirs, masked], axis=0), (("gx", 1),), 1)
    position = initial
    for repeat in range(SUB):
        widened = with_halo(position, (("gx", 1),), 1)
        position = advance(widened, fixed_rim[0:3], fixed_rim[3:6], sampled)
    moved = position - initial
    return (stress, moved[:, None])


LANES = 128
COMPS = 6
FEATURES = 24
SLOTS = 16
VMEM_LIMIT = 48 * 1024 * 1024
VMEM_WHOLE = 63 * 1024 * 1024


def split(value):
    high = value.astype(jnp.bfloat16)
    low = (value - high.astype(jnp.float32)).astype(jnp.bfloat16)
    return high, low


def split_table(table):
    table = np.asarray(table, np.float32)
    high = table.astype(ml_dtypes.bfloat16)
    low = (table - high.astype(np.float32)).astype(ml_dtypes.bfloat16)
    return np.stack([high, low])


def product(left, right, dims=((1,), (0,))):
    left_high, left_low = left
    right_high, right_low = right
    left_all = jnp.concatenate([left_high, left_high, left_low], axis=dims[0][0])
    right_all = jnp.concatenate([right_high, right_low, right_high], axis=dims[1][0])
    return lax.dot_general(
        left_all, right_all, (dims, ((), ())), preferred_element_type=jnp.float32
    )


def gray(count):
    return [i ^ (i >> 1) for i in range(count)]


def tables(grid_len, pa_count, y_local):
    index = np.arange(grid_len)
    bins = np.arange(grid_len // 2)
    angle = 2.0 * np.pi * (np.outer(bins, index) % grid_len) / grid_len
    nyquist = 1.0 - 2.0 * (index % 2)
    forward_z = np.stack([np.cos(angle), -np.sin(angle)], axis=1)
    forward_z[0, 1] = nyquist
    inverse_z = 2.0 * forward_z / grid_len
    inverse_z[0] = forward_z[0] / grid_len
    forward_z = forward_z.reshape(grid_len, grid_len)
    inverse_z = inverse_z.reshape(grid_len, grid_len)
    turn = 2.0 * np.pi * (np.outer(index, index) % grid_len) / grid_len
    cos, sin = np.cos(turn), np.sin(turn)
    ahead = np.array([[cos, sin], [-sin, cos]]).transpose(0, 2, 1, 3)
    back = np.array([[cos, -sin], [sin, cos]]).transpose(0, 2, 1, 3) / grid_len
    size = 2 * grid_len
    chips = gray(pa_count // 2)
    forward_y = ahead.reshape(2, grid_len, 2, pa_count // 2, 2, y_local)
    forward_y = forward_y.transpose(3, 4, 2, 5, 0, 1)[chips]
    forward_y = forward_y.reshape(size, size)
    inverse_y = back.reshape(2, pa_count // 2, 2, y_local, 2, grid_len)
    inverse_y = inverse_y.transpose(4, 5, 1, 2, 0, 3)[:, :, chips]
    inverse_y = inverse_y.reshape(size, size)
    forward_x = ahead.reshape(size, size)
    inverse_x = back.reshape(size, size)
    return [split_table(t) for t in (forward_z, forward_y, forward_x, inverse_x, inverse_y, inverse_z)]


def lane_iota(rows):
    return lax.broadcasted_iota(jnp.int32, (rows, LANES), 1)


def forward_z_kernel(
    x_local,
    y_local,
    plane_ref,
    table_ref,
    out_ref,
    planes,
    table,
    table_sem,
    in_sems,
):
    half = LANES // 2
    tiles = COMPS // 2
    per_comp = x_local * y_local
    first_half = lane_iota(half) < half
    fetch_table = pltpu.make_async_copy(table_ref, table, table_sem)
    fetch_table.start()
    fetches = []
    for tile in range(tiles):
        span = pl.ds(2 * tile * per_comp, 2 * per_comp)
        fetches.append(
            pltpu.make_async_copy(plane_ref.at[span], planes.at[span], in_sems.at[tile])
        )
        fetches[-1].start()
    fetch_table.wait()
    stride = tiles * y_local
    for tile in range(tiles):
        fetches[tile].wait()
        for base in range(0, y_local, 4):
            rows = [
                planes[pl.ds((2 * tile + c) * per_comp + base + y, x_local, stride=y_local), :]
                for y in range(4)
                for c in range(2)
            ]
            lines = split(jnp.concatenate(rows, axis=0))
            waves = product((table[0], table[1]), lines, ((1,), (1,)))
            for y in range(0, 4, 2):
                begin = y * LANES // 2
                low_bins = waves[:half, begin : begin + LANES]
                high_bins = waves[half:, begin : begin + LANES]
                even = jnp.where(first_half, low_bins, pltpu.roll(high_bins, half, 1))
                odd = jnp.where(first_half, pltpu.roll(low_bins, half, 1), high_bins)
                begin = tile * y_local + base + y
                out_ref[pl.ds(begin, half, stride=stride), :] = even
                out_ref[pl.ds(begin + 1, half, stride=stride), :] = odd


def spectral_kernel(
    gx_count,
    pa_count,
    y_local,
    freq_ref,
    data_ref,
    forward_y_ref,
    forward_x_ref,
    inverse_x_ref,
    inverse_y_ref,
    out_ref,
    waves,
    blocks_ref,
    sems,
):
    grid_len = LANES
    size = 2 * grid_len
    tile_count = COMPS // 2
    forward_y = (forward_y_ref[0], forward_y_ref[1])
    forward_x = (forward_x_ref[0], forward_x_ref[1])
    inverse_x = (inverse_x_ref[0], inverse_x_ref[1])
    inverse_y = (inverse_y_ref[0], inverse_y_ref[1])
    x_local = grid_len // gx_count
    def along_y(tile):
        fields = [
            data_ref[:, g, :, :, tile].reshape(size, LANES).T for g in range(gx_count)
        ]
        return product(split(jnp.concatenate(fields, axis=0)), forward_y)

    def along_x(tile, lines):
        planes = []
        for slot in range(4):
            rows = [
                lines[g * LANES + slot * x_local :][:x_local] for g in range(gx_count)
            ]
            plane = jnp.concatenate(rows, axis=0)
            planes.append(jnp.concatenate([plane[:, :LANES], plane[:, LANES:]], axis=0))
        waves[tile] = product(forward_x, split(jnp.concatenate(planes, axis=1)))

    lines = along_y(0)
    for tile in range(tile_count):
        later = along_y(tile + 1) if tile + 1 < tile_count else None
        along_x(tile, lines)
        lines = later

    def signed(index):
        plain = jnp.where(index < grid_len // 2, index, index - grid_len)
        return jnp.where(index == grid_len // 2, 0, plain).astype(jnp.float32)

    step = 16
    freq_y = signed(lax.broadcasted_iota(jnp.int32, (step, LANES), 1))
    row_index = lax.broadcasted_iota(jnp.int32, (step, LANES), 0)

    def operate(chunk, carry):
        start = pl.multiple_of(chunk * step, step)
        freq_x = signed(row_index + start)
        for j in range(2):
            freq_z = freq_ref[j]
            square = freq_x * freq_x + freq_y * freq_y + freq_z * freq_z
            inverse = 1.0 / jnp.maximum(square, 1.0)
            scaled = inverse * inverse * green_coef
            for part in range(2):
                rows = pl.ds(part * grid_len + start, step)

                def at(comp):
                    return (comp // 2, rows, pl.ds((2 * j + comp % 2) * LANES, LANES))

                e_xx, e_yy, e_zz, e_yz, e_xz, e_xy = [waves[at(c)] for c in range(COMPS)]
                trace = (0.5 * lame_lambda) * (e_xx + e_yy + e_zz)
                n_x = (trace + e_xx) * freq_x + e_xy * freq_y + e_xz * freq_z
                n_y = e_xy * freq_x + (trace + e_yy) * freq_y + e_yz * freq_z
                n_z = e_xz * freq_x + e_yz * freq_y + (trace + e_zz) * freq_z
                along = (freq_x * n_x + freq_y * n_y + freq_z * n_z) * scaled
                u_x = n_x * inverse - freq_x * along
                u_y = n_y * inverse - freq_y * along
                u_z = n_z * inverse - freq_z * along
                waves[at(0)] = 2.0 * (freq_x * u_x)
                waves[at(1)] = 2.0 * (freq_y * u_y)
                waves[at(2)] = 2.0 * (freq_z * u_z)
                waves[at(3)] = freq_y * u_z + freq_z * u_y
                waves[at(4)] = freq_x * u_z + freq_z * u_x
                waves[at(5)] = freq_x * u_y + freq_y * u_x
        return carry

    lax.fori_loop(0, grid_len // step, operate, 0, unroll=True)

    stores = []
    for tile in range(tile_count):
        planes = product(inverse_x, split(waves[tile]))
        rows = []
        for g in range(gx_count):
            for slot in range(4):
                lanes = slice(slot * LANES, (slot + 1) * LANES)
                parts = [
                    planes[part * grid_len + g * x_local :][:x_local, lanes] for part in range(2)
                ]
                rows.append(jnp.concatenate(parts, axis=1))
        lines = product(split(jnp.concatenate(rows, axis=0)), inverse_y)
        for g in range(gx_count):
            field = lines[g * LANES : (g + 1) * LANES].T
            blocks_ref[tile, :, g] = field.reshape(pa_count // 2, 2, 2, y_local, LANES)
        place = out_ref.at[:, :, :, :, tile]
        stores.append(pltpu.make_async_copy(blocks_ref.at[tile], place, sems.at[tile]))
        stores[-1].start()
    for store in stores:
        store.wait()


def sample(field_ref, voxel_ref, per_comp, cell_count, cell):
    cell_rows = per_comp // cell_count
    place = lax.broadcasted_iota(jnp.int32, (LANES, LANES), 0)
    row = lax.broadcasted_iota(jnp.int32, (cell_rows, LANES), 0)
    voxel = voxel_ref[pl.ds(cell, 1), :]
    picked_row = lax.shift_right_logical(voxel, LANES.bit_length() - 1)
    picked_place = lax.bitwise_and(voxel, LANES - 1)
    choose = (place == picked_place).astype(jnp.bfloat16)
    keep = row == picked_row - cell * cell_rows
    blocks = [
        jnp.concatenate(
            split(field_ref[pl.ds(comp * per_comp + cell * cell_rows, cell_rows), :]), axis=1
        )
        for comp in range(COMPS)
    ]
    picked = jnp.dot(
        jnp.concatenate(blocks, axis=0),
        jnp.concatenate([choose, choose], axis=0),
        preferred_element_type=jnp.float32,
    )
    found = [
        jnp.sum(
            jnp.where(keep, picked[comp * cell_rows : (comp + 1) * cell_rows], 0.0),
            axis=0,
            keepdims=True,
        )
        for comp in range(COMPS)
    ]
    return jnp.concatenate(found + [jnp.zeros((8 - COMPS, LANES), jnp.float32)], axis=0)


def stress_from(elastic):
    trace = lame_lambda * (elastic[0] + elastic[1] + elastic[2])
    return [
        2.0 * shear_modulus * value + (trace if comp < 3 else 0.0)
        for comp, value in enumerate(elastic)
    ]


def inverse_z_kernel(
    x_local,
    y_local,
    cell_count,
    voxel_ref,
    waves_ref,
    local_ref,
    table_ref,
    strain_ref,
    own_ref,
    low_cells_ref,
    high_cells_ref,
):
    table = (table_ref[0], table_ref[1])
    half = LANES // 2
    per_comp = x_local * y_local
    stride = (COMPS // 2) * y_local
    first_half = lane_iota(half) < half
    for pair in range(y_local // 2):
        for tile in range(COMPS // 2):
            base = tile * y_local + 2 * pair
            even = waves_ref[pl.ds(base, half, stride=stride), :]
            odd = waves_ref[pl.ds(base + 1, half, stride=stride), :]
            low_bins = jnp.where(first_half, even, pltpu.roll(odd, half, 1))
            high_bins = jnp.where(first_half, pltpu.roll(even, half, 1), odd)
            turned = jnp.concatenate([low_bins, high_bins], axis=0).T
            lines = product(split(turned), table)
            for y in range(2):
                for c in range(2):
                    begin = (2 * y + c) * x_local
                    place = (2 * tile + c) * per_comp + 2 * pair + y
                    strain_ref[pl.ds(place, x_local, stride=y_local), :] = lines[begin:][:x_local]
    for cell in range(cell_count):
        found = sample(strain_ref, voxel_ref, per_comp, cell_count, cell) - local_ref[cell]
        own_ref[cell] = found
        if cell < 2:
            low_cells_ref[cell] = found
        if cell >= cell_count - 2:
            high_cells_ref[cell - cell_count + 2] = found


def pair_moments(position, fixed, scratch, pairs, add=(), fresh=True):
    columns, features, moments = scratch
    slots = position[0].shape[0]
    lines, burgers = fixed
    moved = [
        position[1] * lines[2] - position[2] * lines[1],
        position[2] * lines[0] - position[0] * lines[2],
        position[0] * lines[1] - position[1] * lines[0],
    ]
    for shift in range(3):
        offset = shift - 1.0
        shifted = [moved[0], moved[1] - offset * lines[2], moved[2] + offset * lines[1]]
        for b in range(3):
            for a in range(3):
                if fresh:
                    features[shift, pl.ds((3 * a + b) * slots, slots), :] = lines[a] * burgers[b]
                features[shift, pl.ds((9 + 3 * a + b) * slots, slots), :] = shifted[a] * burgers[b]
    for source in sorted({target + shift - 1 for target in pairs for shift in pairs[target]}):
        for a in range(3):
            row = position[a][source : source + 1]
            columns[source, a] = jnp.broadcast_to(row, (LANES, LANES)).T
    for target, shifts in pairs.items():
        weights = []
        sources = []
        own = [position[a][target : target + 1] for a in range(3)]
        for shift in shifts:
            source = target + shift - 1
            d_x = (own[0] - (shift - 1.0)) - columns[source, 0]
            d_y = own[1] - columns[source, 1]
            d_z = own[2] - columns[source, 2]
            inverse = lax.rsqrt(d_x * d_x + d_y * d_y + d_z * d_z + core_square)
            weights.append(inverse * inverse * inverse)
            sources.append(features[shift, pl.ds(source, FEATURES, stride=slots), :])
        source = jnp.concatenate(sources, axis=1)
        high, rest = split(source)
        low = (source - high.astype(jnp.float32) - rest.astype(jnp.float32)).astype(jnp.bfloat16)
        parts = jnp.concatenate([high, rest, low], axis=0)
        total = jnp.dot(
            jnp.concatenate([parts, parts], axis=1),
            jnp.concatenate(split(jnp.concatenate(weights, axis=0)), axis=0),
            preferred_element_type=jnp.float32,
        )
        total = total[:FEATURES] + (total[FEATURES : 2 * FEATURES] + total[2 * FEATURES :])
        rows = pl.ds(target * FEATURES, FEATURES)
        moments[rows, :] = moments[rows, :] + total if target in add else total


def every_pair(first, last):
    return {target: (0, 1, 2) for target in range(first, last)}


def pair_field(position, moments):
    slots = position[0].shape[0]

    def feature(index):
        return moments[pl.ds(index, slots, stride=FEATURES), :]

    moment = [[None] * 3 for _ in range(3)]
    for b in range(3):
        g = [feature(3 * a + b) for a in range(3)]
        moment[0][b] = position[1] * g[2] - position[2] * g[1] - feature(9 + b)
        moment[1][b] = position[2] * g[0] - position[0] * g[2] - feature(12 + b)
        moment[2][b] = position[0] * g[1] - position[1] * g[0] - feature(15 + b)
    pairs = ((0, 0), (1, 1), (2, 2), (1, 2), (0, 2), (0, 1))
    return [pair_factor * (moment[a][b] + moment[b][a]) for a, b in pairs]


def load_fixed(start_ref):
    values = [start_ref[a] for a in range(9)]
    return values[0:3], values[3:6], values[6:9]


def first_field_kernel(
    per_comp,
    cell_count,
    start_ref,
    voxel_ref,
    plastic_ref,
    out_ref,
    local_ref,
    columns,
    features,
    moments,
):
    for cell in range(cell_count):
        local_ref[cell] = sample(plastic_ref, voxel_ref, per_comp, cell_count, cell)
    moments[...] = jnp.zeros_like(moments)
    position, lines, burgers = load_fixed(start_ref)
    pair_moments(
        position, (lines, burgers), (columns, features, moments), every_pair(1, cell_count + 5)
    )
    for comp, value in enumerate(pair_field(position, moments)):
        out_ref[comp] = value


def moved_on(position, lines, burgers, sampled, field):
    sigma = [sampled[comp] + field[comp] for comp in range(COMPS)]
    traction = [
        sigma[full_index[a][0]] * burgers[0]
        + sigma[full_index[a][1]] * burgers[1]
        + sigma[full_index[a][2]] * burgers[2]
        for a in range(3)
    ]
    return [
        position[0] + step_size * (traction[1] * lines[2] - traction[2] * lines[1]),
        position[1] + step_size * (traction[2] * lines[0] - traction[0] * lines[2]),
        position[2] + step_size * (traction[0] * lines[1] - traction[1] * lines[0]),
    ]


def spread(sampled_ref, parts):
    sampled_ref[...] = jnp.zeros_like(sampled_ref)
    for begin, part in parts:
        sampled_ref[pl.ds(8 * begin, 8 * part.shape[0]), :] = part[...].reshape(-1, LANES)
    return stress_from([sampled_ref[pl.ds(comp, SLOTS, stride=8), :] for comp in range(COMPS)])


def own_moves_kernel(
    cell_count,
    start_ref,
    first_ref,
    own_ref,
    strain_ref,
    plastic_ref,
    stress_ref,
    part_ref,
    columns,
    features,
    moments,
    sampled_ref,
    block,
    sems,
):
    rows = stress_ref.shape[1] // cell_count
    stores = []
    for cell in range(cell_count):
        span = pl.ds(cell * rows, rows)
        elastic = [strain_ref[c, span, :] - plastic_ref[c, span, :] for c in range(COMPS)]
        for comp, value in enumerate(stress_from(elastic)):
            block[comp, span, :] = value
        stores.append(
            pltpu.make_async_copy(block.at[:, span], stress_ref.at[:, span], sems.at[cell])
        )
        stores[-1].start()
    moments[...] = jnp.zeros_like(moments)
    position, lines, burgers = load_fixed(start_ref)
    sampled = spread(sampled_ref, [(3, own_ref)])
    field = [first_ref[comp] for comp in range(COMPS)]
    position = moved_on(position, lines, burgers, sampled, field)
    first, last = 3, cell_count + 3
    pairs = {
        target: [s for s in range(3) if first <= target + s - 1 < last]
        for target in range(first, last)
    }
    pair_moments(position, (lines, burgers), (columns, features, moments), pairs)
    part_ref[...] = moments[...]
    for store in stores:
        store.wait()


def moves_kernel(
    cell_count,
    start_ref,
    first_ref,
    left_ref,
    own_ref,
    right_ref,
    part_ref,
    out_ref,
    columns,
    features,
    moments,
    sampled_ref,
):
    moments[...] = part_ref[...]
    position, lines, burgers = load_fixed(start_ref)
    initial = position
    first, last = 3, cell_count + 3
    sampled = spread(sampled_ref, [(1, left_ref), (first, own_ref), (last, right_ref)])
    rest = {first - 1: (0, 1, 2), first: (0,), last - 1: (2,), last: (0, 1, 2)}
    for repeat in range(SUB):
        if repeat == 0:
            field = [first_ref[comp] for comp in range(COMPS)]
        else:
            pair_moments(
                position,
                (lines, burgers),
                (columns, features, moments),
                rest if repeat == 1 else every_pair(first, last),
                (first, last - 1) if repeat == 1 else (),
                repeat == 1,
            )
            field = pair_field(position, moments)
        position = moved_on(position, lines, burgers, sampled, field)
    for a in range(3):
        out_ref[a] = (position[a] - initial[a])[first:last]


def kernel_call(kernel, outs, scratch=(), flops=0, places="", out_places="", limit=VMEM_LIMIT):
    spaces = {"s": pltpu.SMEM, "v": pltpu.VMEM, "h": pltpu.HBM}
    return pl.pallas_call(
        kernel,
        out_shape=outs,
        in_specs=[pl.BlockSpec(memory_space=spaces[p]) for p in places],
        out_specs=[pl.BlockSpec(memory_space=spaces[p]) for p in out_places],
        scratch_shapes=list(scratch),
        compiler_params=pltpu.CompilerParams(vmem_limit_bytes=limit),
        cost_estimate=pl.CostEstimate(flops=flops, bytes_accessed=1 << 20, transcendentals=0),
    )


def in_hbm(array):
    return pltpu.with_memory_space_constraint(array, pltpu.HBM)


def neighbours(low, high):
    count = lax.axis_size("gx")
    forward = [(i, (i + 1) % count) for i in range(count)]
    backward = [(target, source) for source, target in forward]
    return lax.ppermute(high, "gx", forward), lax.ppermute(low, "gx", backward)


def slab_body(plastic, offsets, lines, burgers, counts, voxels):
    f32 = jnp.float32
    comp_count, x_local, y_local, grid_len = plastic.shape
    gx_count = lax.axis_size("gx")
    pa_count = lax.axis_size("pa")
    devices = gx_count * pa_count
    cell_count, cap = voxels.shape[1:]
    tiles = comp_count // 2
    rows = devices * 2 * tiles * y_local
    blocks = (devices, rows // devices, LANES)
    parts = (pa_count // 2, gx_count, 2, 2, tiles, y_local, LANES)
    forward_z, forward_y, forward_x, inverse_x, inverse_y, inverse_z = [
        jnp.asarray(t) for t in tables(grid_len, pa_count, y_local)
    ]
    order = [
        [
            g * pa_count + 2 * z + core
            for z in gray(pa_count // 2)
            for g in range(gx_count)
            for core in range(2)
        ]
    ]
    exchange = functools.partial(
        lax.all_to_all,
        axis_name=("gx", "pa"),
        split_axis=0,
        concat_axis=0,
        axis_index_groups=order,
        tiled=True,
    )
    pa_index = lax.axis_index("pa")
    place = pa_index // 2
    for shift in (1, 2, 4, 8):
        place = place ^ (pa_index // 2 >> shift)
    own = (place * gx_count + lax.axis_index("gx")) * 2 + pa_index % 2
    bins = (own + devices * jnp.arange(2, dtype=jnp.int32)).astype(f32)
    flat_plastic = plastic.reshape(-1, grid_len)
    tile_sems = pltpu.SemaphoreType.DMA((tiles,))

    bins, flat_plastic = lax.optimization_barrier((bins, flat_plastic))

    (waves,) = kernel_call(
        functools.partial(forward_z_kernel, x_local, y_local),
        [pltpu.VMEM((rows, LANES), f32)],
        [
            pltpu.VMEM(flat_plastic.shape, f32),
            pltpu.VMEM(forward_z.shape, jnp.bfloat16),
            pltpu.SemaphoreType.DMA,
            tile_sems,
        ],
        places="hh",
        out_places="v",
    )(in_hbm(flat_plastic), in_hbm(forward_z))
    waves = exchange(waves.reshape(blocks))
    (waves,) = kernel_call(
        functools.partial(spectral_kernel, gx_count, pa_count, y_local),
        [pltpu.HBM(parts, f32)],
        [
            pltpu.VMEM((tiles, 2 * grid_len, 4 * LANES), f32),
            pltpu.VMEM((tiles, pa_count // 2, gx_count, 2, 2, y_local, LANES), f32),
            tile_sems,
        ],
        places="svvvvv",
        out_places="h",
    )(bins, waves.reshape(parts), forward_y, forward_x, inverse_x, inverse_y)
    waves, offsets, lines, burgers, counts = lax.optimization_barrier(
        (waves, offsets, lines, burgers, counts)
    )
    waves = exchange(waves.reshape(blocks))

    live = (jnp.arange(cap, dtype=jnp.int32)[None, :] < counts[0][:, None]).astype(f32)
    start = jnp.concatenate([offsets[:, 0], lines[:, 0], burgers[:, 0] * live[None]], axis=0)
    below, above = neighbours(start[:, :3], start[:, cell_count - 3 :])
    padding = jnp.zeros((9, SLOTS - cell_count - 6, cap), f32)
    start = jnp.concatenate([below, start, above, padding], axis=1)
    pair_scratch = [
        pltpu.VMEM((SLOTS, 3, LANES, LANES), f32),
        pltpu.VMEM((3, FEATURES * SLOTS, LANES), f32),
        pltpu.VMEM((SLOTS * FEATURES, LANES), f32),
    ]
    per_comp = x_local * y_local
    cells = jax.ShapeDtypeStruct((cell_count, 8, cap), f32)
    first, local = kernel_call(
        functools.partial(first_field_kernel, per_comp, cell_count),
        [jax.ShapeDtypeStruct((comp_count, SLOTS, cap), f32), cells],
        pair_scratch,
        places="vvv",
        out_places="vv",
    )(start, voxels[0], flat_plastic)

    waves, first, local = lax.optimization_barrier((waves, first, local))
    end = jax.ShapeDtypeStruct((2, 8, cap), f32)
    strain, own_cells, low_cells, high_cells = kernel_call(
        functools.partial(inverse_z_kernel, x_local, y_local, cell_count),
        [pltpu.VMEM(flat_plastic.shape, f32), cells, end, end],
        places="vvvv",
        out_places="vvvv",
    )(voxels[0], waves.reshape(rows, LANES), local, inverse_z)
    left, right = neighbours(low_cells, high_cells)
    sampled = pltpu.VMEM((8 * SLOTS, LANES), f32)
    whole = (comp_count, per_comp, LANES)
    stress, part = kernel_call(
        functools.partial(own_moves_kernel, cell_count),
        [
            jax.ShapeDtypeStruct(whole, f32),
            jax.ShapeDtypeStruct((SLOTS * FEATURES, cap), f32),
        ],
        pair_scratch
        + [sampled, pltpu.VMEM(whole, f32), pltpu.SemaphoreType.DMA((cell_count,))],
        places="vvvvv",
        out_places="hv",
    )(start, first, own_cells, strain.reshape(whole), plastic.reshape(whole))
    (moved,) = kernel_call(
        functools.partial(moves_kernel, cell_count),
        [jax.ShapeDtypeStruct((3, cell_count, cap), f32)],
        pair_scratch + [sampled],
        places="vvvvvv",
        out_places="v",
    )(start, first, left, own_cells, right, part)
    return (stress.reshape(plastic.shape), moved[:, None])


def fits(mesh, plastic, voxels):
    gx_count, pa_count = mesh.shape["gx"], mesh.shape["pa"]
    grid_len = plastic.shape[3]
    x_local, y_local = plastic.shape[1] // gx_count, plastic.shape[2] // pa_count
    cell_count = voxels.shape[1] // gx_count
    return (
        plastic.shape == (COMPS, LANES, LANES, LANES)
        and 4 * gx_count * pa_count == grid_len
        and 4 * x_local == LANES
        and pa_count % 2 == 0
        and y_local % 8 == 0
        and voxels.shape[2] == LANES
        and 3 <= cell_count <= SLOTS - 6
        and x_local % cell_count == 0
    )


def solution(mesh):
    placed = (
        P(None, "gx", "pa", None),
        P(None, "pa", "gx", None),
        P(None, "pa", "gx", None),
        P(None, "pa", "gx", None),
        P("pa", "gx"),
        P("pa", "gx", None),
    )

    def step(plastic, offsets, lines, burgers, counts, voxels):
        chosen = slab_body if fits(mesh, plastic, voxels) else body
        return jax.shard_map(
            chosen,
            mesh=mesh,
            in_specs=placed,
            out_specs=(P(None, "gx", "pa", None), P(None, "pa", "gx", None)),
            check_vma=False,
        )(plastic, offsets, lines, burgers, counts, voxels)

    return step
```
